32 devices in a mesh: rep: 2 (over x), fsdp: 16 (over z, y, core).
Axes of the slice: x: 2, y: 2, z: 4, core: 2. Of those that a mesh axis runs over, the one named last changes fastest.
Arguments:
- tokens: bfloat16 [8192, 768], P(('rep', 'fsdp')), may hold values from -6 to 6
- cotangent: bfloat16 [8192, 768], P(('rep', 'fsdp')), may hold values from -6 to 6
- clip_index: int32 [8192], P(('rep', 'fsdp')), may hold values from 0 to 3, as said below
- key_valid: int32 [8192], P(('rep', 'fsdp')), may hold values from 0 to 1, as said below
- patch_masked: int32 [8192], P(('rep', 'fsdp')), may hold values 0 or 1
- attn_weight: float32 [768, 3072], P('fsdp')
- mlp_weight: float32 [768, 6144], P('fsdp')
- gain_vector: float32 [1536], P('fsdp'), may hold values from 0.25 to 1.75
- offset_vector: float32 [8448], P('fsdp'), may hold values from -1.8 to 1.8
- attn_moment: float32 [768, 3072], P('fsdp')
- mlp_moment: float32 [768, 6144], P('fsdp')
- gain_moment: float32 [1536], P('fsdp')
- offset_moment: float32 [8448], P('fsdp')
- attn_average: float32 [768, 3072], P('fsdp')
- mlp_average: float32 [768, 6144], P('fsdp')
- gain_average: float32 [1536], P('fsdp'), may hold values from 0.25 to 1.75
- offset_average: float32 [8448], P('fsdp'), may hold values from -1.8 to 1.8
Outputs:
- activations: bfloat16 [8192, 768], P(('rep', 'fsdp'))
- input_grad: bfloat16 [8192, 768], P(('rep', 'fsdp'))
- attn_new: float32 [768, 3072], P('fsdp')
- attn_momentum: float32 [768, 3072], P('fsdp')
- attn_ema: float32 [768, 3072], P('fsdp')
- attn_copy: bfloat16 [768, 3072], P('fsdp')
- mlp_new: float32 [768, 6144], P('fsdp')
- mlp_momentum: float32 [768, 6144], P('fsdp')
- mlp_ema: float32 [768, 6144], P('fsdp')
- mlp_copy: bfloat16 [768, 6144], P('fsdp')
- gain_new: float32 [1536], P('fsdp')
- gain_momentum: float32 [1536], P('fsdp')
- gain_ema: float32 [1536], P('fsdp')
- gain_copy: bfloat16 [1536], P('fsdp')
- offset_new: float32 [8448], P('fsdp')
- offset_momentum: float32 [8448], P('fsdp')
- offset_ema: float32 [8448], P('fsdp')
- offset_copy: bfloat16 [8448], P('fsdp')
The draws below stay inside these ranges and needn't reach their ends.
Inputs may be any that keep to these rules, and one draw needn't show every extreme that they name: `clip_index`: each aligned block of 256 slots holds whole clips of consecutive slots, numbered from 0 in order within the block; every clip has a multiple of 64 slots, from 64 to 256; some block holds a single clip, and some block holds clips of 64 slots only. `key_valid`: padded slots lie only at the end of a clip, at most 32 of them in one clip.
All inputs are finite; a program needn't handle non-finite values. No bound on the sum of `patch_masked` on one device may be relied on, other than what follows from the above.
Results may differ from the reference program's by a relative error of at most 0.013.
The reference program's roundings to bfloat16 on the way count: a program that leaves them out, or rounds other values in their place, can miss the bound.
Values may be sent and summed in bfloat16 or wider, within the bound.
No kernel may reach another device: no remote copies, remote signals or barrier semaphores. Data moves between devices by JAX's collectives and lax.ppermute only.
A program may use at most 128 MiB of HBM per device.

```python
import math
import jax
import jax.numpy as jnp
from jax import lax

D = 768
HEADS = 12
HEAD_DIM = 64
FF = 3072
TOK_DEV = 256
CLIP_UNIT = 64
TOKENS = 8192
OFFS = 8448


def clip_layout(key):
    devices_all = TOKENS // TOK_DEV
    unit_count = TOK_DEV // CLIP_UNIT
    cut_level = jax.random.randint(jax.random.fold_in(key, 101), (devices_all, 1), 0, 8)
    cut_rolls = jax.random.randint(jax.random.fold_in(key, 102), (devices_all, unit_count), 0, 8)
    cut_flags = (cut_rolls < cut_level).astype(jnp.int32)
    row_ids = lax.broadcasted_iota(jnp.int32, (devices_all, unit_count), 0)
    col_ids = lax.broadcasted_iota(jnp.int32, (devices_all, unit_count), 1)
    cut_flags = jnp.where(row_ids == devices_all - 1, 1, cut_flags)
    cut_flags = jnp.where((row_ids == 0) | (col_ids == 0), 0, cut_flags)
    clip_of_unit = jnp.cumsum(cut_flags, axis=1).astype(jnp.int32)
    following = jnp.concatenate([cut_flags[:, 1:], jnp.ones((devices_all, 1), jnp.int32)], axis=1)
    pad_count = jax.random.randint(jax.random.fold_in(key, 103), (devices_all, unit_count), 0, CLIP_UNIT // 2 + 1)
    pad_count = jnp.where((row_ids == 0) & (col_ids == unit_count - 1), CLIP_UNIT // 2, pad_count)
    pad_count = jnp.where(following == 1, pad_count, 0)
    position = lax.broadcasted_iota(jnp.int32, (devices_all, unit_count, CLIP_UNIT), 2)
    key_flags = (position < CLIP_UNIT - pad_count[:, :, None]).astype(jnp.int32)
    clip_ids = jnp.broadcast_to(clip_of_unit[:, :, None], (devices_all, unit_count, CLIP_UNIT))
    return (clip_ids.reshape(TOKENS).astype(jnp.int32), key_flags.reshape(TOKENS))


def draw_clip_index(key, part):
    return clip_layout(key)[0]


def draw_key_valid(key, part):
    return clip_layout(key)[1]


def attn_law(key):
    normals = jnp.clip(jax.random.normal(key, (D, 4 * D), jnp.float32), -6.0, 6.0)
    col_ids = lax.broadcasted_iota(jnp.int32, (D, 4 * D), 1)
    return normals * jnp.where(col_ids >= 3 * D, 8.0, 1.0) / math.sqrt(D)


def mlp_law(key):
    normals = jnp.clip(jax.random.normal(key, (D, 2 * FF), jnp.float32), -6.0, 6.0)
    col_ids = lax.broadcasted_iota(jnp.int32, (D, 2 * FF), 1)
    return normals * jnp.where(col_ids >= FF, 1.0 / math.sqrt(FF), 1.0 / math.sqrt(D))


def moment_law(key, shape_of):
    normals = jnp.clip(jax.random.normal(key, shape_of, jnp.float32), -6.0, 6.0)
    return normals * (0.5 * math.sqrt(TOKENS))


def draw_attn_weight(key, part):
    return attn_law(jax.random.fold_in(key, 11))


def draw_attn_average(key, part):
    return attn_law(jax.random.fold_in(key, 12))


def draw_mlp_weight(key, part):
    return mlp_law(jax.random.fold_in(key, 21))


def draw_mlp_average(key, part):
    return mlp_law(jax.random.fold_in(key, 22))


def draw_attn_moment(key, part):
    return moment_law(jax.random.fold_in(key, 31), (D, 4 * D))


def draw_mlp_moment(key, part):
    return moment_law(jax.random.fold_in(key, 32), (D, 2 * FF))


def draw_gain_moment(key, part):
    return moment_law(jax.random.fold_in(key, 33), (2 * D,))


def draw_offset_moment(key, part):
    return moment_law(jax.random.fold_in(key, 34), (7 * D + FF,))


def set_ends(drawn, key, least, high):
    extent = drawn.shape
    spot = [jax.random.randint(jax.random.fold_in(key, axis), (), 0, extent[axis]) for axis in range(len(extent))]
    drawn = drawn.at[tuple(spot)].set(least)
    longest = extent.index(max(extent))
    spot[longest] = (spot[longest] + 1) % extent[longest]
    return drawn.at[tuple(spot)].set(high)


def raised(result, stream_key, source, target, shards_of, factor):
    owner, partner = [(jnp.arange(result.shape[axis_at]) // (result.shape[axis_at] // shards_of)).reshape([-1 if axis == axis_at else 1 for axis in range(result.ndim)]) for axis_at in (source, target)]
    chosen = jax.random.permutation(stream_key, shards_of)[partner]
    strong = (owner == chosen) | (owner == (partner + shards_of // 2) % shards_of)
    return jnp.where(strong, factor * result, result)


def steps_of(key, shape, cuts, smallest, top_value):
    gain, own = 1.0, jax.random.fold_in(key, 6)
    for dim, blocks in cuts:
        heights = jnp.exp(jax.random.uniform(jax.random.fold_in(own, dim), (blocks,), jnp.float32, smallest / len(cuts), top_value / len(cuts)))
        gain = gain * jnp.repeat(heights, shape[dim] // blocks).reshape([-1 if axis == dim else 1 for axis in range(len(shape))])
    return gain


def scatter_about(stream_key, dims, deviation, reach, cuts=(), held_as=jnp.bfloat16):
    loudness = steps_of(stream_key, dims, cuts, -0.22, 0.18) if cuts else 1.0
    values = jax.random.normal(stream_key, dims, jnp.float32) * deviation * loudness
    return jnp.minimum(jnp.maximum(values, -reach), reach).astype(held_as)


def noise_with(rng, shape, deviation, bound, split, heavy, held_as=jnp.bfloat16):
    values = deviation * jax.random.normal(rng, shape, jnp.float32)
    if split:
        values = values * steps_of(rng, shape, split, -0.22, 0.18)
    return jnp.clip(raised(values, jax.random.fold_in(rng, 3), *heavy), -bound, bound).astype(held_as)


def setup_inputs(seed: int = 0) -> dict:
    key_of = jax.random.split(jax.random.key(seed), 18)
    return {
        "tokens": scatter_about(key_of[0], (TOKENS, D), 1.0, 6.0, ((0, 32),)),
        "cotangent": noise_with(key_of[1], (TOKENS, D), 1.0, 6.0, ((0, 32),), (0, 1, 32, 2.75)),
        "clip_index": draw_clip_index(jax.random.fold_in(key_of[17], 71), 0),
        "key_valid": draw_key_valid(jax.random.fold_in(key_of[17], 71), 0),
        "patch_masked": set_ends((jax.random.randint(key_of[4], (TOKENS,), 0, 3) < 1).astype(jnp.int32), jax.random.fold_in(key_of[4], 1), 0, 1),
        "attn_weight": draw_attn_weight(jax.random.fold_in(key_of[17], 71), 0),
        "mlp_weight": draw_mlp_weight(jax.random.fold_in(key_of[17], 71), 0),
        "gain_vector": jnp.clip(1.0 + 0.15 * jax.random.normal(key_of[7], (2 * D,), jnp.float32), 0.25, 1.75),
        "offset_vector": scatter_about(key_of[8], (OFFS,), 0.3, 1.8, ((0, 16),), jnp.float32),
        "attn_moment": draw_attn_moment(jax.random.fold_in(key_of[17], 71), 0),
        "mlp_moment": draw_mlp_moment(jax.random.fold_in(key_of[17], 71), 0),
        "gain_moment": draw_gain_moment(jax.random.fold_in(key_of[17], 71), 0),
        "offset_moment": draw_offset_moment(jax.random.fold_in(key_of[17], 71), 0),
        "attn_average": draw_attn_average(jax.random.fold_in(key_of[17], 71), 0),
        "mlp_average": draw_mlp_average(jax.random.fold_in(key_of[17], 71), 0),
        "gain_average": jnp.clip(1.0 + 0.15 * jax.random.normal(key_of[15], (2 * D,), jnp.float32), 0.25, 1.75),
        "offset_average": scatter_about(key_of[16], (OFFS,), 0.3, 1.8, ((0, 16),), jnp.float32),
    }


@jax.custom_vjp
def low(v):
    return lax.optimization_barrier(v.astype(jnp.bfloat16)).astype(jnp.float32)

@jax.custom_vjp
def low_back(v):
    return v

def low_keep(v):
    return (low(v), None)

def low_pass(kept, grad):
    return (grad,)

def back_keep(v):
    return (v, None)

def back_low(kept, grad):
    return (low(grad),)
low.defvjp(low_keep, low_pass)
low_back.defvjp(back_keep, back_low)
momentum_decay = 0.9
average_decay = 0.8
base_rate = 0.02
norm_eps = 1e-06
mask_fill = -1e+30

def normalize(inputs):
    mean_val = lax.optimization_barrier(jnp.mean(inputs, axis=-1, keepdims=True))
    centred = inputs - mean_val
    variance = lax.optimization_barrier(jnp.mean(centred * centred, axis=-1, keepdims=True))
    return centred * lax.rsqrt(variance + norm_eps)

def dense_hi(left_mat, right_mat):
    return jnp.dot(left_mat, right_mat, precision=lax.Precision.HIGHEST, preferred_element_type=jnp.float32)

def block_forward(inputs, attn_param, mlp_param, gain_param, offset_param, clip_ids, key_ok, masked):
    attn_low = low(attn_param)
    mlp_low = low(mlp_param)
    gain_low = low(gain_param)
    offset_low = low(offset_param)
    tok_rows = inputs.shape[0]
    is_masked = masked[:, None] == 1
    embedded = jnp.where(is_masked, offset_low[6 * D:7 * D][None, :], inputs)
    normed_one = low(normalize(embedded) * gain_low[:D] + offset_low[:D])
    qkv_bias = jnp.concatenate([offset_low[D:2 * D], jnp.zeros((D,), jnp.float32), offset_low[2 * D:3 * D]])
    projected = low(low_back(dense_hi(normed_one, attn_low[:, :3 * D]) + qkv_bias))
    queries = projected[:, :D].reshape(tok_rows, HEADS, HEAD_DIM)
    key_heads = projected[:, D:2 * D].reshape(tok_rows, HEADS, HEAD_DIM)
    value_heads = projected[:, 2 * D:].reshape(tok_rows, HEADS, HEAD_DIM)
    scores = jnp.einsum('qhd,khd->hqk', queries, key_heads, precision=lax.Precision.HIGHEST)
    scores = low_back(scores * HEAD_DIM ** (-0.5))
    allowed = (clip_ids[:, None] == clip_ids[None, :]) & (key_ok[None, :] == 1)
    scores = jnp.where(allowed[None], scores, mask_fill)
    row_peak = lax.optimization_barrier(jnp.max(scores, axis=-1, keepdims=True))
    exponent = jnp.exp(scores - row_peak)
    attn_prob = low(exponent / lax.optimization_barrier(jnp.sum(exponent, axis=-1, keepdims=True)))
    mixed_out = jnp.einsum('hqk,khd->qhd', attn_prob, value_heads, precision=lax.Precision.HIGHEST)
    mixed_out = low(low_back(mixed_out.reshape(tok_rows, D)))
    after_attn = embedded + low_back(dense_hi(mixed_out, attn_low[:, 3 * D:].T)) + offset_low[3 * D:4 * D]
    normed_two = low(normalize(after_attn) * gain_low[D:] + offset_low[4 * D:5 * D])
    hidden_pre = low_back(dense_hi(normed_two, mlp_low[:, :FF]) + offset_low[7 * D:])
    hidden_act = low(jax.nn.gelu(hidden_pre, approximate=False))
    return after_attn + low_back(dense_hi(hidden_act, mlp_low[:, FF:].T)) + offset_low[5 * D:6 * D]

def advance(gradient, weight, moment, average, learn_rate):
    moment_new = momentum_decay * moment + gradient
    weight_new = weight - learn_rate * (gradient + momentum_decay * moment_new)
    average_new = average_decay * average + (1.0 - average_decay) * weight_new
    return (weight_new, moment_new, average_new, weight_new.astype(jnp.bfloat16))

def reference(tokens, cotangent, clip_index, key_valid, patch_masked, attn_weight, mlp_weight, gain_vector, offset_vector, attn_moment, mlp_moment, gain_moment, offset_moment, attn_average, mlp_average, gain_average, offset_average):
    block_count = TOKENS // TOK_DEV
    blocked = (tokens.astype(jnp.float32).reshape(block_count, TOK_DEV, D), cotangent.astype(jnp.float32).reshape(block_count, TOK_DEV, D), clip_index.reshape(block_count, TOK_DEV), key_valid.reshape(block_count, TOK_DEV), patch_masked.reshape(block_count, TOK_DEV))

    def advance_block(summed, block_item):
        inputs, upstream, clip_ids, key_ok, masked = block_item

        def forward(inputs_f, attn_param, mlp_param, gain_param, offset_param):
            return block_forward(inputs_f, attn_param, mlp_param, gain_param, offset_param, clip_ids, key_ok, masked)
        output, pullback = jax.vjp(forward, inputs, attn_weight, mlp_weight, gain_vector, offset_vector)
        gradients = pullback(upstream)
        summed = (summed[0] + gradients[1], summed[1] + gradients[2], summed[2] + gradients[3], summed[3] + gradients[4])
        return (summed, (output.astype(jnp.bfloat16), gradients[0].astype(jnp.bfloat16)))
    zero_grads = (jnp.zeros(attn_weight.shape, jnp.float32), jnp.zeros(mlp_weight.shape, jnp.float32), jnp.zeros(gain_vector.shape, jnp.float32), jnp.zeros(offset_vector.shape, jnp.float32))
    summed, (out_blocks, grad_blocks) = lax.scan(advance_block, zero_grads, blocked)
    learn_rate = base_rate / math.sqrt(TOKENS)
    attn_new, attn_momentum, attn_ema, attn_copy = advance(summed[0], attn_weight, attn_moment, attn_average, learn_rate)
    mlp_new, mlp_momentum, mlp_ema, mlp_copy = advance(summed[1], mlp_weight, mlp_moment, mlp_average, learn_rate)
    gain_new, gain_momentum, gain_ema, gain_copy = advance(summed[2], gain_vector, gain_moment, gain_average, learn_rate)
    offset_new, offset_momentum, offset_ema, offset_copy = advance(summed[3], offset_vector, offset_moment, offset_average, learn_rate)
    return (out_blocks.reshape(TOKENS, D), grad_blocks.reshape(TOKENS, D), attn_new, attn_momentum, attn_ema, attn_copy, mlp_new, mlp_momentum, mlp_ema, mlp_copy, gain_new, gain_momentum, gain_ema, gain_copy, offset_new, offset_momentum, offset_ema, offset_copy)
```

```python
import functools
import math

import jax
import jax.numpy as jnp
from jax import lax
from jax.experimental import pallas as pl
from jax.experimental.pallas import tpu as pltpu
from jax.sharding import PartitionSpec as P

D = 768
HEADS = 12
HEAD_DIM = 64
FF = 3072
BF = jnp.bfloat16
F32 = jnp.float32


momentum_decay = 0.9
average_decay = 0.8
base_rate = 0.02
norm_eps = 1e-06
mask_fill = -1e30


def normalize(inputs):
    mean_val = jnp.mean(inputs, axis=-1, keepdims=True)
    centred = inputs - mean_val
    variance = jnp.mean(centred * centred, axis=-1, keepdims=True)
    return centred * lax.rsqrt(variance + norm_eps)


def norm_affine(inputs, gain_part, shift_part):
    return normalize(inputs) * gain_part + shift_part


def gelu_exact(inputs):
    return jax.nn.gelu(inputs, approximate=False)


def over_tokens(left_mat, right_mat):
    return lax.dot_general(
        left_mat, right_mat, (((0,), (0,)), ((), ())), preferred_element_type=jnp.float32
    )


def against_rows(left_mat, right_mat):
    return lax.dot_general(
        left_mat, right_mat, (((1,), (1,)), ((), ())), preferred_element_type=jnp.float32
    )


def block_mask(clip_ids, key_ok):
    return (clip_ids[:, None] == clip_ids[None, :]) & (key_ok[None, :] == 1)


def forward(inputs, params, clip_ids, key_ok, masked):
    attn_full = params[0]
    mlp_full = params[1]
    gain_f = params[2].astype(jnp.float32)
    shift_f = params[3].astype(jnp.float32)
    tok_rows = inputs.shape[0]
    score_scale = HEAD_DIM ** (-0.5)
    is_masked = masked[:, None] == 1
    embedded = jnp.where(is_masked, shift_f[6 * D : 7 * D][None, :], inputs)
    normed_one = norm_affine(embedded, gain_f[:D], shift_f[:D]).astype(jnp.bfloat16)
    qkv_bias = jnp.concatenate(
        [shift_f[D : 2 * D], jnp.zeros((D,), jnp.float32), shift_f[2 * D : 3 * D]]
    )
    projected = (
        jnp.dot(normed_one, attn_full[:, : 3 * D], preferred_element_type=jnp.float32) + qkv_bias
    )
    projected = projected.astype(jnp.bfloat16)
    queries = projected[:, :D].reshape(tok_rows, HEADS, HEAD_DIM)
    key_heads = projected[:, D : 2 * D].reshape(tok_rows, HEADS, HEAD_DIM)
    value_heads = projected[:, 2 * D :].reshape(tok_rows, HEADS, HEAD_DIM)
    allowed = block_mask(clip_ids, key_ok)
    scores = (
        jnp.einsum("qhd,khd->hqk", queries, key_heads, preferred_element_type=jnp.float32)
        * score_scale
    )
    scores = jnp.where(allowed[None], scores, mask_fill)
    row_peak = jnp.max(scores, axis=-1, keepdims=True)
    exponent = jnp.exp(scores - row_peak)
    summed = jnp.sum(exponent, axis=-1, keepdims=True)
    attn_prob = (exponent / summed).astype(jnp.bfloat16)
    mixed_parts = jnp.einsum(
        "hqk,khd->qhd", attn_prob, value_heads, preferred_element_type=jnp.float32
    )
    lse_parts = [row_peak + jnp.log(summed)]
    mixed_out = mixed_parts.reshape(tok_rows, D).astype(jnp.bfloat16)
    after_attn = embedded + against_rows(mixed_out, attn_full[:, 3 * D :]) + shift_f[3 * D : 4 * D]
    normed_two = norm_affine(after_attn, gain_f[D:], shift_f[4 * D : 5 * D]).astype(jnp.bfloat16)
    hidden_pre = (
        jnp.dot(normed_two, mlp_full[:, :FF], preferred_element_type=jnp.float32) + shift_f[7 * D :]
    )
    hidden_act = gelu_exact(hidden_pre).astype(jnp.bfloat16)
    output = after_attn + against_rows(hidden_act, mlp_full[:, FF:]) + shift_f[5 * D : 6 * D]
    kept_values = (
        embedded,
        normed_one,
        queries,
        key_heads,
        value_heads,
        lse_parts,
        mixed_out,
        after_attn,
        normed_two,
        hidden_pre,
        hidden_act,
        gain_f,
        shift_f,
    )
    return (output, kept_values)


def backward(cotangent, params, kept_values, clip_ids, key_ok, masked):
    attn_full = params[0]
    mlp_full = params[1]
    (
        embedded,
        normed_one,
        queries,
        key_heads,
        value_heads,
        lse_parts,
        mixed_out,
        after_attn,
        normed_two,
        hidden_pre,
        hidden_act,
        gain_f,
        shift_f,
    ) = kept_values
    tok_rows = cotangent.shape[0]
    score_scale = HEAD_DIM ** (-0.5)
    d_out = cotangent.astype(jnp.float32)
    d_bias_two = jnp.sum(d_out, axis=0)
    d_down = over_tokens(cotangent, hidden_act)
    d_act = jnp.dot(cotangent, mlp_full[:, FF:], preferred_element_type=jnp.float32)
    gelu_value, gelu_pull = jax.vjp(gelu_exact, hidden_pre)
    d_pre_low = gelu_pull(d_act)[0].astype(jnp.bfloat16)
    d_bias_one = jnp.sum(d_pre_low.astype(jnp.float32), axis=0)
    d_up = over_tokens(normed_two, d_pre_low)
    mlp_grad = jnp.concatenate([d_up, d_down], axis=1)
    d_normed_two = against_rows(d_pre_low, mlp_full[:, :FF])
    norm_value, norm_pull = jax.vjp(norm_affine, after_attn, gain_f[D:], shift_f[4 * D : 5 * D])
    d_after_norm, d_gain_two, d_shift_two = norm_pull(d_normed_two)
    d_after = d_out + d_after_norm
    d_after_low = d_after.astype(jnp.bfloat16)
    d_bias_out = jnp.sum(d_after, axis=0)
    d_outproj = over_tokens(d_after_low, mixed_out)
    d_mixed = jnp.dot(d_after_low, attn_full[:, 3 * D :], preferred_element_type=jnp.float32)
    d_mixed_low = d_mixed.astype(jnp.bfloat16).reshape(tok_rows, HEADS, HEAD_DIM)
    block_rows = min(512, tok_rows)
    d_query_parts = []
    d_keys = jnp.zeros((tok_rows, HEADS, HEAD_DIM), jnp.float32)
    d_values = jnp.zeros((tok_rows, HEADS, HEAD_DIM), jnp.float32)
    for block_number, offset in enumerate(range(0, tok_rows, block_rows)):
        allowed = block_mask(clip_ids, key_ok)
        scores = (
            jnp.einsum("qhd,khd->hqk", queries, key_heads, preferred_element_type=jnp.float32)
            * score_scale
        )
        scores = jnp.where(allowed[None], scores, mask_fill)
        attn_prob = jnp.exp(scores - lse_parts[block_number])
        prob_low = attn_prob.astype(jnp.bfloat16)
        d_prob = jnp.einsum(
            "qhd,khd->hqk", d_mixed_low, value_heads, preferred_element_type=jnp.float32
        )
        row_delta = jnp.sum(d_prob * attn_prob, axis=-1, keepdims=True)
        d_scores = (attn_prob * (d_prob - row_delta)).astype(jnp.bfloat16)
        d_query_parts.append(
            jnp.einsum("hqk,khd->qhd", d_scores, key_heads, preferred_element_type=jnp.float32)
            * score_scale
        )
        d_keys = (
            jnp.einsum("hqk,qhd->khd", d_scores, queries, preferred_element_type=jnp.float32)
            * score_scale
        )
        d_values = jnp.einsum(
            "hqk,qhd->khd", prob_low, d_mixed_low, preferred_element_type=jnp.float32
        )
    d_queries = d_query_parts[0]
    d_proj_low = jnp.concatenate(
        [
            d_queries.reshape(tok_rows, D),
            d_keys.reshape(tok_rows, D),
            d_values.reshape(tok_rows, D),
        ],
        axis=1,
    ).astype(jnp.bfloat16)
    d_bias_q = jnp.sum(d_proj_low[:, :D].astype(jnp.float32), axis=0)
    d_bias_v = jnp.sum(d_proj_low[:, 2 * D :].astype(jnp.float32), axis=0)
    d_qkv = over_tokens(normed_one, d_proj_low)
    d_normed_one = against_rows(d_proj_low, attn_full[:, : 3 * D])
    first_value, first_pull = jax.vjp(norm_affine, embedded, gain_f[:D], shift_f[:D])
    d_embed_norm, d_gain_one, d_shift_one = first_pull(d_normed_one)
    d_embedded = d_after + d_embed_norm
    is_masked = masked[:, None] == 1
    d_mask_vec = jnp.sum(jnp.where(is_masked, d_embedded, 0.0), axis=0)
    input_grad = jnp.where(is_masked, 0.0, d_embedded).astype(jnp.bfloat16)
    attn_grad = jnp.concatenate([d_qkv, d_outproj], axis=1)
    gain_grad = jnp.concatenate([d_gain_one, d_gain_two])
    offset_grad = jnp.concatenate(
        [
            d_shift_one,
            d_bias_q,
            d_bias_v,
            d_bias_out,
            d_shift_two,
            d_bias_two,
            d_mask_vec,
            d_bias_one,
        ]
    )
    return (input_grad, (attn_grad, mlp_grad, gain_grad, offset_grad))


def advance(gradient, weight, moment, average, learn_rate):
    moment_new = momentum_decay * moment + gradient
    weight_new = weight - learn_rate * (gradient + momentum_decay * moment_new)
    average_new = average_decay * average + (1.0 - average_decay) * weight_new
    return (weight_new, moment_new, average_new, weight_new.astype(jnp.bfloat16))


def per_device(
    tokens,
    cotangent,
    clip_index,
    key_valid,
    patch_masked,
    attn_weight,
    mlp_weight,
    gain_vector,
    offset_vector,
    attn_moment,
    mlp_moment,
    gain_moment,
    offset_moment,
    attn_average,
    mlp_average,
    gain_average,
    offset_average,
):
    attn_shard = attn_weight.astype(jnp.bfloat16)
    mlp_shard = mlp_weight.astype(jnp.bfloat16)
    gain_shard = gain_vector.astype(jnp.bfloat16)
    offset_shard = offset_vector.astype(jnp.bfloat16)
    params = (
        lax.all_gather(attn_shard, "fsdp", axis=0, tiled=True),
        lax.all_gather(mlp_shard, "fsdp", axis=0, tiled=True),
        lax.all_gather(gain_shard, "fsdp", axis=0, tiled=True),
        lax.all_gather(offset_shard, "fsdp", axis=0, tiled=True),
    )
    inputs = tokens.astype(jnp.float32)
    output, first_kept = forward(inputs, params, clip_index, key_valid, patch_masked)
    again = (
        lax.all_gather(attn_shard, "fsdp", axis=0, tiled=True),
        lax.all_gather(mlp_shard, "fsdp", axis=0, tiled=True),
        lax.all_gather(gain_shard, "fsdp", axis=0, tiled=True),
        lax.all_gather(offset_shard, "fsdp", axis=0, tiled=True),
    )
    output_again, kept_values = forward(inputs, again, clip_index, key_valid, patch_masked)
    input_grad, gradients = backward(
        cotangent, again, kept_values, clip_index, key_valid, patch_masked
    )
    owned = (
        lax.psum_scatter(gradients[0], "fsdp", scatter_dimension=0, tiled=True),
        lax.psum_scatter(gradients[1], "fsdp", scatter_dimension=0, tiled=True),
        lax.psum_scatter(gradients[2], "fsdp", scatter_dimension=0, tiled=True),
        lax.psum_scatter(gradients[3], "fsdp", scatter_dimension=0, tiled=True),
    )
    shares = (
        lax.psum_scatter(
            owned[0].astype(jnp.bfloat16), "rep", scatter_dimension=1, tiled=True
        ).astype(jnp.float32),
        lax.psum_scatter(
            owned[1].astype(jnp.bfloat16), "rep", scatter_dimension=1, tiled=True
        ).astype(jnp.float32),
        lax.psum_scatter(
            owned[2].astype(jnp.bfloat16), "rep", scatter_dimension=0, tiled=True
        ).astype(jnp.float32),
        lax.psum_scatter(
            owned[3].astype(jnp.bfloat16), "rep", scatter_dimension=0, tiled=True
        ).astype(jnp.float32),
    )
    reduced = (
        lax.all_gather(shares[0].astype(jnp.bfloat16), "rep", axis=1, tiled=True).astype(
            jnp.float32
        ),
        lax.all_gather(shares[1].astype(jnp.bfloat16), "rep", axis=1, tiled=True).astype(
            jnp.float32
        ),
        lax.all_gather(shares[2].astype(jnp.bfloat16), "rep", axis=0, tiled=True).astype(
            jnp.float32
        ),
        lax.all_gather(shares[3].astype(jnp.bfloat16), "rep", axis=0, tiled=True).astype(
            jnp.float32
        ),
    )
    learn_rate = base_rate / math.sqrt(
        tokens.shape[0] * lax.axis_size("rep") * lax.axis_size("fsdp")
    )
    attn_new, attn_momentum, attn_ema, attn_copy = advance(
        reduced[0], attn_weight, attn_moment, attn_average, learn_rate
    )
    mlp_new, mlp_momentum, mlp_ema, mlp_copy = advance(
        reduced[1], mlp_weight, mlp_moment, mlp_average, learn_rate
    )
    gain_new, gain_momentum, gain_ema, gain_copy = advance(
        reduced[2], gain_vector, gain_moment, gain_average, learn_rate
    )
    offset_new, offset_momentum, offset_ema, offset_copy = advance(
        reduced[3], offset_vector, offset_moment, offset_average, learn_rate
    )
    return (
        output.astype(jnp.bfloat16),
        input_grad,
        attn_new,
        attn_momentum,
        attn_ema,
        attn_copy,
        mlp_new,
        mlp_momentum,
        mlp_ema,
        mlp_copy,
        gain_new,
        gain_momentum,
        gain_ema,
        gain_copy,
        offset_new,
        offset_momentum,
        offset_ema,
        offset_copy,
    )


def scalars(co):
    return co[0], co[1], co[2], co[3]


def call(kernel, outs, args, flops=0, limit=24):
    specs = []
    total = 0
    for arg in args:
        if arg.dtype == jnp.int32 and arg.ndim == 1:
            specs.append(pl.BlockSpec(memory_space=pltpu.SMEM))
        else:
            specs.append(pl.BlockSpec(memory_space=pltpu.VMEM))
        total += arg.size * arg.dtype.itemsize
    for shape, dtype in outs:
        total += math.prod(shape) * jnp.dtype(dtype).itemsize
    return pl.pallas_call(
        kernel,
        out_shape=[jax.ShapeDtypeStruct(shape, dtype) for shape, dtype in outs],
        in_specs=specs,
        out_specs=[pl.BlockSpec(memory_space=pltpu.VMEM)] * len(outs),
        compiler_params=pltpu.CompilerParams(vmem_limit_bytes=limit * 2**20),
        cost_estimate=pl.CostEstimate(flops=flops, bytes_accessed=total, transcendentals=0),
    )


def lanes(offset, size):
    return pl.ds(pl.multiple_of(offset, 128), size)


def nn(left, right):
    return lax.dot_general(left, right, (((1,), (0,)), ((), ())), preferred_element_type=jnp.float32)


def nt(left, right):
    return lax.dot_general(left, right, (((1,), (1,)), ((), ())), preferred_element_type=jnp.float32)


def row_norm(values):
    mean = jnp.mean(values, axis=-1, keepdims=True)
    centred = values - mean
    var = jnp.mean(centred * centred, axis=-1, keepdims=True)
    rstd = lax.rsqrt(var + norm_eps)
    return centred * rstd, rstd


def prep_kernel(co, attn, mlp, s0, s1, s2, w2):
    r = co[0]
    for part in range(3):
        s0[:, part * 384 : part * 384 + 384] = attn[:, lanes(part * D + 384 * r, 384)].astype(BF)
    s1[:, :384] = attn[:, lanes(3 * D + 384 * r, 384)].astype(BF)
    s1[:, 384:] = mlp[:, lanes(1536 * r, 768)].astype(BF)
    s2[...] = mlp[:, lanes(1536 * r + 768, 768)].astype(BF)
    w2[...] = mlp[:, FF:].astype(BF)


def assemble_kernel(maps, co, *refs):
    r, z, y, c = scalars(co)
    pieces = refs[:8]
    outs = refs[8:]
    for number in range(8):
        a, b, i = number // 4, (number // 2) % 2, number % 2
        half = lax.bitwise_xor(r, b)
        for k in range(4):
            zi, yi, ci = lax.bitwise_xor(z, k), lax.bitwise_xor(y, i), lax.bitwise_xor(c, a)
            for out, src, size, base, stride in maps:
                outs[out][zi, yi, ci, :, lanes(base + stride * half, size)] = pieces[number][
                    k * 48 : k * 48 + 48, src : src + size
                ]


def first_norm_kernel(tokens, masked, vec, h1, h1t):
    x0 = jnp.where(masked[...] == 1, vec[8:9, :], tokens[...].astype(F32))
    xh, rstd = row_norm(x0)
    h = xh * vec[0:1, :] + vec[2:3, :]
    h1[...] = h.astype(BF)
    h1t[...] = h.T.astype(BF)


def allowed_pairs(clip_col, clip_row, valid_col):
    return (clip_col[...] == clip_row[...]) & (valid_col[...] == 1)


def attention_kernel(h1, weight, vec, clip_col, clip_row, valid_col, qkv, att, lse):
    for part in range(3):
        out = nn(h1[...], weight[:, part * D : part * D + D])
        if part != 1:
            out = out + vec[3:4, :] if part == 0 else out + vec[4:5, :]
        qkv[:, part * D : part * D + D] = out.astype(BF)
    allowed = allowed_pairs(clip_col, clip_row, valid_col)
    low = lax.broadcasted_iota(jnp.int32, (256, 128), 1) < 64
    for pair in range(6):
        q2 = qkv[:, pair * 128 : pair * 128 + 128]
        k2 = qkv[:, D + pair * 128 : D + pair * 128 + 128]
        v2 = qkv[:, 2 * D + pair * 128 : 2 * D + pair * 128 + 128]
        mixed = []
        for side in range(2):
            qm = jnp.where(low if side == 0 else ~low, q2, jnp.zeros_like(q2))
            s = jnp.where(allowed, nt(k2, qm) * 0.125, mask_fill)
            peak = jnp.max(s, axis=0, keepdims=True)
            e = jnp.exp(s - peak)
            total = jnp.sum(e, axis=0, keepdims=True)
            prob = (e * (1.0 / total)).astype(BF)
            lse[2 * pair + side : 2 * pair + side + 1, :] = peak + jnp.log(total)
            mixed.append(over_tokens(prob, v2))
        att[:, pair * 128 : pair * 128 + 128] = jnp.where(low, mixed[0], mixed[1]).astype(BF)


def second_norm_kernel(tokens, masked, att, weight, vec, y1, h2, h2t):
    x0 = jnp.where(masked[...] == 1, vec[8:9, :], tokens[...].astype(F32))
    y = x0 + nt(att[...], weight[...]) + vec[5:6, :]
    y1[...] = y
    xh, rstd = row_norm(y)
    h = xh * vec[1:2, :] + vec[6:7, :]
    h2[...] = h.astype(BF)
    h2t[...] = h.T.astype(BF)


def hidden_kernel(part, h2, weight, vec, g, slope):
    for half in range(2):
        for sub in range(0, D, 256):
            u = nn(h2[...], weight[:, half * D + sub : half * D + sub + 256])
            u = u + vec[9 + 2 * half + part : 10 + 2 * half + part, sub : sub + 256]
            phi = 0.5 * (1.0 + lax.erf(u * math.sqrt(0.5)))
            g[:, half * D + sub : half * D + sub + 256] = (u * phi).astype(BF)
            slope[:, half * D + sub : half * D + sub + 256] = phi + u * (
                jnp.exp(-0.5 * u * u) * (1.0 / math.sqrt(2.0 * math.pi))
            )


def down_grad_kernel(dz, g0, g1, out, dzt):
    dzt[...] = dz[...].astype(F32).T.astype(BF)
    for half in range(2):
        for part, g in ((0, g0), (1, g1)):
            for sub in range(0, D, 384):
                res = nn(dzt[...], g[:, half * D + sub : half * D + sub + 384])
                start = half * 2 * D + part * D + sub
                out[:, start : start + 384] = res.astype(BF)


def hidden_grad_kernel(dz, weight, y1, g0, g1, slope0, slope1, vec, du0, du1, db1, act):
    acc = y1[...] + vec[7:8, :]
    for half in range(2):
        for part, g, slope, du in ((0, g0, slope0, du0), (1, g1, slope1, du1)):
            start = half * 2 * D + part * D
            w = weight[:, start : start + D]
            da = nn(dz[...], w)
            d = (da * slope[:, half * D : half * D + D]).astype(BF)
            du[:, half * D : half * D + D] = d
            row = 2 * half + part
            db1[row : row + 1, :] = jnp.sum(d.astype(F32), axis=0, keepdims=True)
            acc = acc + nt(g[:, half * D : half * D + D], w)
    act[...] = acc.astype(BF)


def weight_grad_kernel(groups, width, co, left, right, send, keep, scratch):
    r, z, y, c = scalars(co)
    for b in range(2):
        half = lax.bitwise_xor(r, b)
        for col, size, base, stride in groups:
            for sub in range(0, size, 384):
                scratch[...] = nn(left[...], right[:, lanes(base + stride * half + sub, 384)])
                dst = b * width + col + sub
                for k in range(4):
                    for i in range(2):
                        row = k * 192 + i * 96
                        send[k, i, :, dst : dst + 384] = scratch[
                            pl.ds(pl.multiple_of(row + 48 * (1 - c), 16), 48), :
                        ].astype(BF)
                        keep[k, i, :, dst : dst + 384] = scratch[
                            pl.ds(pl.multiple_of(row + 48 * c, 16), 48), :
                        ]


def second_back_kernel(dz, du0, du1, w0, w1, y1, weight_o, vec, dy1, datt, dpt, small):
    dh = nt(du0[...], w0[...]) + nt(du1[...], w1[...])
    yh, rstd = row_norm(y1[...])
    dy = dz[...].astype(F32)
    small[0:1, :] = jnp.sum(dh * yh, axis=0, keepdims=True)
    small[1:2, :] = jnp.sum(dh, axis=0, keepdims=True)
    small[3:4, :] = jnp.sum(dy, axis=0, keepdims=True)
    e = dh * vec[1:2, :]
    d = dy + rstd * (
        e - jnp.mean(e, axis=-1, keepdims=True) - yh * jnp.mean(e * yh, axis=-1, keepdims=True)
    )
    dy1[...] = d
    small[2:3, :] = jnp.sum(d, axis=0, keepdims=True)
    dp = d.astype(BF)
    dpt[...] = d.T.astype(BF)
    datt[...] = nn(dp, weight_o[...]).astype(BF)


def attention_back_kernel(qkv, datt, lse, clip_col, clip_row, valid_col, dqkv, small):
    allowed = allowed_pairs(clip_col, clip_row, valid_col)
    low = lax.broadcasted_iota(jnp.int32, (256, 128), 1) < 64
    for pair in range(6):
        cols = slice(pair * 128, pair * 128 + 128)
        q2 = qkv[:, pair * 128 : pair * 128 + 128]
        k2 = qkv[:, D + pair * 128 : D + pair * 128 + 128]
        v2 = qkv[:, 2 * D + pair * 128 : 2 * D + pair * 128 + 128]
        o2 = datt[:, cols]
        dqs, dks, dvs = [], [], []
        for side in range(2):
            mine = low if side == 0 else ~low
            qm = jnp.where(mine, q2, jnp.zeros_like(q2))
            om = jnp.where(mine, o2, jnp.zeros_like(o2))
            s = jnp.where(allowed, nt(k2, qm) * 0.125, mask_fill)
            prob = jnp.exp(s - lse[2 * pair + side : 2 * pair + side + 1, :])
            dprob = nt(v2, om)
            delta = jnp.sum(dprob * prob, axis=0, keepdims=True)
            ds = (prob * (dprob - delta)).astype(BF)
            dqs.append(over_tokens(ds, k2))
            dks.append(nn(ds, q2))
            dvs.append(nn(prob.astype(BF), o2))
        dq = (jnp.where(low, dqs[0], dqs[1]) * 0.125).astype(BF)
        dk = (jnp.where(low, dks[0], dks[1]) * 0.125).astype(BF)
        dv = jnp.where(low, dvs[0], dvs[1]).astype(BF)
        dqkv[:, cols] = dq
        dqkv[:, D + pair * 128 : D + pair * 128 + 128] = dk
        dqkv[:, 2 * D + pair * 128 : 2 * D + pair * 128 + 128] = dv
        small[0:1, cols] = jnp.sum(dq.astype(F32), axis=0, keepdims=True)
        small[1:2, cols] = jnp.sum(dv.astype(F32), axis=0, keepdims=True)


def first_back_kernel(
    dqkv, weight, tokens, masked, dy1, vec, db1, small2, small_a, input_grad, total
):
    dh = nt(dqkv[...], weight[...])
    hidden = masked[...] == 1
    x0 = jnp.where(hidden, vec[8:9, :], tokens[...].astype(F32))
    xh, rstd = row_norm(x0)
    e = dh * vec[0:1, :]
    dx = dy1[...] + rstd * (
        e - jnp.mean(e, axis=-1, keepdims=True) - xh * jnp.mean(e * xh, axis=-1, keepdims=True)
    )
    input_grad[...] = jnp.where(hidden, 0.0, dx).astype(BF)
    total[0:1, :] = jnp.sum(dh * xh, axis=0, keepdims=True)
    total[1:2, :] = small2[0:1, :]
    total[2:3, :] = jnp.sum(dh, axis=0, keepdims=True)
    total[3:5, :] = small_a[0:2, :]
    total[5:6, :] = small2[2:3, :]
    total[6:7, :] = small2[1:2, :]
    total[7:8, :] = small2[3:4, :]
    total[8:9, :] = jnp.sum(jnp.where(hidden, dx, 0.0), axis=0, keepdims=True)
    total[9:13, :] = db1[0:4, :]
    total[13:16, :] = jnp.zeros((3, D), F32)


def sum_cores_kernel(width, keep, got, x_send, x_keep):
    x_keep[...] = keep[:, :width] + got[:, :width].astype(F32)
    x_send[...] = (keep[:, width:] + got[:, width:].astype(F32)).astype(BF)


def sum_reps_kernel(co, keep, got, y_send, y_keep):
    y = co[2]
    for k in range(4):
        y_send[k] = (keep[k, 1 - y] + got[k, 1 - y].astype(F32)).astype(BF)
        y_keep[k] = keep[k, y] + got[k, y].astype(F32)


def sum_y_kernel(co, keep, got, z1, z2, z3, z_keep):
    z = co[1]
    for k, out in ((1, z1), (2, z2), (3, z3)):
        at = lax.bitwise_xor(z, k)
        out[...] = (keep[at] + got[at].astype(F32)).astype(BF)
    z_keep[...] = keep[z] + got[z].astype(F32)


def sum_z_kernel(keep, g1, g2, g3, out):
    out[...] = (
        keep[...] + g1[...].astype(F32) + g2[...].astype(F32) + g3[...].astype(F32)
    ).astype(BF)


def update_kernel(rate, co, *refs):
    ins, outs = refs[:16], refs[16:]
    attn, mlp = ins[0:3], ins[3:6]
    qkv_g, out_g, up0_g, up1_g = ins[6:8], ins[8:10], ins[10:12], ins[12:14]
    down_g = ins[14:16]
    r = co[0]

    def step(state, new, start, size, grad):
        cols = lanes(start, size)
        w, m, a = (ref[:, cols] for ref in state)
        m_new = momentum_decay * m + grad
        w_new = w - rate * (grad + momentum_decay * m_new)
        new[0][:, cols] = w_new
        new[1][:, cols] = m_new
        new[2][:, cols] = average_decay * a + (1.0 - average_decay) * w_new
        new[3][:, cols] = w_new.astype(BF)

    for b in range(2):
        half = lax.bitwise_xor(r, b)
        for part in range(3):
            grad = qkv_g[b][:, part * 384 : part * 384 + 384].astype(F32)
            step(attn, outs[:4], part * D + 384 * half, 384, grad)
        step(attn, outs[:4], 3 * D + 384 * half, 384, out_g[b][...].astype(F32))
        step(mlp, outs[4:], 1536 * half, 768, up0_g[b][...].astype(F32))
        step(mlp, outs[4:], 1536 * half + 768, 768, up1_g[b][...].astype(F32))
    for start in range(0, FF, 768):
        grad = down_g[0][:, start : start + 768].astype(F32) + down_g[1][
            :, start : start + 768
        ].astype(F32)
        step(mlp, outs[4:], FF + start, 768, grad)


def fast_device(
    tokens,
    cotangent,
    clip_index,
    key_valid,
    patch_masked,
    attn_weight,
    mlp_weight,
    gain_vector,
    offset_vector,
    attn_moment,
    mlp_moment,
    gain_moment,
    offset_moment,
    attn_average,
    mlp_average,
    gain_average,
    offset_average,
):
    r, f = lax.axis_index("rep"), lax.axis_index("fsdp")
    co = jnp.stack([r, f // 4, (f // 2) % 2, f % 2]).astype(jnp.int32)

    def swap(array, mask):
        return lax.ppermute(array, ("rep", "fsdp"), [(i, i ^ mask) for i in range(32)])

    CORE, Y, Z, X = 1, 2, 4, 16

    s0, s1, s2, w2_shard = call(
        prep_kernel,
        [((48, 1152), BF), ((48, 1152), BF), ((48, 768), BF), ((48, FF), BF)],
        [co, attn_weight, mlp_weight],
    )(co, attn_weight, mlp_weight)
    flat = jnp.zeros((16 * D,), F32)
    flat = lax.dynamic_update_slice(flat, gain_vector.astype(BF).astype(F32), (96 * f,))
    flat = lax.dynamic_update_slice(flat, offset_vector.astype(BF).astype(F32), (2 * D + 528 * f,))
    vec = flat.reshape(16, D)
    for mask in (CORE, Y, Z, 2 * Z):
        vec = vec + swap(vec, mask)
    w2 = lax.all_gather(w2_shard, "fsdp", axis=0, tiled=True)

    def gather(shard, maps, widths):
        stack = jnp.concatenate([shard] + [swap(shard, Z * k) for k in (1, 2, 3)], axis=0)
        across = swap(stack, Y)
        mine = [stack, across, swap(stack, X), swap(across, X)]
        pieces = mine + [swap(piece, CORE) for piece in mine]
        outs = [((4, 2, 2, 48, width), BF) for width in widths]
        args = [co] + pieces
        full = call(functools.partial(assemble_kernel, maps), outs, args)(*args)
        return [w.reshape(D, -1) for w in full]

    (w_qkv,) = gather(s0, [(0, part * 384, 384, part * D, 384) for part in range(3)], [3 * D])
    w_out, w_up0 = gather(s1, [(0, 0, 384, 0, 384), (1, 384, 768, 0, 768)], [D, 2 * D])
    (w_up1,) = gather(s2, [(0, 0, 768, 0, 768)], [2 * D])

    masked = patch_masked[:, None]
    clip_col, clip_row, valid_col = clip_index[:, None], clip_index[None, :], key_valid[:, None]
    args = [tokens, masked, vec]
    h1, h1t = call(first_norm_kernel, [((256, D), BF), ((D, 256), BF)], args)(*args)
    args = [h1, w_qkv, vec, clip_col, clip_row, valid_col]
    qkv, att, lse = call(
        attention_kernel,
        [((256, 3 * D), BF), ((256, D), BF), ((16, 256), F32)],
        args,
        flops=2_000_000_000,
    )(*args)
    args = [tokens, masked, att, w_out, vec]
    y1, h2, h2t = call(
        second_norm_kernel, [((256, D), F32), ((256, D), BF), ((D, 256), BF)], args, flops=10**9
    )(*args)
    hidden = []
    for part, weight in ((0, w_up0), (1, w_up1)):
        args = [h2, weight, vec]
        hidden.append(
            call(
                functools.partial(hidden_kernel, part),
                [((256, 2 * D), BF), ((256, 2 * D), F32)],
                args,
                flops=10**9,
            )(*args)
        )
    (g0, slope0), (g1, slope1) = hidden

    args = [cotangent, g0, g1]
    down_local, _ = call(down_grad_kernel, [((D, FF), BF), ((D, 256), BF)], args, flops=10**9)(*args)
    down_mine = lax.psum_scatter(down_local, "fsdp", scatter_dimension=0, tiled=True)
    args = [cotangent, w2, y1, g0, g1, slope0, slope1, vec]
    du0, du1, db1, activations = call(
        hidden_grad_kernel,
        [((256, 2 * D), BF), ((256, 2 * D), BF), ((8, D), F32), ((256, D), BF)],
        args,
        flops=3 * 10**9,
        limit=30,
    )(*args)

    def weight_grad(left, right, groups, width):
        args = [co, left, right]
        specs = [pl.BlockSpec(memory_space=pltpu.SMEM)] + [pl.BlockSpec(memory_space=pltpu.VMEM)] * 2
        return pl.pallas_call(
            functools.partial(weight_grad_kernel, groups, width),
            out_shape=[
                jax.ShapeDtypeStruct((4, 2, 48, 2 * width), BF),
                jax.ShapeDtypeStruct((4, 2, 48, 2 * width), F32),
            ],
            in_specs=specs,
            out_specs=[pl.BlockSpec(memory_space=pltpu.VMEM)] * 2,
            scratch_shapes=[pltpu.VMEM((D, 384), F32)],
            compiler_params=pltpu.CompilerParams(vmem_limit_bytes=20 * 2**20),
            cost_estimate=pl.CostEstimate(
                flops=2 * 256 * D * 2 * width, bytes_accessed=10 * 384 * width, transcendentals=0
            ),
        )(*args)

    def reduce(local, width):
        send, keep = local
        got = swap(send.reshape(384, 2 * width), CORE)
        args = [keep.reshape(384, 2 * width), got]
        x_send, x_keep = call(
            functools.partial(sum_cores_kernel, width), [((384, width), BF), ((384, width), F32)], args
        )(*args)
        got = swap(x_send, X)
        args = [co, x_keep.reshape(4, 2, 48, width), got.reshape(4, 2, 48, width)]
        y_send, y_keep = call(
            sum_reps_kernel, [((4, 48, width), BF), ((4, 48, width), F32)], args
        )(*args)
        got = swap(y_send, Y)
        args = [co, y_keep, got]
        *z_send, z_keep = call(
            sum_y_kernel, [((48, width), BF)] * 3 + [((48, width), F32)], args
        )(*args)
        args = [z_keep] + [swap(z_send[k - 1], Z * k) for k in (1, 2, 3)]
        (mine,) = call(sum_z_kernel, [((48, width), BF)], args)(*args)
        return mine, swap(mine, X)

    up_groups = [(0, 768, 0, 768)]
    up0_g = reduce(weight_grad(h2t, du0, up_groups, 768), 768)
    up1_g = reduce(weight_grad(h2t, du1, up_groups, 768), 768)
    args = [cotangent, du0, du1, w_up0, w_up1, y1, w_out, vec]
    dy1, datt, dpt, small2 = call(
        second_back_kernel,
        [((256, D), F32), ((256, D), BF), ((D, 256), BF), ((8, D), F32)],
        args,
        flops=3 * 10**9,
    )(*args)
    out_g = reduce(weight_grad(dpt, att, [(0, 384, 0, 384)], 384), 384)
    args = [qkv, datt, lse, clip_col, clip_row, valid_col]
    dqkv, small_a = call(
        attention_back_kernel, [((256, 3 * D), BF), ((8, D), F32)], args, flops=3 * 10**9
    )(*args)
    qkv_groups = [(part * 384, 384, part * D, 384) for part in range(3)]
    qkv_g = reduce(weight_grad(h1t, dqkv, qkv_groups, 1152), 1152)
    args = [dqkv, w_qkv, tokens, masked, dy1, vec, db1, small2, small_a]
    input_grad, total = call(
        first_back_kernel, [((256, D), BF), ((16, D), F32)], args, flops=10**9
    )(*args)
    for mask in (CORE, Y, Z, 2 * Z, X):
        total = total + swap(total, mask)
    flat = total.reshape(-1)
    gain_g = lax.dynamic_slice(flat, (96 * f,), (96,))
    offset_g = lax.dynamic_slice(flat, (2 * D + 528 * f,), (528,))

    rate = base_rate / math.sqrt(tokens.shape[0] * 32)
    args = [co, attn_weight, attn_moment, attn_average, mlp_weight, mlp_moment, mlp_average]
    args += [*qkv_g, *out_g, *up0_g, *up1_g, down_mine, swap(down_mine, X)]
    updated = call(
        functools.partial(update_kernel, rate),
        [((48, 4 * D), F32)] * 3
        + [((48, 4 * D), BF)]
        + [((48, 2 * FF), F32)] * 3
        + [((48, 2 * FF), BF)],
        args,
    )(*args)
    gains = advance(gain_g, gain_vector, gain_moment, gain_average, rate)
    offsets = advance(offset_g, offset_vector, offset_moment, offset_average, rate)
    return (activations, input_grad, *updated, *gains, *offsets)


def solution(mesh):
    placed = (
        P(("rep", "fsdp"), None),
        P(("rep", "fsdp"), None),
        P(("rep", "fsdp")),
        P(("rep", "fsdp")),
        P(("rep", "fsdp")),
        P("fsdp", None),
        P("fsdp", None),
        P("fsdp"),
        P("fsdp"),
        P("fsdp", None),
        P("fsdp", None),
        P("fsdp"),
        P("fsdp"),
        P("fsdp", None),
        P("fsdp", None),
        P("fsdp"),
        P("fsdp"),
    )
    small = mesh.shape["rep"] == 2 and mesh.shape["fsdp"] == 16
    return jax.shard_map(
        fast_device if small else per_device,
        mesh=mesh,
        in_specs=placed,
        out_specs=(
            P(("rep", "fsdp"), None),
            P(("rep", "fsdp"), None),
            P("fsdp", None),
            P("fsdp", None),
            P("fsdp", None),
            P("fsdp", None),
            P("fsdp", None),
            P("fsdp", None),
            P("fsdp", None),
            P("fsdp", None),
            P("fsdp"),
            P("fsdp"),
            P("fsdp"),
            P("fsdp"),
            P("fsdp"),
            P("fsdp"),
            P("fsdp"),
            P("fsdp"),
        ),
        check_vma=False,
    )
```

```python
import functools
import math

import jax
import jax.numpy as jnp
from jax import lax
from jax.experimental import pallas as pl
from jax.experimental.pallas import tpu as pltpu
from jax.sharding import PartitionSpec as P

D = 768
HEADS = 12
HEAD_DIM = 64
FF = 3072
BF = jnp.bfloat16
F32 = jnp.float32


momentum_decay = 0.9
average_decay = 0.8
base_rate = 0.02
norm_eps = 1e-06
mask_fill = -1e30


def normalize(inputs):
    mean_val = jnp.mean(inputs, axis=-1, keepdims=True)
    centred = inputs - mean_val
    variance = jnp.mean(centred * centred, axis=-1, keepdims=True)
    return centred * lax.rsqrt(variance + norm_eps)


def norm_affine(inputs, gain_part, shift_part):
    return normalize(inputs) * gain_part + shift_part


def gelu_exact(inputs):
    return jax.nn.gelu(inputs, approximate=False)


def over_tokens(left_mat, right_mat):
    return lax.dot_general(
        left_mat, right_mat, (((0,), (0,)), ((), ())), preferred_element_type=jnp.float32
    )


def against_rows(left_mat, right_mat):
    return lax.dot_general(
        left_mat, right_mat, (((1,), (1,)), ((), ())), preferred_element_type=jnp.float32
    )


def block_mask(clip_ids, key_ok):
    return (clip_ids[:, None] == clip_ids[None, :]) & (key_ok[None, :] == 1)


def forward(inputs, params, clip_ids, key_ok, masked):
    attn_full = params[0]
    mlp_full = params[1]
    gain_f = params[2].astype(jnp.float32)
    shift_f = params[3].astype(jnp.float32)
    tok_rows = inputs.shape[0]
    score_scale = HEAD_DIM ** (-0.5)
    is_masked = masked[:, None] == 1
    embedded = jnp.where(is_masked, shift_f[6 * D : 7 * D][None, :], inputs)
    normed_one = norm_affine(embedded, gain_f[:D], shift_f[:D]).astype(jnp.bfloat16)
    qkv_bias = jnp.concatenate(
        [shift_f[D : 2 * D], jnp.zeros((D,), jnp.float32), shift_f[2 * D : 3 * D]]
    )
    projected = (
        jnp.dot(normed_one, attn_full[:, : 3 * D], preferred_element_type=jnp.float32) + qkv_bias
    )
    projected = projected.astype(jnp.bfloat16)
    queries = projected[:, :D].reshape(tok_rows, HEADS, HEAD_DIM)
    key_heads = projected[:, D : 2 * D].reshape(tok_rows, HEADS, HEAD_DIM)
    value_heads = projected[:, 2 * D :].reshape(tok_rows, HEADS, HEAD_DIM)
    allowed = block_mask(clip_ids, key_ok)
    scores = (
        jnp.einsum("qhd,khd->hqk", queries, key_heads, preferred_element_type=jnp.float32)
        * score_scale
    )
    scores = jnp.where(allowed[None], scores, mask_fill)
    row_peak = jnp.max(scores, axis=-1, keepdims=True)
    exponent = jnp.exp(scores - row_peak)
    summed = jnp.sum(exponent, axis=-1, keepdims=True)
    attn_prob = (exponent / summed).astype(jnp.bfloat16)
    mixed_parts = jnp.einsum(
        "hqk,khd->qhd", attn_prob, value_heads, preferred_element_type=jnp.float32
    )
    lse_parts = [row_peak + jnp.log(summed)]
    mixed_out = mixed_parts.reshape(tok_rows, D).astype(jnp.bfloat16)
    after_attn = embedded + against_rows(mixed_out, attn_full[:, 3 * D :]) + shift_f[3 * D : 4 * D]
    normed_two = norm_affine(after_attn, gain_f[D:], shift_f[4 * D : 5 * D]).astype(jnp.bfloat16)
    hidden_pre = (
        jnp.dot(normed_two, mlp_full[:, :FF], preferred_element_type=jnp.float32) + shift_f[7 * D :]
    )
    hidden_act = gelu_exact(hidden_pre).astype(jnp.bfloat16)
    output = after_attn + against_rows(hidden_act, mlp_full[:, FF:]) + shift_f[5 * D : 6 * D]
    kept_values = (
        embedded,
        normed_one,
        queries,
        key_heads,
        value_heads,
        lse_parts,
        mixed_out,
        after_attn,
        normed_two,
        hidden_pre,
        hidden_act,
        gain_f,
        shift_f,
    )
    return (output, kept_values)


def backward(cotangent, params, kept_values, clip_ids, key_ok, masked):
    attn_full = params[0]
    mlp_full = params[1]
    (
        embedded,
        normed_one,
        queries,
        key_heads,
        value_heads,
        lse_parts,
        mixed_out,
        after_attn,
        normed_two,
        hidden_pre,
        hidden_act,
        gain_f,
        shift_f,
    ) = kept_values
    tok_rows = cotangent.shape[0]
    score_scale = HEAD_DIM ** (-0.5)
    d_out = cotangent.astype(jnp.float32)
    d_bias_two = jnp.sum(d_out, axis=0)
    d_down = over_tokens(cotangent, hidden_act)
    d_act = jnp.dot(cotangent, mlp_full[:, FF:], preferred_element_type=jnp.float32)
    gelu_value, gelu_pull = jax.vjp(gelu_exact, hidden_pre)
    d_pre_low = gelu_pull(d_act)[0].astype(jnp.bfloat16)
    d_bias_one = jnp.sum(d_pre_low.astype(jnp.float32), axis=0)
    d_up = over_tokens(normed_two, d_pre_low)
    mlp_grad = jnp.concatenate([d_up, d_down], axis=1)
    d_normed_two = against_rows(d_pre_low, mlp_full[:, :FF])
    norm_value, norm_pull = jax.vjp(norm_affine, after_attn, gain_f[D:], shift_f[4 * D : 5 * D])
    d_after_norm, d_gain_two, d_shift_two = norm_pull(d_normed_two)
    d_after = d_out + d_after_norm
    d_after_low = d_after.astype(jnp.bfloat16)
    d_bias_out = jnp.sum(d_after, axis=0)
    d_outproj = over_tokens(d_after_low, mixed_out)
    d_mixed = jnp.dot(d_after_low, attn_full[:, 3 * D :], preferred_element_type=jnp.float32)
    d_mixed_low = d_mixed.astype(jnp.bfloat16).reshape(tok_rows, HEADS, HEAD_DIM)
    block_rows = min(512, tok_rows)
    d_query_parts = []
    d_keys = jnp.zeros((tok_rows, HEADS, HEAD_DIM), jnp.float32)
    d_values = jnp.zeros((tok_rows, HEADS, HEAD_DIM), jnp.float32)
    for block_number, offset in enumerate(range(0, tok_rows, block_rows)):
        allowed = block_mask(clip_ids, key_ok)
        scores = (
            jnp.einsum("qhd,khd->hqk", queries, key_heads, preferred_element_type=jnp.float32)
            * score_scale
        )
        scores = jnp.where(allowed[None], scores, mask_fill)
        attn_prob = jnp.exp(scores - lse_parts[block_number])
        prob_low = attn_prob.astype(jnp.bfloat16)
        d_prob = jnp.einsum(
            "qhd,khd->hqk", d_mixed_low, value_heads, preferred_element_type=jnp.float32
        )
        row_delta = jnp.sum(d_prob * attn_prob, axis=-1, keepdims=True)
        d_scores = (attn_prob * (d_prob - row_delta)).astype(jnp.bfloat16)
        d_query_parts.append(
            jnp.einsum("hqk,khd->qhd", d_scores, key_heads, preferred_element_type=jnp.float32)
            * score_scale
        )
        d_keys = (
            jnp.einsum("hqk,qhd->khd", d_scores, queries, preferred_element_type=jnp.float32)
            * score_scale
        )
        d_values = jnp.einsum(
            "hqk,qhd->khd", prob_low, d_mixed_low, preferred_element_type=jnp.float32
        )
    d_queries = d_query_parts[0]
    d_proj_low = jnp.concatenate(
        [
            d_queries.reshape(tok_rows, D),
            d_keys.reshape(tok_rows, D),
            d_values.reshape(tok_rows, D),
        ],
        axis=1,
    ).astype(jnp.bfloat16)
    d_bias_q = jnp.sum(d_proj_low[:, :D].astype(jnp.float32), axis=0)
    d_bias_v = jnp.sum(d_proj_low[:, 2 * D :].astype(jnp.float32), axis=0)
    d_qkv = over_tokens(normed_one, d_proj_low)
    d_normed_one = against_rows(d_proj_low, attn_full[:, : 3 * D])
    first_value, first_pull = jax.vjp(norm_affine, embedded, gain_f[:D], shift_f[:D])
    d_embed_norm, d_gain_one, d_shift_one = first_pull(d_normed_one)
    d_embedded = d_after + d_embed_norm
    is_masked = masked[:, None] == 1
    d_mask_vec = jnp.sum(jnp.where(is_masked, d_embedded, 0.0), axis=0)
    input_grad = jnp.where(is_masked, 0.0, d_embedded).astype(jnp.bfloat16)
    attn_grad = jnp.concatenate([d_qkv, d_outproj], axis=1)
    gain_grad = jnp.concatenate([d_gain_one, d_gain_two])
    offset_grad = jnp.concatenate(
        [
            d_shift_one,
            d_bias_q,
            d_bias_v,
            d_bias_out,
            d_shift_two,
            d_bias_two,
            d_mask_vec,
            d_bias_one,
        ]
    )
    return (input_grad, (attn_grad, mlp_grad, gain_grad, offset_grad))


def advance(gradient, weight, moment, average, learn_rate):
    moment_new = momentum_decay * moment + gradient
    weight_new = weight - learn_rate * (gradient + momentum_decay * moment_new)
    average_new = average_decay * average + (1.0 - average_decay) * weight_new
    return (weight_new, moment_new, average_new, weight_new.astype(jnp.bfloat16))


def per_device(
    tokens,
    cotangent,
    clip_index,
    key_valid,
    patch_masked,
    attn_weight,
    mlp_weight,
    gain_vector,
    offset_vector,
    attn_moment,
    mlp_moment,
    gain_moment,
    offset_moment,
    attn_average,
    mlp_average,
    gain_average,
    offset_average,
):
    attn_shard = attn_weight.astype(jnp.bfloat16)
    mlp_shard = mlp_weight.astype(jnp.bfloat16)
    gain_shard = gain_vector.astype(jnp.bfloat16)
    offset_shard = offset_vector.astype(jnp.bfloat16)
    params = (
        lax.all_gather(attn_shard, "fsdp", axis=0, tiled=True),
        lax.all_gather(mlp_shard, "fsdp", axis=0, tiled=True),
        lax.all_gather(gain_shard, "fsdp", axis=0, tiled=True),
        lax.all_gather(offset_shard, "fsdp", axis=0, tiled=True),
    )
    inputs = tokens.astype(jnp.float32)
    output, first_kept = forward(inputs, params, clip_index, key_valid, patch_masked)
    again = (
        lax.all_gather(attn_shard, "fsdp", axis=0, tiled=True),
        lax.all_gather(mlp_shard, "fsdp", axis=0, tiled=True),
        lax.all_gather(gain_shard, "fsdp", axis=0, tiled=True),
        lax.all_gather(offset_shard, "fsdp", axis=0, tiled=True),
    )
    output_again, kept_values = forward(inputs, again, clip_index, key_valid, patch_masked)
    input_grad, gradients = backward(
        cotangent, again, kept_values, clip_index, key_valid, patch_masked
    )
    owned = (
        lax.psum_scatter(gradients[0], "fsdp", scatter_dimension=0, tiled=True),
        lax.psum_scatter(gradients[1], "fsdp", scatter_dimension=0, tiled=True),
        lax.psum_scatter(gradients[2], "fsdp", scatter_dimension=0, tiled=True),
        lax.psum_scatter(gradients[3], "fsdp", scatter_dimension=0, tiled=True),
    )
    shares = (
        lax.psum_scatter(
            owned[0].astype(jnp.bfloat16), "rep", scatter_dimension=1, tiled=True
        ).astype(jnp.float32),
        lax.psum_scatter(
            owned[1].astype(jnp.bfloat16), "rep", scatter_dimension=1, tiled=True
        ).astype(jnp.float32),
        lax.psum_scatter(
            owned[2].astype(jnp.bfloat16), "rep", scatter_dimension=0, tiled=True
        ).astype(jnp.float32),
        lax.psum_scatter(
            owned[3].astype(jnp.bfloat16), "rep", scatter_dimension=0, tiled=True
        ).astype(jnp.float32),
    )
    reduced = (
        lax.all_gather(shares[0].astype(jnp.bfloat16), "rep", axis=1, tiled=True).astype(
            jnp.float32
        ),
        lax.all_gather(shares[1].astype(jnp.bfloat16), "rep", axis=1, tiled=True).astype(
            jnp.float32
        ),
        lax.all_gather(shares[2].astype(jnp.bfloat16), "rep", axis=0, tiled=True).astype(
            jnp.float32
        ),
        lax.all_gather(shares[3].astype(jnp.bfloat16), "rep", axis=0, tiled=True).astype(
            jnp.float32
        ),
    )
    learn_rate = base_rate / math.sqrt(
        tokens.shape[0] * lax.axis_size("rep") * lax.axis_size("fsdp")
    )
    attn_new, attn_momentum, attn_ema, attn_copy = advance(
        reduced[0], attn_weight, attn_moment, attn_average, learn_rate
    )
    mlp_new, mlp_momentum, mlp_ema, mlp_copy = advance(
        reduced[1], mlp_weight, mlp_moment, mlp_average, learn_rate
    )
    gain_new, gain_momentum, gain_ema, gain_copy = advance(
        reduced[2], gain_vector, gain_moment, gain_average, learn_rate
    )
    offset_new, offset_momentum, offset_ema, offset_copy = advance(
        reduced[3], offset_vector, offset_moment, offset_average, learn_rate
    )
    return (
        output.astype(jnp.bfloat16),
        input_grad,
        attn_new,
        attn_momentum,
        attn_ema,
        attn_copy,
        mlp_new,
        mlp_momentum,
        mlp_ema,
        mlp_copy,
        gain_new,
        gain_momentum,
        gain_ema,
        gain_copy,
        offset_new,
        offset_momentum,
        offset_ema,
        offset_copy,
    )


class Operand:
    def __init__(self, ref):
        self.ref = ref

    def __getitem__(self, index):
        return self.ref[index]


def call(kernel, outs, args, scratch=(), name=None, limit=8):
    def body(co_ref, *refs):
        operands = [Operand(ref) for ref in refs[: len(args) - 1]]
        kernel(co_ref, *operands, *refs[len(args) - 1 :])

    return pl.pallas_call(
        body,
        out_shape=[jax.ShapeDtypeStruct(shape, dtype) for shape, dtype in outs],
        in_specs=[pl.BlockSpec(memory_space=pltpu.SMEM)]
        + [pl.BlockSpec(memory_space=pltpu.VMEM)] * (len(args) - 1),
        out_specs=[pl.BlockSpec(memory_space=pltpu.VMEM)] * len(outs),
        scratch_shapes=list(scratch),
        compiler_params=pltpu.CompilerParams(vmem_limit_bytes=limit * 2**20),
        cost_estimate=pl.CostEstimate(flops=2**20, bytes_accessed=2**20, transcendentals=0),
        name=name,
    )(*args)


def assemble_kernel(ranges, co, *refs):
    count = len(refs) - len(ranges)
    for number in range(count):
        a, i = (number // 4, number % 2) if count == 8 else (number // 2, number % 2)
        b = (number // 2) % 2 if count == 8 else 0
        for k in range(4):
            row = lax.bitwise_xor(co[1], k) * 192
            row = row + lax.bitwise_xor(co[2], i) * 96 + lax.bitwise_xor(co[3], a) * 48
            rows = pl.ds(pl.multiple_of(row, 16), 48)
            for (start, size), out in zip(ranges, refs[count:]):
                out[rows, b * size : b * size + size] = refs[number][
                    k * 48 : k * 48 + 48, start : start + size
                ]


def assemble(co, pieces, *ranges):
    widths = [size * (2 if len(pieces) == 8 else 1) for start, size in ranges]
    return call(
        functools.partial(assemble_kernel, ranges),
        [((D, width), BF) for width in widths],
        [co, *pieces],
        name="assemble",
    )


def lanes(offset, size):
    return pl.ds(pl.multiple_of(offset, 128), size)


def nn(left, right):
    return lax.dot_general(left, right, (((1,), (0,)), ((), ())), preferred_element_type=jnp.float32)


def nt(left, right):
    return lax.dot_general(left, right, (((1,), (1,)), ((), ())), preferred_element_type=jnp.float32)


def whole(weight, start, size):
    return weight[:, start : start + size]


def row_norm(values):
    mean = jnp.mean(values, axis=-1, keepdims=True)
    centred = values - mean
    var = jnp.mean(centred * centred, axis=-1, keepdims=True)
    rstd = lax.rsqrt(var + norm_eps)
    return centred * rstd, rstd


def prep_kernel(co, attn, mlp, s0, s1, s2, s3, s4):
    r = co[0]
    for part in range(3):
        cols = lanes(part * D + 384 * r, 384)
        s0[:, part * 384 : part * 384 + 384] = attn[:, cols].astype(BF)
    s1[:, :384] = attn[:, lanes(3 * D + 384 * r, 384)].astype(BF)
    s1[:, 384:] = mlp[:, lanes(1536 * r, 768)].astype(BF)
    for b, out in ((0, s3), (1, s4)):
        half = lax.bitwise_xor(r, b)
        s2[:, b * 768 : b * 768 + 768] = mlp[:, lanes(1536 * half + 768, 768)].astype(BF)
        out[...] = mlp[:, lanes(FF + 1536 * half, 1536)].astype(BF)


def first_norm_kernel(co, tokens, info, vec, h1, h1t, cols):
    turned = jnp.transpose(info[...])
    cols[:, 0:8] = turned
    x0 = jnp.where(turned[:, 2:3] == 1.0, vec[8:9, :], tokens[...].astype(F32))
    xh, rstd = row_norm(x0)
    h = xh * vec[0:1, :] + vec[2:3, :]
    h1[...] = h.astype(BF)
    h1t[...] = h.T.astype(BF)


def allowed_pairs(info, cols):
    return (cols[:, 0:1] == info[0:1, :]) & (cols[:, 1:2] == 1.0)


def attention_kernel(co, h1, vec, info, cols, weight, qkv, att, lse):
    for b in range(2):
        half = lax.bitwise_xor(co[0], b)
        for part in range(3):
            out = nn(h1[...], whole(weight, b * 1152 + part * 384, 384))
            if part != 1:
                row = 3 if part == 0 else 4
                out = out + vec.ref[row : row + 1, lanes(384 * half, 384)]
            qkv[:, b * 1152 + part * 384 : b * 1152 + part * 384 + 384] = out.astype(BF)
    allowed = allowed_pairs(info, cols)
    low = lax.broadcasted_iota(jnp.int32, (256, 128), 1) < 64
    for pair in range(6):
        base = (pair // 3) * 1152 + (pair % 3) * 128
        q2 = qkv[:, base : base + 128]
        k2 = qkv[:, base + 384 : base + 512]
        v2 = qkv[:, base + 768 : base + 896]
        mixed = []
        for side in range(2):
            qm = jnp.where(low if side == 0 else ~low, q2, jnp.zeros_like(q2))
            s = jnp.where(allowed, nt(k2, qm) * 0.125, mask_fill)
            peak = jnp.max(s, axis=0, keepdims=True)
            e = jnp.exp(s - peak)
            total = jnp.sum(e, axis=0, keepdims=True)
            prob = (e * (1.0 / total)).astype(BF)
            lse[2 * pair + side : 2 * pair + side + 1, :] = peak + jnp.log(total)
            mixed.append(over_tokens(prob, v2))
        att[:, pair * 128 : pair * 128 + 128] = jnp.where(low, mixed[0], mixed[1]).astype(BF)


def second_norm_kernel(co, tokens, cols, vec, att, weight, y1, h2, h2t):
    x0 = jnp.where(cols[:, 2:3] == 1.0, vec[8:9, :], tokens[...].astype(F32))
    y = x0 + nt(att[...], whole(weight, 0, D)) + vec[5:6, :]
    y1[...] = y
    xh, rstd = row_norm(y)
    h = xh * vec[1:2, :] + vec[6:7, :]
    h2[...] = h.astype(BF)
    h2t[...] = h.T.astype(BF)


def hidden_kernel(co, h2, vec, dz, w0, w1, g0, g1, slope0, slope1, send, keep, dzt, scratch):
    dzt[...] = dz[...].astype(F32).T.astype(BF)
    for part, weight, g, slope in ((0, w0, g0, slope0), (1, w1, g1, slope1)):
        for b in range(2):
            half = lax.bitwise_xor(co[0], b)
            for sub in range(0, D, 384):
                at = slice(b * D + sub, b * D + sub + 384)
                u = nn(h2[...], weight[:, at])
                u = u + vec[pl.ds(9 + 2 * half + part, 1), sub : sub + 384]
                phi = 0.5 * (1.0 + lax.erf(u * math.sqrt(0.5)))
                act = (u * phi).astype(BF)
                g[:, at] = act
                slope[:, at] = phi + u * (
                    jnp.exp(-0.5 * u * u) * (1.0 / math.sqrt(2.0 * math.pi))
                )
                scratch[...] = nn(dzt[...], act)
                dst = lanes(half * D + sub, 384) if part == 0 else lanes((2 + b) * D + sub, 384)
                share_rows(co[3], scratch, send, keep, dst)


def hidden_grad_kernel(
    co, dz, slope0, slope1, w0, w1, left, du0, du1, db1, send, keep, scratch
):
    for part, slope, du in ((0, slope0, du0), (1, slope1, du1)):
        for b, weight in ((0, w0), (1, w1)):
            half = lax.bitwise_xor(co[0], b)
            for sub in range(0, D, 384):
                at = slice(b * D + sub, b * D + sub + 384)
                da = nn(dz[...], weight[:, part * D + sub : part * D + sub + 384])
                d = (da * slope[:, at]).astype(BF)
                du[:, at] = d
                db1[pl.ds(2 * half + part, 1), sub : sub + 384] = jnp.sum(
                    d.astype(F32), axis=0, keepdims=True
                )
                scratch[...] = nn(left[...], d)
                dst = lanes(half * D + sub, 384) if part == 0 else lanes((2 + b) * D + sub, 384)
                share_rows(co[3], scratch, send, keep, dst)


def output_kernel(co, y1, vec, g0, g1, w0, w1, act):
    acc = y1[...] + vec[7:8, :]
    for part, g in ((0, g0), (1, g1)):
        for b, weight in ((0, w0), (1, w1)):
            w = weight[:, part * D : part * D + D]
            acc = acc + nt(g[:, b * D : b * D + D], w)
    act[...] = acc.astype(BF)


def share_rows(c, scratch, send, keep, dst):
    for k in range(4):
        for i in range(2):
            row = k * 192 + i * 96
            theirs = scratch[pl.ds(pl.multiple_of(row + 48 * (1 - c), 16), 48), :]
            mine = scratch[pl.ds(pl.multiple_of(row + 48 * c, 16), 48), :]
            send[k, i, :, dst] = theirs.astype(BF)
            keep[k, i, :, dst] = mine


def attention_grad_kernel(co, h1t, dqkv, dpt, att, send, keep, scratch):
    moves = [(h1t, dqkv, b * 1152 + 384 + n * 384, b * D + n * 384) for b in (0, 1) for n in (0, 1)]
    for b in range(2):
        place = 384 * lax.bitwise_xor(co[0], b)
        moves.append((h1t, dqkv, b * 1152, 2 * D + place))
        moves.append((dpt, att, b * 384, 3 * D + place))
    for left, right, src, dst in moves:
        scratch[...] = nn(left[...], right[:, src : src + 384])
        share_rows(co[3], scratch, send, keep, lanes(dst, 384))


def second_back_kernel(co, dz, y1, vec, du0, du1, w0, w1, weight_o, dy1, datt, dpt, small):
    yh, rstd = row_norm(y1[...])
    dy = dz[...].astype(F32)
    dh = nt(du0[...], whole(w0, 0, 2 * D)) + nt(du1[...], whole(w1, 0, 2 * D))
    small[0:1, :] = jnp.sum(dh * yh, axis=0, keepdims=True)
    small[1:2, :] = jnp.sum(dh, axis=0, keepdims=True)
    small[3:4, :] = jnp.sum(dy, axis=0, keepdims=True)
    e = dh * vec[1:2, :]
    d = dy + rstd * (
        e - jnp.mean(e, axis=-1, keepdims=True) - yh * jnp.mean(e * yh, axis=-1, keepdims=True)
    )
    dy1[...] = d
    small[2:3, :] = jnp.sum(d, axis=0, keepdims=True)
    dpt[...] = d.T.astype(BF)
    datt[...] = nn(d.astype(BF), whole(weight_o, 0, D)).astype(BF)


def attention_back_kernel(co, info, cols, lse, qkv, datt, dqkv, small):
    allowed = allowed_pairs(info, cols)
    low = lax.broadcasted_iota(jnp.int32, (256, 128), 1) < 64
    for pair in range(6):
        half = lax.bitwise_xor(co[0], pair // 3)
        base = (pair // 3) * 1152 + (pair % 3) * 128
        q2 = qkv[:, base : base + 128]
        k2 = qkv[:, base + 384 : base + 512]
        v2 = qkv[:, base + 768 : base + 896]
        o2 = datt[:, pair * 128 : pair * 128 + 128]
        dqs, dks, dvs = [], [], []
        for side in range(2):
            mine = low if side == 0 else ~low
            qm = jnp.where(mine, q2, jnp.zeros_like(q2))
            om = jnp.where(mine, o2, jnp.zeros_like(o2))
            s = jnp.where(allowed, nt(k2, qm) * 0.125, mask_fill)
            prob = jnp.exp(s - lse[2 * pair + side : 2 * pair + side + 1, :])
            dprob = nt(v2, om)
            delta = jnp.sum(dprob * prob, axis=0, keepdims=True)
            ds = (prob * (dprob - delta)).astype(BF)
            dqs.append(over_tokens(ds, k2))
            dks.append(nn(ds, q2))
            dvs.append(nn(prob.astype(BF), o2))
        dq = (jnp.where(low, dqs[0], dqs[1]) * 0.125).astype(BF)
        dk = (jnp.where(low, dks[0], dks[1]) * 0.125).astype(BF)
        dv = jnp.where(low, dvs[0], dvs[1]).astype(BF)
        dqkv[:, base : base + 128] = dq
        dqkv[:, base + 384 : base + 512] = dk
        dqkv[:, base + 768 : base + 896] = dv
        place = lanes(384 * half + (pair % 3) * 128, 128)
        small[0:1, place] = jnp.sum(dq.astype(F32), axis=0, keepdims=True)
        small[1:2, place] = jnp.sum(dv.astype(F32), axis=0, keepdims=True)


def first_back_kernel(
    co, dqkv, tokens, cols, vec, dy1, db1, small2, small_a, weight, input_grad, total
):
    hidden = cols[:, 2:3] == 1.0
    x0 = jnp.where(hidden, vec[8:9, :], tokens[...].astype(F32))
    xh, rstd = row_norm(x0)
    dh = nt(dqkv[...], whole(weight, 0, 3 * D))
    e = dh * vec[0:1, :]
    dx = dy1[...] + rstd * (
        e - jnp.mean(e, axis=-1, keepdims=True) - xh * jnp.mean(e * xh, axis=-1, keepdims=True)
    )
    input_grad[...] = jnp.where(hidden, 0.0, dx).astype(BF)
    total[0:1, :] = jnp.sum(dh * xh, axis=0, keepdims=True)
    total[1:2, :] = small2[0:1, :]
    total[2:3, :] = jnp.sum(dh, axis=0, keepdims=True)
    total[3:5, :] = small_a[0:2, :]
    total[5:6, :] = small2[2:3, :]
    total[6:7, :] = small2[1:2, :]
    total[7:8, :] = small2[3:4, :]
    total[8:9, :] = jnp.sum(jnp.where(hidden, dx, 0.0), axis=0, keepdims=True)
    total[9:13, :] = db1[0:4, :]
    total[13:16, :] = jnp.zeros((3, D), F32)


def both(keep, got, *at):
    return keep[at] + got[at].astype(F32)


def split_first_kernel(co, keep, got, y_send, y_keep, x_send, x_keep):
    y = co[2]
    every = slice(None)
    for k in range(4):
        for out, i in ((y_send, 1 - y), (y_keep, y)):
            out[k] = both(keep, got, k, i, every, slice(0, 2 * D)).astype(out.dtype)
    x_keep[...] = both(keep, got, every, every, every, slice(2 * D, 3 * D))
    x_send[...] = both(keep, got, every, every, every, slice(3 * D, 4 * D)).astype(BF)


def split_second_kernel(co, x_keep, x_got, keep, got, y_send, y_keep, x_send, x_next, rest):
    y = co[2]
    every = slice(None)
    for k in range(4):
        for out, i in ((y_send, 1 - y), (y_keep, y)):
            out[k, :, :D] = both(x_keep, x_got, k, i).astype(out.dtype)
            out[k, :, D:] = both(keep, got, k, i, every, slice(0, D)).astype(out.dtype)
    rest[...] = both(keep, got, every, every, every, slice(D, 2 * D))
    x_next[...] = both(keep, got, every, every, every, slice(2 * D, 3 * D))
    x_send[...] = both(keep, got, every, every, every, slice(3 * D, 4 * D)).astype(BF)


def split_third_kernel(co, x_keep, x_got, rest, keep, got, y_send, y_keep, x_send, x_next, last):
    y = co[2]
    every = slice(None)
    for k in range(4):
        for out, i in ((y_send, 1 - y), (y_keep, y)):
            out[k, :, :D] = both(x_keep, x_got, k, i).astype(out.dtype)
            out[k, :, D:] = rest[k, i].astype(out.dtype)
    x_next[...] = both(keep, got, every, every, every, slice(0, D))
    x_send[...] = both(keep, got, every, every, every, slice(D, 2 * D)).astype(BF)
    last[...] = both(keep, got, every, every, every, slice(2 * D, 4 * D))


def split_fourth_kernel(co, x_keep, x_got, rest, y_send, y_keep):
    y = co[2]
    for k in range(4):
        for out, i in ((y_send, 1 - y), (y_keep, y)):
            out[k, :, :D] = both(x_keep, x_got, k, i).astype(out.dtype)
            out[k, :, D:] = rest[k, i].astype(out.dtype)


def split_z_kernel(co, keep, got, z1, z2, z3, z_keep):
    z = co[1]
    for k, out in ((1, z1), (2, z2), (3, z3)):
        out[...] = both(keep, got, lax.bitwise_xor(z, k)).astype(BF)
    z_keep[...] = both(keep, got, z)


def sum_z_kernel(co, keep, g1, g2, g3, out):
    out[...] = (
        keep[...] + g1[...].astype(F32) + g2[...].astype(F32) + g3[...].astype(F32)
    ).astype(BF)


def update_kernel(rate, moves, co, *refs):
    state, grads, new = refs[:3], refs[3:-4], refs[-4:]
    for numbers, src, size, b, col, stride in moves:
        grad = grads[numbers[0]][:, src : src + size].astype(F32)
        if len(numbers) == 2:
            grad = grad + grads[numbers[1]][:, src : src + size].astype(F32)
        place = col if b is None else col + stride * lax.bitwise_xor(co[0], b)
        at = lanes(place, size)
        w, m, a = (ref.ref[:, at] for ref in state)
        m_new = momentum_decay * m + grad
        w_new = w - rate * (grad + momentum_decay * m_new)
        new[0][:, at] = w_new
        new[1][:, at] = m_new
        new[2][:, at] = average_decay * a + (1.0 - average_decay) * w_new
        new[3][:, at] = w_new.astype(BF)


def hold(arrays):
    return lax.optimization_barrier(arrays)


def fast_device(
    tokens,
    cotangent,
    clip_index,
    key_valid,
    patch_masked,
    attn_weight,
    mlp_weight,
    gain_vector,
    offset_vector,
    attn_moment,
    mlp_moment,
    gain_moment,
    offset_moment,
    attn_average,
    mlp_average,
    gain_average,
    offset_average,
):
    r, f = lax.axis_index("rep"), lax.axis_index("fsdp")
    co = jnp.stack([r, f // 4, (f // 2) % 2, f % 2]).astype(jnp.int32)

    def swap(array, mask):
        return lax.ppermute(array, ("rep", "fsdp"), [(i, i ^ mask) for i in range(32)])

    CORE, Y, Z, X = 1, 2, 4, 16

    s0, s1, s2, s3, s4 = call(
        prep_kernel,
        [((48, 1152), BF)] * 2 + [((48, 1536), BF)] * 3,
        [co, attn_weight, mlp_weight],
        name="prep",
    )
    info = jnp.zeros((8, 256), F32).at[0:3].set(
        jnp.stack([clip_index, key_valid, patch_masked]).astype(F32)
    )
    flat = jnp.zeros((16 * D,), F32)
    flat = lax.dynamic_update_slice(flat, gain_vector.astype(BF).astype(F32), (96 * f,))
    flat = lax.dynamic_update_slice(flat, offset_vector.astype(BF).astype(F32), (2 * D + 528 * f,))
    vec = flat.reshape(16, D)

    def along_z(shard):
        return [swap(shard, Z * k) for k in (1, 2, 3)]

    def rows(shard, others):
        return jnp.concatenate([shard] + others, axis=0)

    def core_pair(pieces):
        return pieces + [swap(piece, CORE) for piece in pieces]

    z0 = along_z(s0)
    vec = vec + swap(vec, CORE)
    vec = vec + swap(vec, Y)
    stack0, s1, vec = hold((rows(s0, z0), s1, vec))
    across0 = swap(stack0, Y)
    far0 = swap(stack0, X)
    z1 = along_z(s1)
    vec = vec + swap(vec, Z)
    stack1, across0, far0, s2, vec = hold((rows(s1, z1), across0, far0, s2, vec))
    far_across0 = swap(across0, X)
    across1 = swap(stack1, Y)
    z2 = along_z(s2)
    vec = vec + swap(vec, 2 * Z)
    pieces0 = core_pair([stack0, across0, far0])
    stack2, stack1, across1, far_across0, vec, s3 = hold(
        (rows(s2, z2), stack1, across1, far_across0, vec, s3)
    )
    far1 = swap(stack1, X)
    across2 = swap(stack2, Y)
    z3 = along_z(s3)
    pieces0 = pieces0[:3] + [far_across0] + pieces0[3:] + [swap(far_across0, CORE)]
    pieces1 = core_pair([stack1, across1])
    h1, h1t, cols = call(
        first_norm_kernel,
        [((256, D), BF), ((D, 256), BF), ((256, 128), F32)],
        [co, tokens, info, vec],
        name="norm1",
    )
    stack3, far1, across1, across2, pieces0, h1, s4 = hold(
        (rows(s3, z3), far1, across1, across2, pieces0, h1, s4)
    )
    far_across1 = swap(across1, X)
    across3 = swap(stack3, Y)
    z4 = along_z(s4)
    pieces1 = [*pieces1[:2], far1, *pieces1[2:], swap(far1, CORE)]
    pieces2 = core_pair([stack2, across2])
    (w_qkv,) = assemble(co, pieces0, (0, 1152))
    qkv, att, lse = call(
        attention_kernel,
        [((256, 3 * D), BF), ((256, D), BF), ((16, 256), F32)],
        [co, h1, vec, info, cols, w_qkv],
        name="attention",
    )
    stack4, far_across1, across3, pieces1, pieces2, att = hold(
        (rows(s4, z4), far_across1, across3, pieces1, pieces2, att)
    )
    across4 = swap(stack4, Y)
    pieces1 = [*pieces1[:3], far_across1, *pieces1[3:], swap(far_across1, CORE)]
    pieces3 = core_pair([stack3, across3])
    (w_up1,) = assemble(co, pieces2, (0, 1536))
    w_out, w_up0 = assemble(co, pieces1, (0, 384), (384, 768))

    y1, h2, h2t = call(
        second_norm_kernel,
        [((256, D), F32), ((256, D), BF), ((D, 256), BF)],
        [co, tokens, cols, vec, att, w_out],
        name="norm2",
    )
    shares = [((4, 2, 48, 4 * D), BF), ((4, 2, 48, 4 * D), F32)]
    g0, g1, slope0, slope1, down_send, down_keep = call(
        hidden_kernel,
        [((256, 2 * D), BF)] * 2 + [((256, 2 * D), F32)] * 2 + shares,
        [co, h2, vec, cotangent, w_up0, w_up1],
        scratch=[pltpu.VMEM((D, 256), BF), pltpu.VMEM((D, 384), F32)],
        name="hidden",
    )
    pieces4 = core_pair([stack4, across4])

    down_got = swap(down_send, CORE)
    (w_down0,) = assemble(co, pieces3, (0, 1536))
    (w_down1,) = assemble(co, pieces4, (0, 1536))
    du0, du1, db1, up_send, up_keep = call(
        hidden_grad_kernel,
        [((256, 2 * D), BF), ((256, 2 * D), BF), ((8, D), F32)] + shares,
        [co, cotangent, slope0, slope1, w_down0, w_down1, h2t],
        scratch=[pltpu.VMEM((D, 384), F32)],
        name="hidden_grad",
    )
    down_got, up_send = hold((down_got, up_send))
    y_shares = [((4, 48, 2 * D), BF), ((4, 48, 2 * D), F32)]
    x_shares = [((4, 2, 48, D), BF), ((4, 2, 48, D), F32)]
    y_send0, y_keep0, x_send1, x_keep1 = call(
        split_first_kernel, y_shares + x_shares, [co, down_keep, down_got], name="split_first"
    )
    y_send0, x_send1, up_send, du0 = hold((y_send0, x_send1, up_send, du0))
    y_got0 = swap(y_send0, Y)
    x_got1 = swap(x_send1, X)
    up_got = swap(up_send, CORE)
    dy1, datt, dpt, small2 = call(
        second_back_kernel,
        [((256, D), F32), ((256, D), BF), ((D, 256), BF), ((8, D), F32)],
        [co, cotangent, y1, vec, du0, du1, w_up0, w_up1, w_out],
        name="norm2_back",
    )
    dqkv, small_a = call(
        attention_back_kernel,
        [((256, 3 * D), BF), ((8, D), F32)],
        [co, info, cols, lse, qkv, datt],
        name="attention_back",
    )
    attn_send, attn_keep = call(
        attention_grad_kernel,
        shares,
        [co, h1t, dqkv, dpt, att],
        scratch=[pltpu.VMEM((D, 384), F32)],
        name="attention_grad",
    )

    def split_z(keep, got):
        width = keep.shape[2]
        *sends, z_keep = call(
            split_z_kernel,
            [((48, width), BF)] * 3 + [((48, width), F32)],
            [co, keep, got],
            name="split_z",
        )
        return sends, z_keep

    def swap_z(sends):
        return [swap(send, Z * k) for send, k in zip(sends, (1, 2, 3))]

    def sum_z(z_keep, z_got):
        return call(sum_z_kernel, [(z_keep.shape, BF)], [co, z_keep, *z_got], name="sum_z")[0]

    y_got0, x_got1, up_got, attn_send = hold((y_got0, x_got1, up_got, attn_send))
    z_send0, z_keep0 = split_z(y_keep0, y_got0)
    y_send1, y_keep1, x_send2, x_keep2, rest2 = call(
        split_second_kernel,
        y_shares + x_shares + x_shares[1:],
        [co, x_keep1, x_got1, up_keep, up_got],
        name="split_second",
    )
    z_send0, y_send1, x_send2, attn_send, dqkv = hold((z_send0, y_send1, x_send2, attn_send, dqkv))
    x_got2 = swap(x_send2, X)
    y_got1 = swap(y_send1, Y)
    z_got0 = swap_z(z_send0)
    attn_got = swap(attn_send, CORE)
    input_grad, total = call(
        first_back_kernel,
        [((256, D), BF), ((16, D), F32)],
        [co, dqkv, tokens, cols, vec, dy1, db1, small2, small_a, w_qkv],
        name="norm1_back",
    )
    z_got0, y_got1, x_got2, attn_got, total = hold((z_got0, y_got1, x_got2, attn_got, total))
    z_send1, z_keep1 = split_z(y_keep1, y_got1)
    y_send2, y_keep2, x_send3, x_keep3, rest3 = call(
        split_third_kernel,
        y_shares + x_shares + [((4, 2, 48, 2 * D), F32)],
        [co, x_keep2, x_got2, rest2, attn_keep, attn_got],
        name="split_third",
    )
    mine0 = sum_z(z_keep0, z_got0)
    z_send1, y_send2, x_send3, mine0, total, y1 = hold(
        (z_send1, y_send2, x_send3, mine0, total, y1)
    )
    x_got3 = swap(x_send3, X)
    y_got2 = swap(y_send2, Y)
    z_got1 = swap_z(z_send1)
    got0 = swap(mine0, X)
    total = total + swap(total, CORE)
    total = total + swap(total, Y)
    (activations,) = call(
        output_kernel, [((256, D), BF)], [co, y1, vec, g0, g1, w_down0, w_down1], name="output"
    )
    z_got1, y_got2, x_got3, got0, total, activations = hold(
        (z_got1, y_got2, x_got3, got0, total, activations)
    )
    z_send2, z_keep2 = split_z(y_keep2, y_got2)
    y_send3, y_keep3 = call(
        split_fourth_kernel,
        [((4, 48, 3 * D), BF), ((4, 48, 3 * D), F32)],
        [co, x_keep3, x_got3, rest3],
        name="split_fourth",
    )
    mine1 = sum_z(z_keep1, z_got1)
    z_send2, y_send3, mine1, total = hold((z_send2, y_send3, mine1, total))
    y_got3 = swap(y_send3, Y)
    z_got2 = swap_z(z_send2)
    got1 = swap(mine1, X)
    total = total + swap(total, X)
    z_got2, y_got3, got1, total = hold((z_got2, y_got3, got1, total))
    z_send3, z_keep3 = split_z(y_keep3, y_got3)
    mine2 = sum_z(z_keep2, z_got2)
    z_send3, mine2, total = hold((z_send3, mine2, total))
    z_got3 = swap_z(z_send3)
    got2 = swap(mine2, X)
    total = total + swap(total, Z)
    z_got3, got2, total = hold((z_got3, got2, total))
    mine3 = sum_z(z_keep3, z_got3)
    got3 = swap(mine3, X)
    total = total + swap(total, 2 * Z)
    flat = total.reshape(-1)
    gain_g = lax.dynamic_slice(flat, (96 * f,), (96,))
    offset_g = lax.dynamic_slice(flat, (2 * D + 528 * f,), (528,))

    rate = base_rate / math.sqrt(tokens.shape[0] * 32)

    def update(moves, state, grads, width, name):
        return call(
            functools.partial(update_kernel, rate, moves),
            [((48, width), F32)] * 3 + [((48, width), BF)],
            [co, *state, *grads],
            name=name,
        )

    mlp_moves = [((0, 1), h * D, D, None, FF + h * 2 * D, 0) for h in range(2)]
    mlp_moves += [((2 + b,), 0, D, b, FF + D, 2 * D) for b in range(2)]
    mlp_moves += [((2, 3), D, D, None, 0, 0), ((4, 5), D, D, None, 2 * D, 0)]
    mlp_moves += [((4 + b,), 0, D, b, D, 2 * D) for b in range(2)]
    mlp = update(
        mlp_moves,
        [mlp_weight, mlp_moment, mlp_average],
        [mine0, got0, mine1, got1, mine2, got2],
        2 * FF,
        "update_mlp",
    )
    attn_moves = [((0, 1), D, D, None, 0, 0)]
    attn_moves += [((b,), 0, 384, b, D, 384) for b in range(2)]
    attn_moves += [((b,), 384, 384, b, 2 * D, 384) for b in range(2)]
    attn_moves += [((0, 1), 2 * D, D, None, 3 * D, 0)]
    attn = update(
        attn_moves,
        [attn_weight, attn_moment, attn_average],
        [mine3, got3],
        4 * D,
        "update_attn",
    )
    gains = advance(gain_g, gain_vector, gain_moment, gain_average, rate)
    offsets = advance(offset_g, offset_vector, offset_moment, offset_average, rate)
    return (activations, input_grad, *attn, *mlp, *gains, *offsets)


def solution(mesh):
    placed = (
        P(("rep", "fsdp"), None),
        P(("rep", "fsdp"), None),
        P(("rep", "fsdp")),
        P(("rep", "fsdp")),
        P(("rep", "fsdp")),
        P("fsdp", None),
        P("fsdp", None),
        P("fsdp"),
        P("fsdp"),
        P("fsdp", None),
        P("fsdp", None),
        P("fsdp"),
        P("fsdp"),
        P("fsdp", None),
        P("fsdp", None),
        P("fsdp"),
        P("fsdp"),
    )
    small = mesh.shape["rep"] == 2 and mesh.shape["fsdp"] == 16
    return jax.shard_map(
        fast_device if small else per_device,
        mesh=mesh,
        in_specs=placed,
        out_specs=(
            P(("rep", "fsdp"), None),
            P(("rep", "fsdp"), None),
            P("fsdp", None),
            P("fsdp", None),
            P("fsdp", None),
            P("fsdp", None),
            P("fsdp", None),
            P("fsdp", None),
            P("fsdp", None),
            P("fsdp", None),
            P("fsdp"),
            P("fsdp"),
            P("fsdp"),
            P("fsdp"),
            P("fsdp"),
            P("fsdp"),
            P("fsdp"),
            P("fsdp"),
        ),
        check_vma=False,
    )
```

```python
import functools
import math

import jax
import jax.numpy as jnp
from jax import lax
from jax.experimental import pallas as pl
from jax.experimental.pallas import tpu as pltpu
from jax.sharding import PartitionSpec as P

D = 768
HEADS = 12
HEAD_DIM = 64
FF = 3072
BF = jnp.bfloat16
F32 = jnp.float32


momentum_decay = 0.9
average_decay = 0.8
base_rate = 0.02
norm_eps = 1e-06
mask_fill = -1e30


def normalize(inputs):
    mean_val = jnp.mean(inputs, axis=-1, keepdims=True)
    centred = inputs - mean_val
    variance = jnp.mean(centred * centred, axis=-1, keepdims=True)
    return centred * lax.rsqrt(variance + norm_eps)


def norm_affine(inputs, gain_part, shift_part):
    return normalize(inputs) * gain_part + shift_part


def gelu_exact(inputs):
    return jax.nn.gelu(inputs, approximate=False)


def over_tokens(left_mat, right_mat):
    return lax.dot_general(
        left_mat, right_mat, (((0,), (0,)), ((), ())), preferred_element_type=jnp.float32
    )


def against_rows(left_mat, right_mat):
    return lax.dot_general(
        left_mat, right_mat, (((1,), (1,)), ((), ())), preferred_element_type=jnp.float32
    )


def block_mask(clip_ids, key_ok):
    return (clip_ids[:, None] == clip_ids[None, :]) & (key_ok[None, :] == 1)


def forward(inputs, params, clip_ids, key_ok, masked):
    attn_full = params[0]
    mlp_full = params[1]
    gain_f = params[2].astype(jnp.float32)
    shift_f = params[3].astype(jnp.float32)
    tok_rows = inputs.shape[0]
    score_scale = HEAD_DIM ** (-0.5)
    is_masked = masked[:, None] == 1
    embedded = jnp.where(is_masked, shift_f[6 * D : 7 * D][None, :], inputs)
    normed_one = norm_affine(embedded, gain_f[:D], shift_f[:D]).astype(jnp.bfloat16)
    qkv_bias = jnp.concatenate(
        [shift_f[D : 2 * D], jnp.zeros((D,), jnp.float32), shift_f[2 * D : 3 * D]]
    )
    projected = (
        jnp.dot(normed_one, attn_full[:, : 3 * D], preferred_element_type=jnp.float32) + qkv_bias
    )
    projected = projected.astype(jnp.bfloat16)
    queries = projected[:, :D].reshape(tok_rows, HEADS, HEAD_DIM)
    key_heads = projected[:, D : 2 * D].reshape(tok_rows, HEADS, HEAD_DIM)
    value_heads = projected[:, 2 * D :].reshape(tok_rows, HEADS, HEAD_DIM)
    allowed = block_mask(clip_ids, key_ok)
    scores = (
        jnp.einsum("qhd,khd->hqk", queries, key_heads, preferred_element_type=jnp.float32)
        * score_scale
    )
    scores = jnp.where(allowed[None], scores, mask_fill)
    row_peak = jnp.max(scores, axis=-1, keepdims=True)
    exponent = jnp.exp(scores - row_peak)
    summed = jnp.sum(exponent, axis=-1, keepdims=True)
    attn_prob = (exponent / summed).astype(jnp.bfloat16)
    mixed_parts = jnp.einsum(
        "hqk,khd->qhd", attn_prob, value_heads, preferred_element_type=jnp.float32
    )
    lse_parts = [row_peak + jnp.log(summed)]
    mixed_out = mixed_parts.reshape(tok_rows, D).astype(jnp.bfloat16)
    after_attn = embedded + against_rows(mixed_out, attn_full[:, 3 * D :]) + shift_f[3 * D : 4 * D]
    normed_two = norm_affine(after_attn, gain_f[D:], shift_f[4 * D : 5 * D]).astype(jnp.bfloat16)
    hidden_pre = (
        jnp.dot(normed_two, mlp_full[:, :FF], preferred_element_type=jnp.float32) + shift_f[7 * D :]
    )
    hidden_act = gelu_exact(hidden_pre).astype(jnp.bfloat16)
    output = after_attn + against_rows(hidden_act, mlp_full[:, FF:]) + shift_f[5 * D : 6 * D]
    kept_values = (
        embedded,
        normed_one,
        queries,
        key_heads,
        value_heads,
        lse_parts,
        mixed_out,
        after_attn,
        normed_two,
        hidden_pre,
        hidden_act,
        gain_f,
        shift_f,
    )
    return (output, kept_values)


def backward(cotangent, params, kept_values, clip_ids, key_ok, masked):
    attn_full = params[0]
    mlp_full = params[1]
    (
        embedded,
        normed_one,
        queries,
        key_heads,
        value_heads,
        lse_parts,
        mixed_out,
        after_attn,
        normed_two,
        hidden_pre,
        hidden_act,
        gain_f,
        shift_f,
    ) = kept_values
    tok_rows = cotangent.shape[0]
    score_scale = HEAD_DIM ** (-0.5)
    d_out = cotangent.astype(jnp.float32)
    d_bias_two = jnp.sum(d_out, axis=0)
    d_down = over_tokens(cotangent, hidden_act)
    d_act = jnp.dot(cotangent, mlp_full[:, FF:], preferred_element_type=jnp.float32)
    gelu_value, gelu_pull = jax.vjp(gelu_exact, hidden_pre)
    d_pre_low = gelu_pull(d_act)[0].astype(jnp.bfloat16)
    d_bias_one = jnp.sum(d_pre_low.astype(jnp.float32), axis=0)
    d_up = over_tokens(normed_two, d_pre_low)
    mlp_grad = jnp.concatenate([d_up, d_down], axis=1)
    d_normed_two = against_rows(d_pre_low, mlp_full[:, :FF])
    norm_value, norm_pull = jax.vjp(norm_affine, after_attn, gain_f[D:], shift_f[4 * D : 5 * D])
    d_after_norm, d_gain_two, d_shift_two = norm_pull(d_normed_two)
    d_after = d_out + d_after_norm
    d_after_low = d_after.astype(jnp.bfloat16)
    d_bias_out = jnp.sum(d_after, axis=0)
    d_outproj = over_tokens(d_after_low, mixed_out)
    d_mixed = jnp.dot(d_after_low, attn_full[:, 3 * D :], preferred_element_type=jnp.float32)
    d_mixed_low = d_mixed.astype(jnp.bfloat16).reshape(tok_rows, HEADS, HEAD_DIM)
    block_rows = min(512, tok_rows)
    d_query_parts = []
    d_keys = jnp.zeros((tok_rows, HEADS, HEAD_DIM), jnp.float32)
    d_values = jnp.zeros((tok_rows, HEADS, HEAD_DIM), jnp.float32)
    for block_number, offset in enumerate(range(0, tok_rows, block_rows)):
        allowed = block_mask(clip_ids, key_ok)
        scores = (
            jnp.einsum("qhd,khd->hqk", queries, key_heads, preferred_element_type=jnp.float32)
            * score_scale
        )
        scores = jnp.where(allowed[None], scores, mask_fill)
        attn_prob = jnp.exp(scores - lse_parts[block_number])
        prob_low = attn_prob.astype(jnp.bfloat16)
        d_prob = jnp.einsum(
            "qhd,khd->hqk", d_mixed_low, value_heads, preferred_element_type=jnp.float32
        )
        row_delta = jnp.sum(d_prob * attn_prob, axis=-1, keepdims=True)
        d_scores = (attn_prob * (d_prob - row_delta)).astype(jnp.bfloat16)
        d_query_parts.append(
            jnp.einsum("hqk,khd->qhd", d_scores, key_heads, preferred_element_type=jnp.float32)
            * score_scale
        )
        d_keys = (
            jnp.einsum("hqk,qhd->khd", d_scores, queries, preferred_element_type=jnp.float32)
            * score_scale
        )
        d_values = jnp.einsum(
            "hqk,qhd->khd", prob_low, d_mixed_low, preferred_element_type=jnp.float32
        )
    d_queries = d_query_parts[0]
    d_proj_low = jnp.concatenate(
        [
            d_queries.reshape(tok_rows, D),
            d_keys.reshape(tok_rows, D),
            d_values.reshape(tok_rows, D),
        ],
        axis=1,
    ).astype(jnp.bfloat16)
    d_bias_q = jnp.sum(d_proj_low[:, :D].astype(jnp.float32), axis=0)
    d_bias_v = jnp.sum(d_proj_low[:, 2 * D :].astype(jnp.float32), axis=0)
    d_qkv = over_tokens(normed_one, d_proj_low)
    d_normed_one = against_rows(d_proj_low, attn_full[:, : 3 * D])
    first_value, first_pull = jax.vjp(norm_affine, embedded, gain_f[:D], shift_f[:D])
    d_embed_norm, d_gain_one, d_shift_one = first_pull(d_normed_one)
    d_embedded = d_after + d_embed_norm
    is_masked = masked[:, None] == 1
    d_mask_vec = jnp.sum(jnp.where(is_masked, d_embedded, 0.0), axis=0)
    input_grad = jnp.where(is_masked, 0.0, d_embedded).astype(jnp.bfloat16)
    attn_grad = jnp.concatenate([d_qkv, d_outproj], axis=1)
    gain_grad = jnp.concatenate([d_gain_one, d_gain_two])
    offset_grad = jnp.concatenate(
        [
            d_shift_one,
            d_bias_q,
            d_bias_v,
            d_bias_out,
            d_shift_two,
            d_bias_two,
            d_mask_vec,
            d_bias_one,
        ]
    )
    return (input_grad, (attn_grad, mlp_grad, gain_grad, offset_grad))


def advance(gradient, weight, moment, average, learn_rate):
    moment_new = momentum_decay * moment + gradient
    weight_new = weight - learn_rate * (gradient + momentum_decay * moment_new)
    average_new = average_decay * average + (1.0 - average_decay) * weight_new
    return (weight_new, moment_new, average_new, weight_new.astype(jnp.bfloat16))


def per_device(
    tokens,
    cotangent,
    clip_index,
    key_valid,
    patch_masked,
    attn_weight,
    mlp_weight,
    gain_vector,
    offset_vector,
    attn_moment,
    mlp_moment,
    gain_moment,
    offset_moment,
    attn_average,
    mlp_average,
    gain_average,
    offset_average,
):
    attn_shard = attn_weight.astype(jnp.bfloat16)
    mlp_shard = mlp_weight.astype(jnp.bfloat16)
    gain_shard = gain_vector.astype(jnp.bfloat16)
    offset_shard = offset_vector.astype(jnp.bfloat16)
    params = (
        lax.all_gather(attn_shard, "fsdp", axis=0, tiled=True),
        lax.all_gather(mlp_shard, "fsdp", axis=0, tiled=True),
        lax.all_gather(gain_shard, "fsdp", axis=0, tiled=True),
        lax.all_gather(offset_shard, "fsdp", axis=0, tiled=True),
    )
    inputs = tokens.astype(jnp.float32)
    output, first_kept = forward(inputs, params, clip_index, key_valid, patch_masked)
    again = (
        lax.all_gather(attn_shard, "fsdp", axis=0, tiled=True),
        lax.all_gather(mlp_shard, "fsdp", axis=0, tiled=True),
        lax.all_gather(gain_shard, "fsdp", axis=0, tiled=True),
        lax.all_gather(offset_shard, "fsdp", axis=0, tiled=True),
    )
    output_again, kept_values = forward(inputs, again, clip_index, key_valid, patch_masked)
    input_grad, gradients = backward(
        cotangent, again, kept_values, clip_index, key_valid, patch_masked
    )
    owned = (
        lax.psum_scatter(gradients[0], "fsdp", scatter_dimension=0, tiled=True),
        lax.psum_scatter(gradients[1], "fsdp", scatter_dimension=0, tiled=True),
        lax.psum_scatter(gradients[2], "fsdp", scatter_dimension=0, tiled=True),
        lax.psum_scatter(gradients[3], "fsdp", scatter_dimension=0, tiled=True),
    )
    shares = (
        lax.psum_scatter(
            owned[0].astype(jnp.bfloat16), "rep", scatter_dimension=1, tiled=True
        ).astype(jnp.float32),
        lax.psum_scatter(
            owned[1].astype(jnp.bfloat16), "rep", scatter_dimension=1, tiled=True
        ).astype(jnp.float32),
        lax.psum_scatter(
            owned[2].astype(jnp.bfloat16), "rep", scatter_dimension=0, tiled=True
        ).astype(jnp.float32),
        lax.psum_scatter(
            owned[3].astype(jnp.bfloat16), "rep", scatter_dimension=0, tiled=True
        ).astype(jnp.float32),
    )
    reduced = (
        lax.all_gather(shares[0].astype(jnp.bfloat16), "rep", axis=1, tiled=True).astype(
            jnp.float32
        ),
        lax.all_gather(shares[1].astype(jnp.bfloat16), "rep", axis=1, tiled=True).astype(
            jnp.float32
        ),
        lax.all_gather(shares[2].astype(jnp.bfloat16), "rep", axis=0, tiled=True).astype(
            jnp.float32
        ),
        lax.all_gather(shares[3].astype(jnp.bfloat16), "rep", axis=0, tiled=True).astype(
            jnp.float32
        ),
    )
    learn_rate = base_rate / math.sqrt(
        tokens.shape[0] * lax.axis_size("rep") * lax.axis_size("fsdp")
    )
    attn_new, attn_momentum, attn_ema, attn_copy = advance(
        reduced[0], attn_weight, attn_moment, attn_average, learn_rate
    )
    mlp_new, mlp_momentum, mlp_ema, mlp_copy = advance(
        reduced[1], mlp_weight, mlp_moment, mlp_average, learn_rate
    )
    gain_new, gain_momentum, gain_ema, gain_copy = advance(
        reduced[2], gain_vector, gain_moment, gain_average, learn_rate
    )
    offset_new, offset_momentum, offset_ema, offset_copy = advance(
        reduced[3], offset_vector, offset_moment, offset_average, learn_rate
    )
    return (
        output.astype(jnp.bfloat16),
        input_grad,
        attn_new,
        attn_momentum,
        attn_ema,
        attn_copy,
        mlp_new,
        mlp_momentum,
        mlp_ema,
        mlp_copy,
        gain_new,
        gain_momentum,
        gain_ema,
        gain_copy,
        offset_new,
        offset_momentum,
        offset_ema,
        offset_copy,
    )


class Operand:
    def __init__(self, ref):
        self.ref = ref

    def __getitem__(self, index):
        return self.ref[index]


def call(kernel, outs, args, scratch=(), name=None, limit=8):
    def body(co_ref, *refs):
        operands = [Operand(ref) for ref in refs[: len(args) - 1]]
        kernel(co_ref, *operands, *refs[len(args) - 1 :])

    return pl.pallas_call(
        body,
        out_shape=[jax.ShapeDtypeStruct(shape, dtype) for shape, dtype in outs],
        in_specs=[pl.BlockSpec(memory_space=pltpu.SMEM)]
        + [pl.BlockSpec(memory_space=pltpu.VMEM)] * (len(args) - 1),
        out_specs=[pl.BlockSpec(memory_space=pltpu.VMEM)] * len(outs),
        scratch_shapes=list(scratch),
        compiler_params=pltpu.CompilerParams(vmem_limit_bytes=limit * 2**20),
        cost_estimate=pl.CostEstimate(flops=2**20, bytes_accessed=2**20, transcendentals=0),
        name=name,
    )(*args)


def assemble_kernel(ranges, co, *refs):
    count = len(refs) - len(ranges)
    for number in range(count):
        a, i = (number // 4, number % 2) if count == 8 else (number // 2, number % 2)
        b = (number // 2) % 2 if count == 8 else 0
        for k in range(4):
            row = k * 192 + lax.bitwise_xor(co[2], i) * 96 + lax.bitwise_xor(co[3], a) * 48
            rows = pl.ds(pl.multiple_of(row, 16), 48)
            for (start, size), out in zip(ranges, refs[count:]):
                out[rows, b * size : b * size + size] = refs[number][
                    k * 48 : k * 48 + 48, start : start + size
                ]


def assemble(co, pieces, *ranges):
    widths = [size * (2 if len(pieces) == 8 else 1) for start, size in ranges]
    return call(
        functools.partial(assemble_kernel, ranges),
        [((D, width), BF) for width in widths],
        [co, *pieces],
        name="assemble",
    )


def lanes(offset, size):
    return pl.ds(pl.multiple_of(offset, 128), size)


def nn(left, right):
    return lax.dot_general(left, right, (((1,), (0,)), ((), ())), preferred_element_type=jnp.float32)


def nt(left, right):
    return lax.dot_general(left, right, (((1,), (1,)), ((), ())), preferred_element_type=jnp.float32)


def whole(weight, start, size):
    return weight[:, start : start + size]


def row_norm(values):
    mean = jnp.mean(values, axis=-1, keepdims=True)
    centred = values - mean
    var = jnp.mean(centred * centred, axis=-1, keepdims=True)
    rstd = lax.rsqrt(var + norm_eps)
    return centred * rstd, rstd


def prep_kernel(co, attn, mlp, s0, s1, s2):
    r = co[0]
    for part in range(3):
        cols = lanes(part * D + 384 * r, 384)
        s0[:, part * 384 : part * 384 + 384] = attn[:, cols].astype(BF)
    s0[:, 1152:1536] = attn[:, lanes(3 * D + 384 * r, 384)].astype(BF)
    s0[:, 1536:] = mlp[:, lanes(1536 * r, 768)].astype(BF)
    for b in range(2):
        half = lax.bitwise_xor(r, b)
        s1[:, b * D : b * D + D] = mlp[:, lanes(1536 * half + D, D)].astype(BF)
    s1[:, 2 * D :] = mlp[:, lanes(FF + 1536 * r, D)].astype(BF)
    s2[:, :D] = mlp[:, lanes(FF + 1536 * r + D, D)].astype(BF)
    s2[:, D:] = mlp[:, lanes(FF + 1536 * (1 - r), 2 * D)].astype(BF)


def first_norm_kernel(co, tokens, info, vec, h1, h1t, cols):
    turned = jnp.transpose(info[...])
    cols[:, 0:8] = turned
    x0 = jnp.where(turned[:, 2:3] == 1.0, vec[8:9, :], tokens[...].astype(F32))
    xh, rstd = row_norm(x0)
    h = xh * vec[0:1, :] + vec[2:3, :]
    h1[...] = h.astype(BF)
    h1t[...] = h.T.astype(BF)


def allowed_pairs(info, cols):
    return (cols[:, 0:1] == info[0:1, :]) & (cols[:, 1:2] == 1.0)


def attention_kernel(co, h1, vec, info, cols, weight, qkv, att, lse):
    for b in range(2):
        half = lax.bitwise_xor(co[0], b)
        for part in range(3):
            out = nn(h1[...], whole(weight, b * 1152 + part * 384, 384))
            if part != 1:
                row = 3 if part == 0 else 4
                out = out + vec.ref[row : row + 1, lanes(384 * half, 384)]
            qkv[:, b * 1152 + part * 384 : b * 1152 + part * 384 + 384] = out.astype(BF)
    allowed = allowed_pairs(info, cols)
    low = lax.broadcasted_iota(jnp.int32, (256, 128), 1) < 64
    for pair in range(6):
        base = (pair // 3) * 1152 + (pair % 3) * 128
        q2 = qkv[:, base : base + 128]
        k2 = qkv[:, base + 384 : base + 512]
        v2 = qkv[:, base + 768 : base + 896]
        mixed = []
        for side in range(2):
            qm = jnp.where(low if side == 0 else ~low, q2, jnp.zeros_like(q2))
            s = jnp.where(allowed, nt(k2, qm) * 0.125, mask_fill)
            peak = jnp.max(s, axis=0, keepdims=True)
            e = jnp.exp(s - peak)
            total = jnp.sum(e, axis=0, keepdims=True)
            prob = (e * (1.0 / total)).astype(BF)
            lse[2 * pair + side : 2 * pair + side + 1, :] = peak + jnp.log(total)
            mixed.append(over_tokens(prob, v2))
        att[:, pair * 128 : pair * 128 + 128] = jnp.where(low, mixed[0], mixed[1]).astype(BF)


def second_norm_kernel(co, tokens, cols, vec, att, weight, y1, h2, h2t):
    x0 = jnp.where(cols[:, 2:3] == 1.0, vec[8:9, :], tokens[...].astype(F32))
    y = x0 + nt(att[...], whole(weight, 0, D)) + vec[5:6, :]
    y1[...] = y
    xh, rstd = row_norm(y)
    h = xh * vec[1:2, :] + vec[6:7, :]
    h2[...] = h.astype(BF)
    h2t[...] = h.T.astype(BF)


def hidden_kernel(co, h2, vec, dz, w0, w1, g0, g1, slope0, slope1, send, keep, dzt, scratch):
    dzt[...] = dz[...].astype(F32).T.astype(BF)
    for part, weight, g, slope in ((0, w0, g0, slope0), (1, w1, g1, slope1)):
        for b in range(2):
            half = lax.bitwise_xor(co[0], b)
            for sub in range(0, D, 384):
                at = slice(b * D + sub, b * D + sub + 384)
                u = nn(h2[...], weight[:, at])
                u = u + vec[pl.ds(9 + 2 * half + part, 1), sub : sub + 384]
                phi = 0.5 * (1.0 + lax.erf(u * math.sqrt(0.5)))
                act = (u * phi).astype(BF)
                g[:, at] = act
                slope[:, at] = phi + u * (
                    jnp.exp(-0.5 * u * u) * (1.0 / math.sqrt(2.0 * math.pi))
                )
                scratch[...] = nn(dzt[...], act)
                dst = lanes(half * D + sub, 384) if part == 0 else lanes((2 + b) * D + sub, 384)
                share_rows(co[3], scratch, send, keep, dst)


def hidden_grad_kernel(
    co, dz, slope0, slope1, w00, w01, w1, left, du0, du1, db1, send, keep, scratch
):
    for part, slope, du in ((0, slope0, du0), (1, slope1, du1)):
        for b in range(2):
            weight, start = (w1, part * D) if b else ((w00, w01)[part], 0)
            half = lax.bitwise_xor(co[0], b)
            for sub in range(0, D, 384):
                at = slice(b * D + sub, b * D + sub + 384)
                da = nn(dz[...], weight[:, start + sub : start + sub + 384])
                d = (da * slope[:, at]).astype(BF)
                du[:, at] = d
                db1[pl.ds(2 * half + part, 1), sub : sub + 384] = jnp.sum(
                    d.astype(F32), axis=0, keepdims=True
                )
                scratch[...] = nn(left[...], d)
                dst = lanes(half * D + sub, 384) if part == 0 else lanes((2 + b) * D + sub, 384)
                share_rows(co[3], scratch, send, keep, dst)


def output_kernel(co, y1, vec, g0, g1, w00, w01, w1, act):
    acc = y1[...] + vec[7:8, :]
    for part, g in ((0, g0), (1, g1)):
        acc = acc + nt(g[:, :D], (w00, w01)[part][...])
        acc = acc + nt(g[:, D:], w1[:, part * D : part * D + D])
    act[...] = acc.astype(BF)


def share_rows(c, scratch, send, keep, dst):
    for k in range(4):
        for i in range(2):
            row = k * 192 + i * 96
            theirs = scratch[pl.ds(pl.multiple_of(row + 48 * (1 - c), 16), 48), :]
            mine = scratch[pl.ds(pl.multiple_of(row + 48 * c, 16), 48), :]
            send[k, i, :, dst] = theirs.astype(BF)
            keep[k, i, :, dst] = mine


def attention_grad_kernel(co, h1t, dqkv, dpt, att, send, keep, scratch):
    moves = [(h1t, dqkv, b * 1152 + 384 + n * 384, b * D + n * 384) for b in (0, 1) for n in (0, 1)]
    for b in range(2):
        place = 384 * lax.bitwise_xor(co[0], b)
        moves.append((h1t, dqkv, b * 1152, 2 * D + place))
        moves.append((dpt, att, b * 384, 3 * D + place))
    for left, right, src, dst in moves:
        scratch[...] = nn(left[...], right[:, src : src + 384])
        share_rows(co[3], scratch, send, keep, lanes(dst, 384))


def second_back_kernel(co, dz, y1, vec, du0, du1, w0, w1, weight_o, dy1, datt, dpt, small):
    yh, rstd = row_norm(y1[...])
    dy = dz[...].astype(F32)
    dh = nt(du0[...], whole(w0, 0, 2 * D)) + nt(du1[...], whole(w1, 0, 2 * D))
    small[0:1, :] = jnp.sum(dh * yh, axis=0, keepdims=True)
    small[1:2, :] = jnp.sum(dh, axis=0, keepdims=True)
    small[3:4, :] = jnp.sum(dy, axis=0, keepdims=True)
    e = dh * vec[1:2, :]
    d = dy + rstd * (
        e - jnp.mean(e, axis=-1, keepdims=True) - yh * jnp.mean(e * yh, axis=-1, keepdims=True)
    )
    dy1[...] = d
    small[2:3, :] = jnp.sum(d, axis=0, keepdims=True)
    dpt[...] = d.T.astype(BF)
    datt[...] = nn(d.astype(BF), whole(weight_o, 0, D)).astype(BF)


def attention_back_kernel(co, info, cols, lse, qkv, datt, dqkv, small):
    allowed = allowed_pairs(info, cols)
    low = lax.broadcasted_iota(jnp.int32, (256, 128), 1) < 64
    for pair in range(6):
        half = lax.bitwise_xor(co[0], pair // 3)
        base = (pair // 3) * 1152 + (pair % 3) * 128
        q2 = qkv[:, base : base + 128]
        k2 = qkv[:, base + 384 : base + 512]
        v2 = qkv[:, base + 768 : base + 896]
        o2 = datt[:, pair * 128 : pair * 128 + 128]
        dqs, dks, dvs = [], [], []
        for side in range(2):
            mine = low if side == 0 else ~low
            qm = jnp.where(mine, q2, jnp.zeros_like(q2))
            om = jnp.where(mine, o2, jnp.zeros_like(o2))
            s = jnp.where(allowed, nt(k2, qm) * 0.125, mask_fill)
            prob = jnp.exp(s - lse[2 * pair + side : 2 * pair + side + 1, :])
            dprob = nt(v2, om)
            delta = jnp.sum(dprob * prob, axis=0, keepdims=True)
            ds = (prob * (dprob - delta)).astype(BF)
            dqs.append(over_tokens(ds, k2))
            dks.append(nn(ds, q2))
            dvs.append(nn(prob.astype(BF), o2))
        dq = (jnp.where(low, dqs[0], dqs[1]) * 0.125).astype(BF)
        dk = (jnp.where(low, dks[0], dks[1]) * 0.125).astype(BF)
        dv = jnp.where(low, dvs[0], dvs[1]).astype(BF)
        dqkv[:, base : base + 128] = dq
        dqkv[:, base + 384 : base + 512] = dk
        dqkv[:, base + 768 : base + 896] = dv
        place = lanes(384 * half + (pair % 3) * 128, 128)
        small[0:1, place] = jnp.sum(dq.astype(F32), axis=0, keepdims=True)
        small[1:2, place] = jnp.sum(dv.astype(F32), axis=0, keepdims=True)


def first_back_kernel(
    co, dqkv, tokens, cols, vec, dy1, db1, small2, small_a, weight, input_grad, total
):
    hidden = cols[:, 2:3] == 1.0
    x0 = jnp.where(hidden, vec[8:9, :], tokens[...].astype(F32))
    xh, rstd = row_norm(x0)
    dh = nt(dqkv[...], whole(weight, 0, 3 * D))
    e = dh * vec[0:1, :]
    dx = dy1[...] + rstd * (
        e - jnp.mean(e, axis=-1, keepdims=True) - xh * jnp.mean(e * xh, axis=-1, keepdims=True)
    )
    input_grad[...] = jnp.where(hidden, 0.0, dx).astype(BF)
    total[0:1, :] = jnp.sum(dh * xh, axis=0, keepdims=True)
    total[1:2, :] = small2[0:1, :]
    total[2:3, :] = jnp.sum(dh, axis=0, keepdims=True)
    total[3:5, :] = small_a[0:2, :]
    total[5:6, :] = small2[2:3, :]
    total[6:7, :] = small2[1:2, :]
    total[7:8, :] = small2[3:4, :]
    total[8:9, :] = jnp.sum(jnp.where(hidden, dx, 0.0), axis=0, keepdims=True)
    total[9:13, :] = db1[0:4, :]
    total[13:16, :] = jnp.zeros((3, D), F32)


def both(keep, got, *at):
    return keep[at] + got[at].astype(F32)


def split_first_kernel(co, keep, got, y_send, y_keep, x_send, x_keep):
    y = co[2]
    every = slice(None)
    for k in range(4):
        for out, i in ((y_send, 1 - y), (y_keep, y)):
            out[k * 48 : k * 48 + 48, :] = both(keep, got, k, i, every, slice(0, 2 * D)).astype(
                out.dtype
            )
    x_keep[...] = both(keep, got, every, every, every, slice(2 * D, 3 * D))
    x_send[...] = both(keep, got, every, every, every, slice(3 * D, 4 * D)).astype(BF)


def split_second_kernel(co, x_keep, x_got, keep, got, y_send, y_keep, x_send, x_next):
    y = co[2]
    every = slice(None)
    for k in range(4):
        rows = slice(k * 48, k * 48 + 48)
        for out, i in ((y_send, 1 - y), (y_keep, y)):
            out[rows, :D] = both(x_keep, x_got, k, i).astype(out.dtype)
            out[rows, D:] = both(keep, got, k, i, every, slice(0, 2 * D)).astype(out.dtype)
    x_next[...] = both(keep, got, every, every, every, slice(2 * D, 3 * D))
    x_send[...] = both(keep, got, every, every, every, slice(3 * D, 4 * D)).astype(BF)


def split_third_kernel(co, x_keep, x_got, keep, got, y_send, y_keep, x_send, x_next, last):
    y = co[2]
    every = slice(None)
    for k in range(4):
        rows = slice(k * 48, k * 48 + 48)
        for out, i in ((y_send, 1 - y), (y_keep, y)):
            out[rows, :D] = both(x_keep, x_got, k, i).astype(out.dtype)
            out[rows, D:] = both(keep, got, k, i, every, slice(2 * D, 3 * D)).astype(out.dtype)
    x_next[...] = both(keep, got, every, every, every, slice(0, D))
    x_send[...] = both(keep, got, every, every, every, slice(D, 2 * D)).astype(BF)
    last[...] = both(keep, got, every, every, every, slice(3 * D, 4 * D))


def split_fourth_kernel(co, x_keep, x_got, last, vec, y_send, y_keep):
    y = co[2]
    for out, i in ((y_send, 1 - y), (y_keep, y)):
        for k in range(4):
            rows = slice(k * 48, k * 48 + 48)
            out[rows, :D] = both(x_keep, x_got, k, i).astype(out.dtype)
            out[rows, D:] = last[k, i].astype(out.dtype)
        out[192:208, :D] = vec[...].astype(out.dtype)
        out[192:208, D:] = jnp.zeros((16, D), out.dtype)


def split_near_kernel(co, keep, got, send, rest, *small):
    side = co[1] % 2
    for out, at in ((send, 1 - side), (rest, side)):
        for far in range(2):
            row = pl.multiple_of((2 * far + at) * 48, 16)
            out[far * 48 : far * 48 + 48, :] = both(keep, got, pl.ds(row, 48)).astype(out.dtype)
    if small:
        small[0][...] = both(keep, got, slice(192, 208), slice(0, D))


def split_far_kernel(co, keep, got, send, rest):
    side = co[1] // 2
    for out, at in ((send, 1 - side), (rest, side)):
        row = pl.multiple_of(at * 48, 16)
        out[...] = both(keep, got, pl.ds(row, 48)).astype(out.dtype)


def sum_far_kernel(co, keep, got, out):
    out[...] = (keep[...] + got[...].astype(F32)).astype(BF)


def update_kernel(rate, moves, co, *refs):
    state, grads, new = refs[:3], refs[3:-4], refs[-4:]
    for numbers, row, src, size, b, col, stride in moves:
        grad = 0.0
        for number in numbers:
            grad = grad + grads[number][row : row + 48, src : src + size].astype(F32)
        place = col if b is None else col + stride * lax.bitwise_xor(co[0], b)
        at = lanes(place, size)
        w, m, a = (ref[:, at] for ref in state)
        m_new = momentum_decay * m + grad
        w_new = w - rate * (grad + momentum_decay * m_new)
        new[0][:, at] = w_new
        new[1][:, at] = m_new
        new[2][:, at] = average_decay * a + (1.0 - average_decay) * w_new
        new[3][:, at] = w_new.astype(BF)


def hold(arrays):
    return lax.optimization_barrier(arrays)


def fast_device(
    tokens,
    cotangent,
    clip_index,
    key_valid,
    patch_masked,
    attn_weight,
    mlp_weight,
    gain_vector,
    offset_vector,
    attn_moment,
    mlp_moment,
    gain_moment,
    offset_moment,
    attn_average,
    mlp_average,
    gain_average,
    offset_average,
):
    r, f = lax.axis_index("rep"), lax.axis_index("fsdp")
    co = jnp.stack([r, f // 4, (f // 2) % 2, f % 2]).astype(jnp.int32)

    def swap(array, mask):
        return lax.ppermute(array, ("rep", "fsdp"), [(i, i ^ mask) for i in range(32)])

    CORE, Y, Z, X = 1, 2, 4, 16

    s0, s1, s2 = call(
        prep_kernel,
        [((48, 3 * D), BF)] * 3,
        [co, attn_weight, mlp_weight],
        name="prep",
    )
    info = jnp.zeros((8, 256), F32).at[0:3].set(
        jnp.stack([clip_index, key_valid, patch_masked]).astype(F32)
    )
    flat = jnp.zeros((16 * D,), F32)
    flat = lax.dynamic_update_slice(flat, gain_vector.astype(BF).astype(F32), (96 * f,))
    flat = lax.dynamic_update_slice(flat, offset_vector.astype(BF).astype(F32), (2 * D + 528 * f,))
    vec = flat.reshape(16, D)

    groups = [[4 * z + at for z in range(4)] for at in range(4)]

    def along_z(shard):
        return lax.all_gather(shard, "fsdp", axis=0, tiled=True, axis_index_groups=groups)

    def core_pair(pieces):
        return pieces + [swap(piece, CORE) for piece in pieces]

    vec = vec + swap(vec, CORE)
    s0, vec = hold((s0, vec))
    stack0 = along_z(s0)
    vec = vec + swap(vec, Y)
    stack0, s1, vec = hold((stack0, s1, vec))
    across0 = swap(stack0, Y)
    far0 = swap(stack0, X)
    near0 = [swap(stack0, CORE)]
    stack1 = along_z(s1)
    vec = vec + swap(vec, Z)
    stack1, across0, far0, near0, s2, vec = hold((stack1, across0, far0, near0, s2, vec))
    far_across0 = swap(across0, X)
    across1 = swap(stack1, Y)
    near0 += [swap(across0, CORE), swap(far0, CORE)]
    stack2 = along_z(s2)
    vec = vec + swap(vec, 2 * Z)
    stack2, across1, far_across0, near0, vec = hold((stack2, across1, far_across0, near0, vec))
    pieces0 = [stack0, across0, far0, far_across0, *near0, swap(far_across0, CORE)]
    across2 = swap(stack2, Y)
    pieces1 = core_pair([stack1, across1])
    h1, h1t, cols = call(
        first_norm_kernel,
        [((256, D), BF), ((D, 256), BF), ((256, 128), F32)],
        [co, tokens, info, vec],
        name="norm1",
    )
    (w_qkv,) = assemble(co, pieces0, (0, 1152))
    qkv, att, lse = call(
        attention_kernel,
        [((256, 3 * D), BF), ((256, D), BF), ((16, 256), F32)],
        [co, h1, vec, info, cols, w_qkv],
        name="attention",
    )
    w_out, w_up0 = assemble(co, pieces0, (1152, 384), (1536, 768))
    w_up1, w_down00 = assemble(co, pieces1, (0, 1536), (1536, 768))

    y1, h2, h2t = call(
        second_norm_kernel,
        [((256, D), F32), ((256, D), BF), ((D, 256), BF)],
        [co, tokens, cols, vec, att, w_out],
        name="norm2",
    )
    shares = [((4, 2, 48, 4 * D), BF), ((4, 2, 48, 4 * D), F32)]
    g0, g1, slope0, slope1, down_send, down_keep = call(
        hidden_kernel,
        [((256, 2 * D), BF)] * 2 + [((256, 2 * D), F32)] * 2 + shares,
        [co, h2, vec, cotangent, w_up0, w_up1],
        scratch=[pltpu.VMEM((D, 256), BF), pltpu.VMEM((D, 384), F32)],
        name="hidden",
    )

    across2, down_send = hold((across2, down_send))
    pieces2 = core_pair([stack2, across2])
    pieces2, down_send = hold((pieces2, down_send))
    down_got = swap(down_send, CORE)
    w_down01, w_down1 = assemble(co, pieces2, (0, 768), (768, 1536))
    du0, du1, db1, up_send, up_keep = call(
        hidden_grad_kernel,
        [((256, 2 * D), BF), ((256, 2 * D), BF), ((8, D), F32)] + shares,
        [co, cotangent, slope0, slope1, w_down00, w_down01, w_down1, h2t],
        scratch=[pltpu.VMEM((D, 384), F32)],
        name="hidden_grad",
    )
    down_got, up_send = hold((down_got, up_send))
    y_shares = [((192, 2 * D), BF), ((192, 2 * D), F32)]
    x_shares = [((4, 2, 48, D), BF), ((4, 2, 48, D), F32)]
    y_send0, y_keep0, x_send1, x_keep1 = call(
        split_first_kernel, y_shares + x_shares, [co, down_keep, down_got], name="split_first"
    )
    y_send0, x_send1, up_send, du0 = hold((y_send0, x_send1, up_send, du0))
    y_got0 = swap(y_send0, Y)
    x_got1 = swap(x_send1, X)
    up_got = swap(up_send, CORE)
    dy1, datt, dpt, small2 = call(
        second_back_kernel,
        [((256, D), F32), ((256, D), BF), ((D, 256), BF), ((8, D), F32)],
        [co, cotangent, y1, vec, du0, du1, w_up0, w_up1, w_out],
        name="norm2_back",
    )
    dqkv, small_a = call(
        attention_back_kernel,
        [((256, 3 * D), BF), ((8, D), F32)],
        [co, info, cols, lse, qkv, datt],
        name="attention_back",
    )
    attn_send, attn_keep = call(
        attention_grad_kernel,
        shares,
        [co, h1t, dqkv, dpt, att],
        scratch=[pltpu.VMEM((D, 384), F32)],
        name="attention_grad",
    )

    def split_near(keep, got, small=()):
        width = keep.shape[1]
        return call(
            split_near_kernel,
            [((96, width), BF), ((96, width), F32), *small],
            [co, keep, got],
            name="split_near",
        )

    def split_far(keep, got):
        width = keep.shape[1]
        return call(
            split_far_kernel,
            [((48, width), BF), ((48, width), F32)],
            [co, keep, got],
            name="split_far",
        )

    def sum_far(keep, got):
        return call(sum_far_kernel, [(keep.shape, BF)], [co, keep, got], name="sum_far")[0]

    y_got0, x_got1, up_got, attn_send = hold((y_got0, x_got1, up_got, attn_send))
    y_send1, y_keep1, x_send2, x_keep2 = call(
        split_second_kernel,
        [((192, 3 * D), BF), ((192, 3 * D), F32)] + x_shares,
        [co, x_keep1, x_got1, up_keep, up_got],
        name="split_second",
    )
    near_send0, near_keep0 = split_near(y_keep0, y_got0)
    near_send0, y_send1, x_send2, attn_send, dqkv = hold(
        (near_send0, y_send1, x_send2, attn_send, dqkv)
    )
    y_got1 = swap(y_send1, Y)
    x_got2 = swap(x_send2, X)
    near_got0 = swap(near_send0, Z)
    attn_got = swap(attn_send, CORE)
    input_grad, total = call(
        first_back_kernel,
        [((256, D), BF), ((16, D), F32)],
        [co, dqkv, tokens, cols, vec, dy1, db1, small2, small_a, w_qkv],
        name="norm1_back",
    )
    near_got0, y_got1, x_got2, attn_got, total = hold(
        (near_got0, y_got1, x_got2, attn_got, total)
    )
    y_send2, y_keep2, x_send3, x_keep3, last = call(
        split_third_kernel,
        y_shares + x_shares + x_shares[1:],
        [co, x_keep2, x_got2, attn_keep, attn_got],
        name="split_third",
    )
    near_send1, near_keep1 = split_near(y_keep1, y_got1)
    far_send0, far_keep0 = split_far(near_keep0, near_got0)
    far_send0, near_send1, y_send2, x_send3, total, y1 = hold(
        (far_send0, near_send1, y_send2, x_send3, total, y1)
    )
    x_got3 = swap(x_send3, X)
    y_got2 = swap(y_send2, Y)
    near_got1 = swap(near_send1, Z)
    far_got0 = swap(far_send0, 2 * Z)
    total = total + swap(total, CORE)
    (activations,) = call(
        output_kernel,
        [((256, D), BF)],
        [co, y1, vec, g0, g1, w_down00, w_down01, w_down1],
        name="output",
    )
    far_got0, near_got1, y_got2, x_got3, total, activations = hold(
        (far_got0, near_got1, y_got2, x_got3, total, activations)
    )
    y_send3, y_keep3 = call(
        split_fourth_kernel,
        [((208, 2 * D), BF), ((208, 2 * D), F32)],
        [co, x_keep3, x_got3, last, total],
        name="split_fourth",
    )
    near_send2, near_keep2 = split_near(y_keep2, y_got2)
    far_send1, far_keep1 = split_far(near_keep1, near_got1)
    mine0 = sum_far(far_keep0, far_got0)
    mine0, far_send1, near_send2, y_send3 = hold((mine0, far_send1, near_send2, y_send3))
    y_got3 = swap(y_send3, Y)
    near_got2 = swap(near_send2, Z)
    far_got1 = swap(far_send1, 2 * Z)
    got0 = swap(mine0, X)
    got0, far_got1, near_got2, y_got3 = hold((got0, far_got1, near_got2, y_got3))
    near_send3, near_keep3, total = split_near(y_keep3, y_got3, [((16, D), F32)])
    far_send2, far_keep2 = split_far(near_keep2, near_got2)
    mine1 = sum_far(far_keep1, far_got1)
    mine1, far_send2, near_send3, total = hold((mine1, far_send2, near_send3, total))
    near_got3 = swap(near_send3, Z)
    far_got2 = swap(far_send2, 2 * Z)
    got1 = swap(mine1, X)
    total = total + swap(total, Z)
    got1, far_got2, near_got3, total = hold((got1, far_got2, near_got3, total))
    far_send3, far_keep3 = split_far(near_keep3, near_got3)
    mine2 = sum_far(far_keep2, far_got2)
    mine2, far_send3, total = hold((mine2, far_send3, total))
    far_got3 = swap(far_send3, 2 * Z)
    got2 = swap(mine2, X)
    total = total + swap(total, 2 * Z)
    got2, far_got3, total = hold((got2, far_got3, total))
    mine3 = sum_far(far_keep3, far_got3)
    got3 = swap(mine3, X)
    total = total + swap(total, X)
    flat = total.reshape(-1)
    gain_g = lax.dynamic_slice(flat, (96 * f,), (96,))
    offset_g = lax.dynamic_slice(flat, (2 * D + 528 * f,), (528,))

    rate = base_rate / math.sqrt(tokens.shape[0] * 32)

    def update(moves, state, grads, width, name):
        return call(
            functools.partial(update_kernel, rate, moves),
            [((48, width), F32)] * 3 + [((48, width), BF)],
            [co, *state, *grads],
            name=name,
        )

    mlp_moves = [((0, 1), 0, h * D, D, None, FF + h * 2 * D, 0) for h in range(2)]
    mlp_moves += [((2 + b,), 0, 0, D, b, FF + D, 2 * D) for b in range(2)]
    mlp_moves += [((2, 3), 0, D + h * D, D, None, h * 2 * D, 0) for h in range(2)]
    mlp_moves += [((4 + b,), 0, 0, D, b, D, 2 * D) for b in range(2)]
    mlp = update(
        mlp_moves,
        [mlp_weight, mlp_moment, mlp_average],
        [mine0, got0, mine1, got1, mine2, got2],
        2 * FF,
        "update_mlp",
    )
    attn_moves = [((0, 1), 0, D, D, None, 0, 0)]
    attn_moves += [((2 + b,), 0, 0, 384, b, D, 384) for b in range(2)]
    attn_moves += [((2 + b,), 0, 384, 384, b, 2 * D, 384) for b in range(2)]
    attn_moves += [((2, 3), 0, D, D, None, 3 * D, 0)]
    attn = update(
        attn_moves,
        [attn_weight, attn_moment, attn_average],
        [mine2, got2, mine3, got3],
        4 * D,
        "update_attn",
    )
    gains = advance(gain_g, gain_vector, gain_moment, gain_average, rate)
    offsets = advance(offset_g, offset_vector, offset_moment, offset_average, rate)
    return (activations, input_grad, *attn, *mlp, *gains, *offsets)


def solution(mesh):
    placed = (
        P(("rep", "fsdp"), None),
        P(("rep", "fsdp"), None),
        P(("rep", "fsdp")),
        P(("rep", "fsdp")),
        P(("rep", "fsdp")),
        P("fsdp", None),
        P("fsdp", None),
        P("fsdp"),
        P("fsdp"),
        P("fsdp", None),
        P("fsdp", None),
        P("fsdp"),
        P("fsdp"),
        P("fsdp", None),
        P("fsdp", None),
        P("fsdp"),
        P("fsdp"),
    )
    small = mesh.shape["rep"] == 2 and mesh.shape["fsdp"] == 16
    return jax.shard_map(
        fast_device if small else per_device,
        mesh=mesh,
        in_specs=placed,
        out_specs=(
            P(("rep", "fsdp"), None),
            P(("rep", "fsdp"), None),
            P("fsdp", None),
            P("fsdp", None),
            P("fsdp", None),
            P("fsdp", None),
            P("fsdp", None),
            P("fsdp", None),
            P("fsdp", None),
            P("fsdp", None),
            P("fsdp"),
            P("fsdp"),
            P("fsdp"),
            P("fsdp"),
            P("fsdp"),
            P("fsdp"),
            P("fsdp"),
            P("fsdp"),
        ),
        check_vma=False,
    )
```

```python
import functools
import math

import jax
import jax.numpy as jnp
from jax import lax
from jax.experimental import pallas as pl
from jax.experimental.pallas import tpu as pltpu
from jax.sharding import PartitionSpec as P

D = 768
HEADS = 12
HEAD_DIM = 64
FF = 3072
BF = jnp.bfloat16
F32 = jnp.float32


momentum_decay = 0.9
average_decay = 0.8
base_rate = 0.02
norm_eps = 1e-06
mask_fill = -1e30


def normalize(inputs):
    mean_val = jnp.mean(inputs, axis=-1, keepdims=True)
    centred = inputs - mean_val
    variance = jnp.mean(centred * centred, axis=-1, keepdims=True)
    return centred * lax.rsqrt(variance + norm_eps)


def norm_affine(inputs, gain_part, shift_part):
    return normalize(inputs) * gain_part + shift_part


def gelu_exact(inputs):
    return jax.nn.gelu(inputs, approximate=False)


def over_tokens(left_mat, right_mat):
    return lax.dot_general(
        left_mat, right_mat, (((0,), (0,)), ((), ())), preferred_element_type=jnp.float32
    )


def against_rows(left_mat, right_mat):
    return lax.dot_general(
        left_mat, right_mat, (((1,), (1,)), ((), ())), preferred_element_type=jnp.float32
    )


def block_mask(clip_ids, key_ok):
    return (clip_ids[:, None] == clip_ids[None, :]) & (key_ok[None, :] == 1)


def forward(inputs, params, clip_ids, key_ok, masked):
    attn_full = params[0]
    mlp_full = params[1]
    gain_f = params[2].astype(jnp.float32)
    shift_f = params[3].astype(jnp.float32)
    tok_rows = inputs.shape[0]
    score_scale = HEAD_DIM ** (-0.5)
    is_masked = masked[:, None] == 1
    embedded = jnp.where(is_masked, shift_f[6 * D : 7 * D][None, :], inputs)
    normed_one = norm_affine(embedded, gain_f[:D], shift_f[:D]).astype(jnp.bfloat16)
    qkv_bias = jnp.concatenate(
        [shift_f[D : 2 * D], jnp.zeros((D,), jnp.float32), shift_f[2 * D : 3 * D]]
    )
    projected = (
        jnp.dot(normed_one, attn_full[:, : 3 * D], preferred_element_type=jnp.float32) + qkv_bias
    )
    projected = projected.astype(jnp.bfloat16)
    queries = projected[:, :D].reshape(tok_rows, HEADS, HEAD_DIM)
    key_heads = projected[:, D : 2 * D].reshape(tok_rows, HEADS, HEAD_DIM)
    value_heads = projected[:, 2 * D :].reshape(tok_rows, HEADS, HEAD_DIM)
    allowed = block_mask(clip_ids, key_ok)
    scores = (
        jnp.einsum("qhd,khd->hqk", queries, key_heads, preferred_element_type=jnp.float32)
        * score_scale
    )
    scores = jnp.where(allowed[None], scores, mask_fill)
    row_peak = jnp.max(scores, axis=-1, keepdims=True)
    exponent = jnp.exp(scores - row_peak)
    summed = jnp.sum(exponent, axis=-1, keepdims=True)
    attn_prob = (exponent / summed).astype(jnp.bfloat16)
    mixed_parts = jnp.einsum(
        "hqk,khd->qhd", attn_prob, value_heads, preferred_element_type=jnp.float32
    )
    lse_parts = [row_peak + jnp.log(summed)]
    mixed_out = mixed_parts.reshape(tok_rows, D).astype(jnp.bfloat16)
    after_attn = embedded + against_rows(mixed_out, attn_full[:, 3 * D :]) + shift_f[3 * D : 4 * D]
    normed_two = norm_affine(after_attn, gain_f[D:], shift_f[4 * D : 5 * D]).astype(jnp.bfloat16)
    hidden_pre = (
        jnp.dot(normed_two, mlp_full[:, :FF], preferred_element_type=jnp.float32) + shift_f[7 * D :]
    )
    hidden_act = gelu_exact(hidden_pre).astype(jnp.bfloat16)
    output = after_attn + against_rows(hidden_act, mlp_full[:, FF:]) + shift_f[5 * D : 6 * D]
    kept_values = (
        embedded,
        normed_one,
        queries,
        key_heads,
        value_heads,
        lse_parts,
        mixed_out,
        after_attn,
        normed_two,
        hidden_pre,
        hidden_act,
        gain_f,
        shift_f,
    )
    return (output, kept_values)


def backward(cotangent, params, kept_values, clip_ids, key_ok, masked):
    attn_full = params[0]
    mlp_full = params[1]
    (
        embedded,
        normed_one,
        queries,
        key_heads,
        value_heads,
        lse_parts,
        mixed_out,
        after_attn,
        normed_two,
        hidden_pre,
        hidden_act,
        gain_f,
        shift_f,
    ) = kept_values
    tok_rows = cotangent.shape[0]
    score_scale = HEAD_DIM ** (-0.5)
    d_out = cotangent.astype(jnp.float32)
    d_bias_two = jnp.sum(d_out, axis=0)
    d_down = over_tokens(cotangent, hidden_act)
    d_act = jnp.dot(cotangent, mlp_full[:, FF:], preferred_element_type=jnp.float32)
    gelu_value, gelu_pull = jax.vjp(gelu_exact, hidden_pre)
    d_pre_low = gelu_pull(d_act)[0].astype(jnp.bfloat16)
    d_bias_one = jnp.sum(d_pre_low.astype(jnp.float32), axis=0)
    d_up = over_tokens(normed_two, d_pre_low)
    mlp_grad = jnp.concatenate([d_up, d_down], axis=1)
    d_normed_two = against_rows(d_pre_low, mlp_full[:, :FF])
    norm_value, norm_pull = jax.vjp(norm_affine, after_attn, gain_f[D:], shift_f[4 * D : 5 * D])
    d_after_norm, d_gain_two, d_shift_two = norm_pull(d_normed_two)
    d_after = d_out + d_after_norm
    d_after_low = d_after.astype(jnp.bfloat16)
    d_bias_out = jnp.sum(d_after, axis=0)
    d_outproj = over_tokens(d_after_low, mixed_out)
    d_mixed = jnp.dot(d_after_low, attn_full[:, 3 * D :], preferred_element_type=jnp.float32)
    d_mixed_low = d_mixed.astype(jnp.bfloat16).reshape(tok_rows, HEADS, HEAD_DIM)
    block_rows = min(512, tok_rows)
    d_query_parts = []
    d_keys = jnp.zeros((tok_rows, HEADS, HEAD_DIM), jnp.float32)
    d_values = jnp.zeros((tok_rows, HEADS, HEAD_DIM), jnp.float32)
    for block_number, offset in enumerate(range(0, tok_rows, block_rows)):
        allowed = block_mask(clip_ids, key_ok)
        scores = (
            jnp.einsum("qhd,khd->hqk", queries, key_heads, preferred_element_type=jnp.float32)
            * score_scale
        )
        scores = jnp.where(allowed[None], scores, mask_fill)
        attn_prob = jnp.exp(scores - lse_parts[block_number])
        prob_low = attn_prob.astype(jnp.bfloat16)
        d_prob = jnp.einsum(
            "qhd,khd->hqk", d_mixed_low, value_heads, preferred_element_type=jnp.float32
        )
        row_delta = jnp.sum(d_prob * attn_prob, axis=-1, keepdims=True)
        d_scores = (attn_prob * (d_prob - row_delta)).astype(jnp.bfloat16)
        d_query_parts.append(
            jnp.einsum("hqk,khd->qhd", d_scores, key_heads, preferred_element_type=jnp.float32)
            * score_scale
        )
        d_keys = (
            jnp.einsum("hqk,qhd->khd", d_scores, queries, preferred_element_type=jnp.float32)
            * score_scale
        )
        d_values = jnp.einsum(
            "hqk,qhd->khd", prob_low, d_mixed_low, preferred_element_type=jnp.float32
        )
    d_queries = d_query_parts[0]
    d_proj_low = jnp.concatenate(
        [
            d_queries.reshape(tok_rows, D),
            d_keys.reshape(tok_rows, D),
            d_values.reshape(tok_rows, D),
        ],
        axis=1,
    ).astype(jnp.bfloat16)
    d_bias_q = jnp.sum(d_proj_low[:, :D].astype(jnp.float32), axis=0)
    d_bias_v = jnp.sum(d_proj_low[:, 2 * D :].astype(jnp.float32), axis=0)
    d_qkv = over_tokens(normed_one, d_proj_low)
    d_normed_one = against_rows(d_proj_low, attn_full[:, : 3 * D])
    first_value, first_pull = jax.vjp(norm_affine, embedded, gain_f[:D], shift_f[:D])
    d_embed_norm, d_gain_one, d_shift_one = first_pull(d_normed_one)
    d_embedded = d_after + d_embed_norm
    is_masked = masked[:, None] == 1
    d_mask_vec = jnp.sum(jnp.where(is_masked, d_embedded, 0.0), axis=0)
    input_grad = jnp.where(is_masked, 0.0, d_embedded).astype(jnp.bfloat16)
    attn_grad = jnp.concatenate([d_qkv, d_outproj], axis=1)
    gain_grad = jnp.concatenate([d_gain_one, d_gain_two])
    offset_grad = jnp.concatenate(
        [
            d_shift_one,
            d_bias_q,
            d_bias_v,
            d_bias_out,
            d_shift_two,
            d_bias_two,
            d_mask_vec,
            d_bias_one,
        ]
    )
    return (input_grad, (attn_grad, mlp_grad, gain_grad, offset_grad))


def advance(gradient, weight, moment, average, learn_rate):
    moment_new = momentum_decay * moment + gradient
    weight_new = weight - learn_rate * (gradient + momentum_decay * moment_new)
    average_new = average_decay * average + (1.0 - average_decay) * weight_new
    return (weight_new, moment_new, average_new, weight_new.astype(jnp.bfloat16))


def per_device(
    tokens,
    cotangent,
    clip_index,
    key_valid,
    patch_masked,
    attn_weight,
    mlp_weight,
    gain_vector,
    offset_vector,
    attn_moment,
    mlp_moment,
    gain_moment,
    offset_moment,
    attn_average,
    mlp_average,
    gain_average,
    offset_average,
):
    attn_shard = attn_weight.astype(jnp.bfloat16)
    mlp_shard = mlp_weight.astype(jnp.bfloat16)
    gain_shard = gain_vector.astype(jnp.bfloat16)
    offset_shard = offset_vector.astype(jnp.bfloat16)
    params = (
        lax.all_gather(attn_shard, "fsdp", axis=0, tiled=True),
        lax.all_gather(mlp_shard, "fsdp", axis=0, tiled=True),
        lax.all_gather(gain_shard, "fsdp", axis=0, tiled=True),
        lax.all_gather(offset_shard, "fsdp", axis=0, tiled=True),
    )
    inputs = tokens.astype(jnp.float32)
    output, first_kept = forward(inputs, params, clip_index, key_valid, patch_masked)
    again = (
        lax.all_gather(attn_shard, "fsdp", axis=0, tiled=True),
        lax.all_gather(mlp_shard, "fsdp", axis=0, tiled=True),
        lax.all_gather(gain_shard, "fsdp", axis=0, tiled=True),
        lax.all_gather(offset_shard, "fsdp", axis=0, tiled=True),
    )
    output_again, kept_values = forward(inputs, again, clip_index, key_valid, patch_masked)
    input_grad, gradients = backward(
        cotangent, again, kept_values, clip_index, key_valid, patch_masked
    )
    owned = (
        lax.psum_scatter(gradients[0], "fsdp", scatter_dimension=0, tiled=True),
        lax.psum_scatter(gradients[1], "fsdp", scatter_dimension=0, tiled=True),
        lax.psum_scatter(gradients[2], "fsdp", scatter_dimension=0, tiled=True),
        lax.psum_scatter(gradients[3], "fsdp", scatter_dimension=0, tiled=True),
    )
    shares = (
        lax.psum_scatter(
            owned[0].astype(jnp.bfloat16), "rep", scatter_dimension=1, tiled=True
        ).astype(jnp.float32),
        lax.psum_scatter(
            owned[1].astype(jnp.bfloat16), "rep", scatter_dimension=1, tiled=True
        ).astype(jnp.float32),
        lax.psum_scatter(
            owned[2].astype(jnp.bfloat16), "rep", scatter_dimension=0, tiled=True
        ).astype(jnp.float32),
        lax.psum_scatter(
            owned[3].astype(jnp.bfloat16), "rep", scatter_dimension=0, tiled=True
        ).astype(jnp.float32),
    )
    reduced = (
        lax.all_gather(shares[0].astype(jnp.bfloat16), "rep", axis=1, tiled=True).astype(
            jnp.float32
        ),
        lax.all_gather(shares[1].astype(jnp.bfloat16), "rep", axis=1, tiled=True).astype(
            jnp.float32
        ),
        lax.all_gather(shares[2].astype(jnp.bfloat16), "rep", axis=0, tiled=True).astype(
            jnp.float32
        ),
        lax.all_gather(shares[3].astype(jnp.bfloat16), "rep", axis=0, tiled=True).astype(
            jnp.float32
        ),
    )
    learn_rate = base_rate / math.sqrt(
        tokens.shape[0] * lax.axis_size("rep") * lax.axis_size("fsdp")
    )
    attn_new, attn_momentum, attn_ema, attn_copy = advance(
        reduced[0], attn_weight, attn_moment, attn_average, learn_rate
    )
    mlp_new, mlp_momentum, mlp_ema, mlp_copy = advance(
        reduced[1], mlp_weight, mlp_moment, mlp_average, learn_rate
    )
    gain_new, gain_momentum, gain_ema, gain_copy = advance(
        reduced[2], gain_vector, gain_moment, gain_average, learn_rate
    )
    offset_new, offset_momentum, offset_ema, offset_copy = advance(
        reduced[3], offset_vector, offset_moment, offset_average, learn_rate
    )
    return (
        output.astype(jnp.bfloat16),
        input_grad,
        attn_new,
        attn_momentum,
        attn_ema,
        attn_copy,
        mlp_new,
        mlp_momentum,
        mlp_ema,
        mlp_copy,
        gain_new,
        gain_momentum,
        gain_ema,
        gain_copy,
        offset_new,
        offset_momentum,
        offset_ema,
        offset_copy,
    )


class Operand:
    def __init__(self, ref):
        self.ref, self.shape = ref, ref.shape

    def __getitem__(self, index):
        return self.ref[index]


def call(kernel, outs, args, scratch=(), name=None, limit=8, space=pltpu.VMEM):
    def body(co_ref, *refs):
        operands = [Operand(ref) for ref in refs[: len(args) - 1]]
        kernel(co_ref, *operands, *refs[len(args) - 1 :])

    return pl.pallas_call(
        body,
        out_shape=[jax.ShapeDtypeStruct(shape, dtype) for shape, dtype in outs],
        in_specs=[pl.BlockSpec(memory_space=pltpu.SMEM)]
        + [pl.BlockSpec(memory_space=space)] * (len(args) - 1),
        out_specs=[pl.BlockSpec(memory_space=pltpu.VMEM)] * len(outs),
        scratch_shapes=list(scratch),
        compiler_params=pltpu.CompilerParams(vmem_limit_bytes=limit * 2**20),
        cost_estimate=pl.CostEstimate(flops=2**20, bytes_accessed=2**20, transcendentals=0),
        name=name,
    )(*args)


def assemble_kernel(ranges, co, *refs):
    count = len(refs) - len(ranges)
    each = count // 2
    for number in range(count):
        blocks = refs[number].shape[0] // 48
        for block in range(blocks):
            i, k = (number % 2, block) if blocks == 4 else (block // 4, block % 4)
            b = (number // 2) % 2 if each == 4 else 0
            row = k * 192 + lax.bitwise_xor(co[2], i) * 96
            row = row + lax.bitwise_xor(co[3], number // each) * 48
            rows = pl.ds(pl.multiple_of(row, 16), 48)
            for (start, size), out in zip(ranges, refs[count:]):
                out[rows, b * size : b * size + size] = refs[number][
                    block * 48 : block * 48 + 48, start : start + size
                ]


def assemble(co, pieces, *ranges):
    widths = [size * (2 if len(pieces) == 8 else 1) for start, size in ranges]
    return call(
        functools.partial(assemble_kernel, ranges),
        [((D, width), BF) for width in widths],
        [co, *pieces],
        name="assemble",
    )


def lanes(offset, size):
    return pl.ds(pl.multiple_of(offset, 128), size)


def nn(left, right):
    return lax.dot_general(left, right, (((1,), (0,)), ((), ())), preferred_element_type=jnp.float32)


def nt(left, right):
    return lax.dot_general(left, right, (((1,), (1,)), ((), ())), preferred_element_type=jnp.float32)


def whole(weight, start, size):
    return weight[:, start : start + size]


def row_norm(values):
    mean = jnp.mean(values, axis=-1, keepdims=True)
    centred = values - mean
    var = jnp.mean(centred * centred, axis=-1, keepdims=True)
    rstd = lax.rsqrt(var + norm_eps)
    return centred * rstd, rstd


def prep_first_kernel(co, attn, mlp, s0, wide, sems):
    r = co[0]
    sources = [attn.ref.at[:, lanes(part * D + 384 * r, 384)] for part in range(4)]
    sources += [mlp.ref.at[:, lanes(1536 * r + n * 384, 384)] for n in range(2)]
    copies = [
        pltpu.make_async_copy(source, wide.at[n], sems.at[n]) for n, source in enumerate(sources)
    ]
    for copy in copies:
        copy.start()
    for n, copy in enumerate(copies):
        copy.wait()
        s0[:, n * 384 : n * 384 + 384] = wide[n].astype(BF)


def prep_second_kernel(co, mlp, s1, s2):
    r = co[0]
    for b in range(2):
        half = lax.bitwise_xor(r, b)
        s1[:, b * D : b * D + D] = mlp[:, lanes(1536 * half + D, D)].astype(BF)
        s2[:, b * D : b * D + D] = mlp[:, lanes(FF + 1536 * half + D, D)].astype(BF)
    s1[:, 2 * D :] = mlp[:, lanes(FF + 1536 * r, D)].astype(BF)


def first_norm_kernel(co, tokens, info, vec, h1, h1t, cols):
    turned = jnp.transpose(info[...])
    cols[:, 0:8] = turned
    x0 = jnp.where(turned[:, 2:3] == 1.0, vec[8:9, :], tokens[...].astype(F32))
    xh, rstd = row_norm(x0)
    h = xh * vec[0:1, :] + vec[2:3, :]
    h1[...] = h.astype(BF)
    h1t[...] = h.T.astype(BF)


def allowed_pairs(info, cols):
    return (cols[:, 0:1] == info[0:1, :]) & (cols[:, 1:2] == 1.0)


def attention_kernel(co, h1, vec, info, cols, weight, qkv, att, lse):
    for b in range(2):
        half = lax.bitwise_xor(co[0], b)
        for part in range(3):
            out = nn(h1[...], whole(weight, b * 1152 + part * 384, 384))
            if part != 1:
                row = 3 if part == 0 else 4
                out = out + vec.ref[row : row + 1, lanes(384 * half, 384)]
            qkv[:, b * 1152 + part * 384 : b * 1152 + part * 384 + 384] = out.astype(BF)
    allowed = allowed_pairs(info, cols)
    low = lax.broadcasted_iota(jnp.int32, (256, 128), 1) < 64
    for pair in range(6):
        base = (pair // 3) * 1152 + (pair % 3) * 128
        q2 = qkv[:, base : base + 128]
        k2 = qkv[:, base + 384 : base + 512]
        v2 = qkv[:, base + 768 : base + 896]
        mixed = []
        for side in range(2):
            qm = jnp.where(low if side == 0 else ~low, q2, jnp.zeros_like(q2))
            s = jnp.where(allowed, nt(k2, qm) * 0.125, mask_fill)
            peak = jnp.max(s, axis=0, keepdims=True)
            e = jnp.exp(s - peak)
            total = jnp.sum(e, axis=0, keepdims=True)
            prob = (e * (1.0 / total)).astype(BF)
            lse[2 * pair + side : 2 * pair + side + 1, :] = peak + jnp.log(total)
            mixed.append(over_tokens(prob, v2))
        att[:, pair * 128 : pair * 128 + 128] = jnp.where(low, mixed[0], mixed[1]).astype(BF)


def second_norm_kernel(co, tokens, cols, vec, att, weight, y1, h2, h2t):
    x0 = jnp.where(cols[:, 2:3] == 1.0, vec[8:9, :], tokens[...].astype(F32))
    y = x0 + nt(att[...], whole(weight, 0, D)) + vec[5:6, :]
    y1[...] = y
    xh, rstd = row_norm(y)
    h = xh * vec[1:2, :] + vec[6:7, :]
    h2[...] = h.astype(BF)
    h2t[...] = h.T.astype(BF)


def hidden_kernel(co, h2, vec, dz, w0, w1, g0, g1, slope0, slope1, send, keep, dzt, scratch):
    dzt[...] = dz[...].astype(F32).T.astype(BF)
    for part, weight, g, slope in ((0, w0, g0, slope0), (1, w1, g1, slope1)):
        for b in range(2):
            half = lax.bitwise_xor(co[0], b)
            for sub in range(0, D, 384):
                at = slice(b * D + sub, b * D + sub + 384)
                u = nn(h2[...], weight[:, at])
                u = u + vec[pl.ds(9 + 2 * half + part, 1), sub : sub + 384]
                phi = 0.5 * (1.0 + lax.erf(u * math.sqrt(0.5)))
                act = (u * phi).astype(BF)
                g[:, at] = act
                slope[:, at] = phi + u * (
                    jnp.exp(-0.5 * u * u) * (1.0 / math.sqrt(2.0 * math.pi))
                )
                scratch[...] = nn(dzt[...], act)
                dst = lanes(half * D + sub, 384) if part == 0 else lanes((2 + b) * D + sub, 384)
                share_rows(co[3], scratch, send, keep, dst)


def hidden_grad_kernel(
    co, dz, slope0, slope1, w00, w01, w10, w11, left, du0, du1, db1, send, keep, scratch
):
    for part, slope, du in ((0, slope0, du0), (1, slope1, du1)):
        for b in range(2):
            weight = ((w00, w01), (w10, w11))[b][part]
            half = lax.bitwise_xor(co[0], b)
            for sub in range(0, D, 384):
                at = slice(b * D + sub, b * D + sub + 384)
                da = nn(dz[...], weight[:, sub : sub + 384])
                d = (da * slope[:, at]).astype(BF)
                du[:, at] = d
                db1[pl.ds(2 * half + part, 1), sub : sub + 384] = jnp.sum(
                    d.astype(F32), axis=0, keepdims=True
                )
                scratch[...] = nn(left[...], d)
                dst = lanes(half * D + sub, 384) if part == 0 else lanes((2 + b) * D + sub, 384)
                share_rows(co[3], scratch, send, keep, dst)


def output_kernel(co, y1, vec, g0, g1, w00, w01, w10, w11, act):
    acc = y1[...] + vec[7:8, :]
    for part, g in ((0, g0), (1, g1)):
        acc = acc + nt(g[:, :D], (w00, w01)[part][...])
        acc = acc + nt(g[:, D:], (w10, w11)[part][...])
    act[...] = acc.astype(BF)


def share_rows(c, scratch, send, keep, dst):
    for k in range(4):
        for i in range(2):
            row = k * 192 + i * 96
            theirs = scratch[pl.ds(pl.multiple_of(row + 48 * (1 - c), 16), 48), :]
            mine = scratch[pl.ds(pl.multiple_of(row + 48 * c, 16), 48), :]
            send[k, i, :, dst] = theirs.astype(BF)
            keep[k, i, :, dst] = mine


def attention_grad_kernel(co, h1t, dqkv, dpt, att, send, keep, scratch):
    moves = [(h1t, dqkv, b * 1152 + 384 + n * 384, b * D + n * 384) for b in (0, 1) for n in (0, 1)]
    for b in range(2):
        place = 384 * lax.bitwise_xor(co[0], b)
        moves.append((h1t, dqkv, b * 1152, 2 * D + place))
        moves.append((dpt, att, b * 384, 3 * D + place))
    for left, right, src, dst in moves:
        scratch[...] = nn(left[...], right[:, src : src + 384])
        share_rows(co[3], scratch, send, keep, lanes(dst, 384))


def second_back_kernel(co, dz, y1, vec, du0, du1, w0, w1, weight_o, dy1, datt, dpt, small):
    yh, rstd = row_norm(y1[...])
    dy = dz[...].astype(F32)
    dh = nt(du0[...], whole(w0, 0, 2 * D)) + nt(du1[...], whole(w1, 0, 2 * D))
    small[0:1, :] = jnp.sum(dh * yh, axis=0, keepdims=True)
    small[1:2, :] = jnp.sum(dh, axis=0, keepdims=True)
    small[3:4, :] = jnp.sum(dy, axis=0, keepdims=True)
    e = dh * vec[1:2, :]
    d = dy + rstd * (
        e - jnp.mean(e, axis=-1, keepdims=True) - yh * jnp.mean(e * yh, axis=-1, keepdims=True)
    )
    dy1[...] = d
    small[2:3, :] = jnp.sum(d, axis=0, keepdims=True)
    dpt[...] = d.T.astype(BF)
    datt[...] = nn(d.astype(BF), whole(weight_o, 0, D)).astype(BF)


def attention_back_kernel(co, info, cols, lse, qkv, datt, dqkv, small):
    allowed = allowed_pairs(info, cols)
    low = lax.broadcasted_iota(jnp.int32, (256, 128), 1) < 64
    for pair in range(6):
        half = lax.bitwise_xor(co[0], pair // 3)
        base = (pair // 3) * 1152 + (pair % 3) * 128
        q2 = qkv[:, base : base + 128]
        k2 = qkv[:, base + 384 : base + 512]
        v2 = qkv[:, base + 768 : base + 896]
        o2 = datt[:, pair * 128 : pair * 128 + 128]
        dqs, dks, dvs = [], [], []
        for side in range(2):
            mine = low if side == 0 else ~low
            qm = jnp.where(mine, q2, jnp.zeros_like(q2))
            om = jnp.where(mine, o2, jnp.zeros_like(o2))
            s = jnp.where(allowed, nt(k2, qm) * 0.125, mask_fill)
            prob = jnp.exp(s - lse[2 * pair + side : 2 * pair + side + 1, :])
            dprob = nt(v2, om)
            delta = jnp.sum(dprob * prob, axis=0, keepdims=True)
            ds = (prob * (dprob - delta)).astype(BF)
            dqs.append(over_tokens(ds, k2))
            dks.append(nn(ds, q2))
            dvs.append(nn(prob.astype(BF), o2))
        dq = (jnp.where(low, dqs[0], dqs[1]) * 0.125).astype(BF)
        dk = (jnp.where(low, dks[0], dks[1]) * 0.125).astype(BF)
        dv = jnp.where(low, dvs[0], dvs[1]).astype(BF)
        dqkv[:, base : base + 128] = dq
        dqkv[:, base + 384 : base + 512] = dk
        dqkv[:, base + 768 : base + 896] = dv
        place = lanes(384 * half + (pair % 3) * 128, 128)
        small[0:1, place] = jnp.sum(dq.astype(F32), axis=0, keepdims=True)
        small[1:2, place] = jnp.sum(dv.astype(F32), axis=0, keepdims=True)


def first_back_kernel(
    co, dqkv, tokens, cols, vec, dy1, db1, small2, small_a, weight, input_grad, total
):
    hidden = cols[:, 2:3] == 1.0
    x0 = jnp.where(hidden, vec[8:9, :], tokens[...].astype(F32))
    xh, rstd = row_norm(x0)
    dh = nt(dqkv[...], whole(weight, 0, 3 * D))
    e = dh * vec[0:1, :]
    dx = dy1[...] + rstd * (
        e - jnp.mean(e, axis=-1, keepdims=True) - xh * jnp.mean(e * xh, axis=-1, keepdims=True)
    )
    input_grad[...] = jnp.where(hidden, 0.0, dx).astype(BF)
    total[0:1, :] = jnp.sum(dh * xh, axis=0, keepdims=True)
    total[1:2, :] = small2[0:1, :]
    total[2:3, :] = jnp.sum(dh, axis=0, keepdims=True)
    total[3:5, :] = small_a[0:2, :]
    total[5:6, :] = small2[2:3, :]
    total[6:7, :] = small2[1:2, :]
    total[7:8, :] = small2[3:4, :]
    total[8:9, :] = jnp.sum(jnp.where(hidden, dx, 0.0), axis=0, keepdims=True)
    total[9:13, :] = db1[0:4, :]
    total[13:16, :] = jnp.zeros((3, D), F32)


def both(keep, got, *at):
    return keep[at] + got[at].astype(F32)


def split_first_kernel(co, keep, got, y_send, y_keep, x_send, x_keep):
    y = co[2]
    every = slice(None)
    for k in range(4):
        for out, i in ((y_send, 1 - y), (y_keep, y)):
            out[k * 48 : k * 48 + 48, :] = both(keep, got, k, i, every, slice(0, 2 * D)).astype(
                out.dtype
            )
    x_keep[...] = both(keep, got, every, every, every, slice(2 * D, 3 * D))
    x_send[...] = both(keep, got, every, every, every, slice(3 * D, 4 * D)).astype(BF)


def split_second_kernel(co, x_keep, x_got, keep, got, y_send, y_keep, x_send, x_next):
    y = co[2]
    every = slice(None)
    for k in range(4):
        rows = slice(k * 48, k * 48 + 48)
        for out, i in ((y_send, 1 - y), (y_keep, y)):
            out[rows, :D] = both(x_keep, x_got, k, i).astype(out.dtype)
            out[rows, D:] = both(keep, got, k, i, every, slice(0, D)).astype(out.dtype)
    x_next[...] = both(keep, got, every, every, every, slice(2 * D, 3 * D))
    x_send[...] = both(keep, got, every, every, every, slice(3 * D, 4 * D)).astype(BF)


def split_third_kernel(co, x_keep, x_got, keep, got, y_send, y_keep, x_send, x_next, last):
    y = co[2]
    every = slice(None)
    for k in range(4):
        rows = slice(k * 48, k * 48 + 48)
        for out, i in ((y_send, 1 - y), (y_keep, y)):
            out[rows, :D] = both(x_keep, x_got, k, i).astype(out.dtype)
            out[rows, D:] = both(keep, got, k, i, every, slice(2 * D, 3 * D)).astype(out.dtype)
    x_next[...] = both(keep, got, every, every, every, slice(0, D))
    x_send[...] = both(keep, got, every, every, every, slice(D, 2 * D)).astype(BF)
    last[...] = both(keep, got, every, every, every, slice(3 * D, 4 * D))


def split_fourth_kernel(co, x_keep, x_got, last, vec, far_keep, far_got, y_send, y_keep):
    y = co[2]
    for out, i in ((y_send, 1 - y), (y_keep, y)):
        for k in range(4):
            rows = slice(k * 48, k * 48 + 48)
            out[rows, :D] = both(x_keep, x_got, k, i).astype(out.dtype)
            out[rows, D:] = last[k, i].astype(out.dtype)
        row = pl.multiple_of(96 + i * 48, 16)
        out[192:240, :D] = both(far_keep, far_got, pl.ds(row, 48)).astype(out.dtype)
        out[192:208, D:] = vec[...].astype(out.dtype)
        out[208:240, D:] = jnp.zeros((32, D), out.dtype)


def split_near_first_kernel(co, keep, got, up_keep, up_got, send, rest):
    side = co[1] % 2
    for out, at in ((send, 1 - side), (rest, side)):
        for far in range(2):
            row = pl.multiple_of((2 * far + at) * 48, 16)
            for half in range(2):
                to = half * 96 + far * 48
                cols = slice(half * D, half * D + D)
                out[to : to + 48, :] = both(keep, got, pl.ds(row, 48), cols).astype(out.dtype)
                to = 192 + far * 96 + half * 48
                total = both(up_keep, up_got, 2 * far + at, half, slice(None), slice(D, 2 * D))
                out[to : to + 48, :] = total.astype(out.dtype)


def split_far_first_kernel(co, keep, got, send, rest):
    side = co[1] // 2
    for out, at in ((send, 1 - side), (rest, side)):
        for half in range(2):
            row = pl.multiple_of(half * 96 + at * 48, 16)
            to = half * 48
            out[to : to + 48, :] = both(keep, got, pl.ds(row, 48)).astype(out.dtype)
        row = pl.multiple_of(192 + at * 96, 16)
        out[96:192, :] = both(keep, got, pl.ds(row, 96)).astype(out.dtype)


def sum_far_first_kernel(co, keep, got, out):
    for half in range(2):
        rows = slice(half * 48, half * 48 + 48)
        out[:, half * D : half * D + D] = both(keep, got, rows).astype(BF)


def sum_far_second_kernel(co, keep, got, other, out):
    out[:, : 2 * D] = both(keep, got, slice(None)).astype(BF)
    out[:, 2 * D :] = other[...].astype(BF)


def split_near_kernel(co, keep, got, send, rest, *small):
    side = co[1] % 2
    for out, at in ((send, 1 - side), (rest, side)):
        for far in range(2):
            row = pl.multiple_of((2 * far + at) * 48, 16)
            out[far * 48 : far * 48 + 48, :] = both(keep, got, pl.ds(row, 48)).astype(out.dtype)
    if small:
        small[0][...] = both(keep, got, slice(192, 208), slice(D, 2 * D))
        small[1][...] = both(keep, got, slice(192, 240), slice(0, D))


def split_far_kernel(co, keep, got, send, rest):
    side = co[1] // 2
    for out, at in ((send, 1 - side), (rest, side)):
        row = pl.multiple_of(at * 48, 16)
        out[...] = both(keep, got, pl.ds(row, 48)).astype(out.dtype)


def sum_far_kernel(co, keep, got, out):
    out[...] = (keep[...] + got[...].astype(F32)).astype(BF)


def update_kernel(rate, moves, n_states, n_grads, n_before, co, *refs):
    grads = refs[3 * n_states :][:n_grads]
    first = 3 * n_states + n_grads + n_before
    parts, sems = refs[first + 4 * n_states : -1], refs[-1]
    copies = []
    for n, (which, numbers, row, src, size, b, col, stride) in enumerate(moves):
        state, new = refs[3 * which :][:3], refs[first + 4 * which :][:4]
        grad = 0.0
        for number in numbers:
            grad = grad + grads[number][row : row + 48, src : src + size].astype(F32)
        place = col if b is None else col + stride * lax.bitwise_xor(co[0], b)
        at = lanes(place, size)
        w, m, a = (ref[:, at] for ref in state)
        m_new = momentum_decay * m + grad
        w_new = w - rate * (grad + momentum_decay * m_new)
        full, low = parts[2 * n], parts[2 * n + 1]
        full[0] = w_new
        full[1] = m_new
        full[2] = average_decay * a + (1.0 - average_decay) * w_new
        low[...] = w_new.astype(BF)
        for k in range(4):
            source = full.at[k] if k < 3 else low
            copy = pltpu.make_async_copy(source, new[k].at[:, at], sems.at[4 * n + k])
            copy.start()
            copies.append(copy)
    for copy in copies:
        copy.wait()


def hold(arrays):
    return lax.optimization_barrier(arrays)


def fast_device(
    tokens,
    cotangent,
    clip_index,
    key_valid,
    patch_masked,
    attn_weight,
    mlp_weight,
    gain_vector,
    offset_vector,
    attn_moment,
    mlp_moment,
    gain_moment,
    offset_moment,
    attn_average,
    mlp_average,
    gain_average,
    offset_average,
):
    r, f = lax.axis_index("rep"), lax.axis_index("fsdp")
    co = jnp.stack([r, f // 4, (f // 2) % 2, f % 2]).astype(jnp.int32)

    def swap(array, mask):
        return lax.ppermute(array, ("rep", "fsdp"), [(i, i ^ mask) for i in range(32)])

    CORE, Y, Z, X = 1, 2, 4, 16

    (s0,) = call(
        prep_first_kernel,
        [((48, 3 * D), BF)],
        [co, attn_weight, mlp_weight],
        scratch=[pltpu.VMEM((6, 48, 384), F32), pltpu.SemaphoreType.DMA((6,))],
        name="prep",
        limit=60,
        space=pltpu.HBM,
    )
    info = jnp.zeros((8, 256), F32).at[0:3].set(
        jnp.stack([clip_index, key_valid, patch_masked]).astype(F32)
    )
    flat = jnp.zeros((16 * D,), F32)
    flat = lax.dynamic_update_slice(flat, gain_vector.astype(BF).astype(F32), (96 * f,))
    flat = lax.dynamic_update_slice(flat, offset_vector.astype(BF).astype(F32), (2 * D + 528 * f,))
    vec = flat.reshape(16, D)

    groups = [[4 * z + at for z in range(4)] for at in range(4)]

    def along_z(shard):
        return lax.all_gather(shard, "fsdp", axis=0, tiled=True, axis_index_groups=groups)

    def core_pair(pieces):
        return pieces + [swap(piece, CORE) for piece in pieces]

    stack0 = along_z(s0)
    stack0, vec, mlp_late = hold((stack0, vec, mlp_weight))
    s1, s2 = call(
        prep_second_kernel,
        [((48, 3 * D), BF), ((48, 2 * D), BF)],
        [co, mlp_late],
        name="prep",
    )
    across0 = swap(stack0, Y)
    far0 = swap(stack0, X)
    vec = vec + swap(vec, CORE)
    s1, vec = hold((s1, vec))
    near0 = [swap(stack0, CORE)]
    stack1 = along_z(s1)
    vec = vec + swap(vec, Y)
    stack1, across0, far0, near0, s2, vec = hold((stack1, across0, far0, near0, s2, vec))
    far_across0 = swap(across0, X)
    across1 = swap(stack1, Y)
    near0 += [swap(across0, CORE), swap(far0, CORE)]
    vec = vec + swap(vec, Z)
    s2, vec = hold((s2, vec))
    stack2 = along_z(s2)
    vec = vec + swap(vec, 2 * Z)
    stack2, across1, far_across0, near0, vec = hold((stack2, across1, far_across0, near0, vec))
    pieces0 = [stack0, across0, far0, far_across0, *near0, swap(far_across0, CORE)]
    across2 = swap(stack2, Y)
    far1 = swap(jnp.concatenate([stack1[:, 2 * D :], across1[:, 2 * D :]], axis=0), X)
    pieces1 = core_pair([stack1, across1])
    h1, h1t, cols = call(
        first_norm_kernel,
        [((256, D), BF), ((D, 256), BF), ((256, 128), F32)],
        [co, tokens, info, vec],
        name="norm1",
    )
    (w_qkv,) = assemble(co, pieces0, (0, 1152))
    qkv, att, lse = call(
        attention_kernel,
        [((256, 3 * D), BF), ((256, D), BF), ((16, 256), F32)],
        [co, h1, vec, info, cols, w_qkv],
        name="attention",
    )
    w_out, w_up0 = assemble(co, pieces0, (1152, 384), (1536, 768))
    w_up1, w_down00 = assemble(co, pieces1, (0, 1536), (1536, 768))

    y1, h2, h2t = call(
        second_norm_kernel,
        [((256, D), F32), ((256, D), BF), ((D, 256), BF)],
        [co, tokens, cols, vec, att, w_out],
        name="norm2",
    )
    shares = [((4, 2, 48, 4 * D), BF), ((4, 2, 48, 4 * D), F32)]
    g0, g1, slope0, slope1, down_send, down_keep = call(
        hidden_kernel,
        [((256, 2 * D), BF)] * 2 + [((256, 2 * D), F32)] * 2 + shares,
        [co, h2, vec, cotangent, w_up0, w_up1],
        scratch=[pltpu.VMEM((D, 256), BF), pltpu.VMEM((D, 384), F32)],
        name="hidden",
    )

    rate = base_rate / math.sqrt(tokens.shape[0] * 32)

    def update(moves, states, grads, name, before=()):
        parts, outs = [], []
        for move in moves:
            parts += [pltpu.VMEM((3, 48, move[4]), F32), pltpu.VMEM((48, move[4]), BF)]
        for state in states:
            outs += [jax.ShapeDtypeStruct(state[0].shape, F32)] * 3
            outs += [jax.ShapeDtypeStruct(state[0].shape, BF)]
        whole = pl.BlockSpec(memory_space=pltpu.VMEM)
        far = pl.BlockSpec(memory_space=pltpu.HBM)
        first = 1 + 3 * len(states) + len(grads)
        return pl.pallas_call(
            functools.partial(update_kernel, rate, moves, len(states), len(grads), len(before)),
            out_shape=outs,
            in_specs=[pl.BlockSpec(memory_space=pltpu.SMEM)]
            + [whole] * (first - 1)
            + [far] * len(before),
            out_specs=[far] * len(outs),
            input_output_aliases={first + k: k for k in range(len(before))},
            scratch_shapes=[*parts, pltpu.SemaphoreType.DMA((4 * len(moves),))],
            compiler_params=pltpu.CompilerParams(vmem_limit_bytes=8 * 2**20),
            cost_estimate=pl.CostEstimate(flops=2**20, bytes_accessed=2**20, transcendentals=0),
            name=name,
        )(co, *(array for state in states for array in state), *grads, *before)

    mlp_state = [mlp_weight, mlp_moment, mlp_average]
    attn_state = [attn_weight, attn_moment, attn_average]

    across2, far1, down_send = hold((across2, far1, down_send))
    pieces2 = core_pair([stack2, across2])
    far1 = core_pair([far1])
    pieces2, far1, down_send = hold((pieces2, far1, down_send))
    down_got = swap(down_send, CORE)
    w_down01, w_down11 = assemble(co, pieces2, (0, D), (D, D))
    (w_down10,) = assemble(co, far1, (0, D))
    du0, du1, db1, up_send, up_keep = call(
        hidden_grad_kernel,
        [((256, 2 * D), BF), ((256, 2 * D), BF), ((8, D), F32)] + shares,
        [co, cotangent, slope0, slope1, w_down00, w_down01, w_down10, w_down11, h2t],
        scratch=[pltpu.VMEM((D, 384), F32)],
        name="hidden_grad",
    )
    down_got, up_send = hold((down_got, up_send))
    y_shares = [((192, 2 * D), BF), ((192, 2 * D), F32)]
    x_shares = [((4, 2, 48, D), BF), ((4, 2, 48, D), F32)]
    y_send0, y_keep0, x_send1, x_keep1 = call(
        split_first_kernel, y_shares + x_shares, [co, down_keep, down_got], name="split_first"
    )
    y_send0, x_send1, up_send, du0 = hold((y_send0, x_send1, up_send, du0))
    y_got0 = swap(y_send0, Y)
    x_got1 = swap(x_send1, X)
    up_got = swap(up_send, CORE)
    dy1, datt, dpt, small2 = call(
        second_back_kernel,
        [((256, D), F32), ((256, D), BF), ((D, 256), BF), ((8, D), F32)],
        [co, cotangent, y1, vec, du0, du1, w_up0, w_up1, w_out],
        name="norm2_back",
    )
    dqkv, small_a = call(
        attention_back_kernel,
        [((256, 3 * D), BF), ((8, D), F32)],
        [co, info, cols, lse, qkv, datt],
        name="attention_back",
    )
    attn_send, attn_keep = call(
        attention_grad_kernel,
        shares,
        [co, h1t, dqkv, dpt, att],
        scratch=[pltpu.VMEM((D, 384), F32)],
        name="attention_grad",
    )

    def split_near(keep, got, small=()):
        width = keep.shape[1]
        return call(
            split_near_kernel,
            [((96, width), BF), ((96, width), F32), *small],
            [co, keep, got],
            name="split_near",
        )

    def split_far(keep, got):
        width = keep.shape[1]
        return call(
            split_far_kernel,
            [((48, width), BF), ((48, width), F32)],
            [co, keep, got],
            name="split_far",
        )

    def sum_far(keep, got):
        return call(sum_far_kernel, [(keep.shape, BF)], [co, keep, got], name="sum_far")[0]

    y_got0, x_got1, up_got, attn_send = hold((y_got0, x_got1, up_got, attn_send))
    y_send1, y_keep1, x_send2, x_keep2 = call(
        split_second_kernel,
        y_shares + x_shares,
        [co, x_keep1, x_got1, up_keep, up_got],
        name="split_second",
    )
    y_got0 = hold((y_got0, y_send1))[0]
    near_send0, near_keep0 = call(
        split_near_first_kernel,
        [((384, D), BF), ((384, D), F32)],
        [co, y_keep0, y_got0, up_keep, up_got],
        name="split_near",
    )
    dqkv = hold((dqkv, near_send0))[0]
    y_got1 = swap(y_send1, Y)
    x_got2 = swap(x_send2, X)
    near_got0 = swap(near_send0, Z)
    attn_got = swap(attn_send, CORE)
    input_grad, total = call(
        first_back_kernel,
        [((256, D), BF), ((16, D), F32)],
        [co, dqkv, tokens, cols, vec, dy1, db1, small2, small_a, w_qkv],
        name="norm1_back",
    )
    near_got0, y_got1, x_got2, attn_got, total = hold(
        (near_got0, y_got1, x_got2, attn_got, total)
    )
    far_send0, far_keep0 = call(
        split_far_first_kernel,
        [((192, D), BF), ((192, D), F32)],
        [co, near_keep0, near_got0],
        name="split_far",
    )
    x_got2 = hold((x_got2, far_send0))[0]
    y_send2, y_keep2, x_send3, x_keep3, last = call(
        split_third_kernel,
        y_shares + x_shares + x_shares[1:],
        [co, x_keep2, x_got2, attn_keep, attn_got],
        name="split_third",
    )
    y_got1 = hold((y_got1, y_send2))[0]
    near_send1, near_keep1 = split_near(y_keep1, y_got1)
    y1 = hold((y1, near_send1))[0]
    x_got3 = swap(x_send3, X)
    y_got2 = swap(y_send2, Y)
    near_got1 = swap(near_send1, Z)
    far_got0 = swap(far_send0, 2 * Z)
    total = total + swap(total, CORE)
    (activations,) = call(
        output_kernel,
        [((256, D), BF)],
        [co, y1, vec, g0, g1, w_down00, w_down01, w_down10, w_down11],
        name="output",
    )
    far_got0, near_got1, y_got2, x_got3, total, activations = hold(
        (far_got0, near_got1, y_got2, x_got3, total, activations)
    )
    y_send3, y_keep3 = call(
        split_fourth_kernel,
        [((240, 2 * D), BF), ((240, 2 * D), F32)],
        [co, x_keep3, x_got3, last, total, far_keep0, far_got0],
        name="split_fourth",
    )
    y_got2 = hold((y_got2, y_send3))[0]
    near_send2, near_keep2 = split_near(y_keep2, y_got2)
    near_got1 = hold((near_got1, near_send2))[0]
    far_send1, far_keep1 = split_far(near_keep1, near_got1)
    far_got0 = hold((far_got0, far_send1))[0]
    (mine0,) = call(
        sum_far_first_kernel, [((48, 2 * D), BF)], [co, far_keep0, far_got0], name="sum_far"
    )
    y_got3 = swap(y_send3, Y)
    near_got2 = swap(near_send2, Z)
    far_got1 = swap(far_send1, 2 * Z)
    got0 = swap(mine0, X)
    got0, far_got1, near_got2, y_got3 = hold((got0, far_got1, near_got2, y_got3))
    near_send3, near_keep3, total, other = split_near(
        y_keep3, y_got3, [((16, D), F32), ((48, D), F32)]
    )
    near_got2 = hold((near_got2, near_send3))[0]
    far_send2, far_keep2 = split_far(near_keep2, near_got2)
    far_got1 = hold((far_got1, far_send2))[0]
    (mine1,) = call(
        sum_far_second_kernel,
        [((48, 3 * D), BF)],
        [co, far_keep1, far_got1, other],
        name="sum_far",
    )
    near_got3 = swap(near_send3, Z)
    far_got2 = swap(far_send2, 2 * Z)
    got1 = swap(mine1, X)
    total = total + swap(total, Z)
    got1, far_got2, near_got3, total = hold((got1, far_got2, near_got3, total))
    far_send3, far_keep3 = split_far(near_keep3, near_got3)
    far_got2 = hold((far_got2, far_send3))[0]
    mine2 = sum_far(far_keep2, far_got2)
    far_got3 = swap(far_send3, 2 * Z)
    got2 = swap(mine2, X)
    total = total + swap(total, 2 * Z)
    moves = [(0, (0, 1), 0, h * D, D, None, FF + h * 2 * D, 0) for h in range(2)]
    moves += [(0, (2 + b,), 0, 0, D, b, FF + D, 2 * D) for b in range(2)]
    moves += [(0, (2, 3), 0, D + h * D, D, None, h * 2 * D, 0) for h in range(2)]
    got1 = hold((got1, mine2))[0]
    mlp = update(moves, [mlp_state], [mine0, got0, mine1, got1], "update_mlp")
    got2, far_got3, total, mlp = hold((got2, far_got3, total, mlp))
    mine3 = sum_far(far_keep3, far_got3)
    got3 = swap(mine3, X)
    total = total + swap(total, X)
    got2 = hold((got2, mine3))[0]
    moves = [(0, (b,), 0, 0, D, b, D, 2 * D) for b in range(2)]
    moves += [(1, (0, 1), 0, D, D, None, 0, 0)]
    both_new = update(
        moves,
        [mlp_state, attn_state],
        [mine2, got2],
        "update_both",
        mlp,
    )
    mlp, attn = both_new[:4], both_new[4:]
    moves = [(0, (b,), 0, 0, 384, b, D, 384) for b in range(2)]
    moves += [(0, (b,), 0, 384, 384, b, 2 * D, 384) for b in range(2)]
    moves += [(0, (0, 1), 0, D, D, None, 3 * D, 0)]
    attn = update(moves, [attn_state], [mine3, got3], "update_attn", attn)
    flat = total.reshape(-1)
    gain_g = lax.dynamic_slice(flat, (96 * f,), (96,))
    offset_g = lax.dynamic_slice(flat, (2 * D + 528 * f,), (528,))

    gains = advance(gain_g, gain_vector, gain_moment, gain_average, rate)
    offsets = advance(offset_g, offset_vector, offset_moment, offset_average, rate)
    return (activations, input_grad, *attn, *mlp, *gains, *offsets)


def solution(mesh):
    placed = (
        P(("rep", "fsdp"), None),
        P(("rep", "fsdp"), None),
        P(("rep", "fsdp")),
        P(("rep", "fsdp")),
        P(("rep", "fsdp")),
        P("fsdp", None),
        P("fsdp", None),
        P("fsdp"),
        P("fsdp"),
        P("fsdp", None),
        P("fsdp", None),
        P("fsdp"),
        P("fsdp"),
        P("fsdp", None),
        P("fsdp", None),
        P("fsdp"),
        P("fsdp"),
    )
    small = mesh.shape["rep"] == 2 and mesh.shape["fsdp"] == 16
    return jax.shard_map(
        fast_device if small else per_device,
        mesh=mesh,
        in_specs=placed,
        out_specs=(
            P(("rep", "fsdp"), None),
            P(("rep", "fsdp"), None),
            P("fsdp", None),
            P("fsdp", None),
            P("fsdp", None),
            P("fsdp", None),
            P("fsdp", None),
            P("fsdp", None),
            P("fsdp", None),
            P("fsdp", None),
            P("fsdp"),
            P("fsdp"),
            P("fsdp"),
            P("fsdp"),
            P("fsdp"),
            P("fsdp"),
            P("fsdp"),
            P("fsdp"),
        ),
        check_vma=False,
    )
```

```python
import functools
import math

import jax
import jax.numpy as jnp
from jax import lax
from jax.experimental import pallas as pl
from jax.experimental.pallas import tpu as pltpu
from jax.sharding import PartitionSpec as P

D = 768
HEADS = 12
HEAD_DIM = 64
FF = 3072
BF = jnp.bfloat16
F32 = jnp.float32


momentum_decay = 0.9
average_decay = 0.8
base_rate = 0.02
norm_eps = 1e-06
mask_fill = -1e30


def normalize(inputs):
    mean_val = jnp.mean(inputs, axis=-1, keepdims=True)
    centred = inputs - mean_val
    variance = jnp.mean(centred * centred, axis=-1, keepdims=True)
    return centred * lax.rsqrt(variance + norm_eps)


def norm_affine(inputs, gain_part, shift_part):
    return normalize(inputs) * gain_part + shift_part


def gelu_exact(inputs):
    return jax.nn.gelu(inputs, approximate=False)


def over_tokens(left_mat, right_mat):
    return lax.dot_general(
        left_mat, right_mat, (((0,), (0,)), ((), ())), preferred_element_type=jnp.float32
    )


def against_rows(left_mat, right_mat):
    return lax.dot_general(
        left_mat, right_mat, (((1,), (1,)), ((), ())), preferred_element_type=jnp.float32
    )


def block_mask(clip_ids, key_ok):
    return (clip_ids[:, None] == clip_ids[None, :]) & (key_ok[None, :] == 1)


def forward(inputs, params, clip_ids, key_ok, masked):
    attn_full = params[0]
    mlp_full = params[1]
    gain_f = params[2].astype(jnp.float32)
    shift_f = params[3].astype(jnp.float32)
    tok_rows = inputs.shape[0]
    score_scale = HEAD_DIM ** (-0.5)
    is_masked = masked[:, None] == 1
    embedded = jnp.where(is_masked, shift_f[6 * D : 7 * D][None, :], inputs)
    normed_one = norm_affine(embedded, gain_f[:D], shift_f[:D]).astype(jnp.bfloat16)
    qkv_bias = jnp.concatenate(
        [shift_f[D : 2 * D], jnp.zeros((D,), jnp.float32), shift_f[2 * D : 3 * D]]
    )
    projected = (
        jnp.dot(normed_one, attn_full[:, : 3 * D], preferred_element_type=jnp.float32) + qkv_bias
    )
    projected = projected.astype(jnp.bfloat16)
    queries = projected[:, :D].reshape(tok_rows, HEADS, HEAD_DIM)
    key_heads = projected[:, D : 2 * D].reshape(tok_rows, HEADS, HEAD_DIM)
    value_heads = projected[:, 2 * D :].reshape(tok_rows, HEADS, HEAD_DIM)
    allowed = block_mask(clip_ids, key_ok)
    scores = (
        jnp.einsum("qhd,khd->hqk", queries, key_heads, preferred_element_type=jnp.float32)
        * score_scale
    )
    scores = jnp.where(allowed[None], scores, mask_fill)
    row_peak = jnp.max(scores, axis=-1, keepdims=True)
    exponent = jnp.exp(scores - row_peak)
    summed = jnp.sum(exponent, axis=-1, keepdims=True)
    attn_prob = (exponent / summed).astype(jnp.bfloat16)
    mixed_parts = jnp.einsum(
        "hqk,khd->qhd", attn_prob, value_heads, preferred_element_type=jnp.float32
    )
    lse_parts = [row_peak + jnp.log(summed)]
    mixed_out = mixed_parts.reshape(tok_rows, D).astype(jnp.bfloat16)
    after_attn = embedded + against_rows(mixed_out, attn_full[:, 3 * D :]) + shift_f[3 * D : 4 * D]
    normed_two = norm_affine(after_attn, gain_f[D:], shift_f[4 * D : 5 * D]).astype(jnp.bfloat16)
    hidden_pre = (
        jnp.dot(normed_two, mlp_full[:, :FF], preferred_element_type=jnp.float32) + shift_f[7 * D :]
    )
    hidden_act = gelu_exact(hidden_pre).astype(jnp.bfloat16)
    output = after_attn + against_rows(hidden_act, mlp_full[:, FF:]) + shift_f[5 * D : 6 * D]
    kept_values = (
        embedded,
        normed_one,
        queries,
        key_heads,
        value_heads,
        lse_parts,
        mixed_out,
        after_attn,
        normed_two,
        hidden_pre,
        hidden_act,
        gain_f,
        shift_f,
    )
    return (output, kept_values)


def backward(cotangent, params, kept_values, clip_ids, key_ok, masked):
    attn_full = params[0]
    mlp_full = params[1]
    (
        embedded,
        normed_one,
        queries,
        key_heads,
        value_heads,
        lse_parts,
        mixed_out,
        after_attn,
        normed_two,
        hidden_pre,
        hidden_act,
        gain_f,
        shift_f,
    ) = kept_values
    tok_rows = cotangent.shape[0]
    score_scale = HEAD_DIM ** (-0.5)
    d_out = cotangent.astype(jnp.float32)
    d_bias_two = jnp.sum(d_out, axis=0)
    d_down = over_tokens(cotangent, hidden_act)
    d_act = jnp.dot(cotangent, mlp_full[:, FF:], preferred_element_type=jnp.float32)
    gelu_value, gelu_pull = jax.vjp(gelu_exact, hidden_pre)
    d_pre_low = gelu_pull(d_act)[0].astype(jnp.bfloat16)
    d_bias_one = jnp.sum(d_pre_low.astype(jnp.float32), axis=0)
    d_up = over_tokens(normed_two, d_pre_low)
    mlp_grad = jnp.concatenate([d_up, d_down], axis=1)
    d_normed_two = against_rows(d_pre_low, mlp_full[:, :FF])
    norm_value, norm_pull = jax.vjp(norm_affine, after_attn, gain_f[D:], shift_f[4 * D : 5 * D])
    d_after_norm, d_gain_two, d_shift_two = norm_pull(d_normed_two)
    d_after = d_out + d_after_norm
    d_after_low = d_after.astype(jnp.bfloat16)
    d_bias_out = jnp.sum(d_after, axis=0)
    d_outproj = over_tokens(d_after_low, mixed_out)
    d_mixed = jnp.dot(d_after_low, attn_full[:, 3 * D :], preferred_element_type=jnp.float32)
    d_mixed_low = d_mixed.astype(jnp.bfloat16).reshape(tok_rows, HEADS, HEAD_DIM)
    block_rows = min(512, tok_rows)
    d_query_parts = []
    d_keys = jnp.zeros((tok_rows, HEADS, HEAD_DIM), jnp.float32)
    d_values = jnp.zeros((tok_rows, HEADS, HEAD_DIM), jnp.float32)
    for block_number, offset in enumerate(range(0, tok_rows, block_rows)):
        allowed = block_mask(clip_ids, key_ok)
        scores = (
            jnp.einsum("qhd,khd->hqk", queries, key_heads, preferred_element_type=jnp.float32)
            * score_scale
        )
        scores = jnp.where(allowed[None], scores, mask_fill)
        attn_prob = jnp.exp(scores - lse_parts[block_number])
        prob_low = attn_prob.astype(jnp.bfloat16)
        d_prob = jnp.einsum(
            "qhd,khd->hqk", d_mixed_low, value_heads, preferred_element_type=jnp.float32
        )
        row_delta = jnp.sum(d_prob * attn_prob, axis=-1, keepdims=True)
        d_scores = (attn_prob * (d_prob - row_delta)).astype(jnp.bfloat16)
        d_query_parts.append(
            jnp.einsum("hqk,khd->qhd", d_scores, key_heads, preferred_element_type=jnp.float32)
            * score_scale
        )
        d_keys = (
            jnp.einsum("hqk,qhd->khd", d_scores, queries, preferred_element_type=jnp.float32)
            * score_scale
        )
        d_values = jnp.einsum(
            "hqk,qhd->khd", prob_low, d_mixed_low, preferred_element_type=jnp.float32
        )
    d_queries = d_query_parts[0]
    d_proj_low = jnp.concatenate(
        [
            d_queries.reshape(tok_rows, D),
            d_keys.reshape(tok_rows, D),
            d_values.reshape(tok_rows, D),
        ],
        axis=1,
    ).astype(jnp.bfloat16)
    d_bias_q = jnp.sum(d_proj_low[:, :D].astype(jnp.float32), axis=0)
    d_bias_v = jnp.sum(d_proj_low[:, 2 * D :].astype(jnp.float32), axis=0)
    d_qkv = over_tokens(normed_one, d_proj_low)
    d_normed_one = against_rows(d_proj_low, attn_full[:, : 3 * D])
    first_value, first_pull = jax.vjp(norm_affine, embedded, gain_f[:D], shift_f[:D])
    d_embed_norm, d_gain_one, d_shift_one = first_pull(d_normed_one)
    d_embedded = d_after + d_embed_norm
    is_masked = masked[:, None] == 1
    d_mask_vec = jnp.sum(jnp.where(is_masked, d_embedded, 0.0), axis=0)
    input_grad = jnp.where(is_masked, 0.0, d_embedded).astype(jnp.bfloat16)
    attn_grad = jnp.concatenate([d_qkv, d_outproj], axis=1)
    gain_grad = jnp.concatenate([d_gain_one, d_gain_two])
    offset_grad = jnp.concatenate(
        [
            d_shift_one,
            d_bias_q,
            d_bias_v,
            d_bias_out,
            d_shift_two,
            d_bias_two,
            d_mask_vec,
            d_bias_one,
        ]
    )
    return (input_grad, (attn_grad, mlp_grad, gain_grad, offset_grad))


def advance(gradient, weight, moment, average, learn_rate):
    moment_new = momentum_decay * moment + gradient
    weight_new = weight - learn_rate * (gradient + momentum_decay * moment_new)
    average_new = average_decay * average + (1.0 - average_decay) * weight_new
    return (weight_new, moment_new, average_new, weight_new.astype(jnp.bfloat16))


def per_device(
    tokens,
    cotangent,
    clip_index,
    key_valid,
    patch_masked,
    attn_weight,
    mlp_weight,
    gain_vector,
    offset_vector,
    attn_moment,
    mlp_moment,
    gain_moment,
    offset_moment,
    attn_average,
    mlp_average,
    gain_average,
    offset_average,
):
    attn_shard = attn_weight.astype(jnp.bfloat16)
    mlp_shard = mlp_weight.astype(jnp.bfloat16)
    gain_shard = gain_vector.astype(jnp.bfloat16)
    offset_shard = offset_vector.astype(jnp.bfloat16)
    params = (
        lax.all_gather(attn_shard, "fsdp", axis=0, tiled=True),
        lax.all_gather(mlp_shard, "fsdp", axis=0, tiled=True),
        lax.all_gather(gain_shard, "fsdp", axis=0, tiled=True),
        lax.all_gather(offset_shard, "fsdp", axis=0, tiled=True),
    )
    inputs = tokens.astype(jnp.float32)
    output, first_kept = forward(inputs, params, clip_index, key_valid, patch_masked)
    again = (
        lax.all_gather(attn_shard, "fsdp", axis=0, tiled=True),
        lax.all_gather(mlp_shard, "fsdp", axis=0, tiled=True),
        lax.all_gather(gain_shard, "fsdp", axis=0, tiled=True),
        lax.all_gather(offset_shard, "fsdp", axis=0, tiled=True),
    )
    output_again, kept_values = forward(inputs, again, clip_index, key_valid, patch_masked)
    input_grad, gradients = backward(
        cotangent, again, kept_values, clip_index, key_valid, patch_masked
    )
    owned = (
        lax.psum_scatter(gradients[0], "fsdp", scatter_dimension=0, tiled=True),
        lax.psum_scatter(gradients[1], "fsdp", scatter_dimension=0, tiled=True),
        lax.psum_scatter(gradients[2], "fsdp", scatter_dimension=0, tiled=True),
        lax.psum_scatter(gradients[3], "fsdp", scatter_dimension=0, tiled=True),
    )
    shares = (
        lax.psum_scatter(
            owned[0].astype(jnp.bfloat16), "rep", scatter_dimension=1, tiled=True
        ).astype(jnp.float32),
        lax.psum_scatter(
            owned[1].astype(jnp.bfloat16), "rep", scatter_dimension=1, tiled=True
        ).astype(jnp.float32),
        lax.psum_scatter(
            owned[2].astype(jnp.bfloat16), "rep", scatter_dimension=0, tiled=True
        ).astype(jnp.float32),
        lax.psum_scatter(
            owned[3].astype(jnp.bfloat16), "rep", scatter_dimension=0, tiled=True
        ).astype(jnp.float32),
    )
    reduced = (
        lax.all_gather(shares[0].astype(jnp.bfloat16), "rep", axis=1, tiled=True).astype(
            jnp.float32
        ),
        lax.all_gather(shares[1].astype(jnp.bfloat16), "rep", axis=1, tiled=True).astype(
            jnp.float32
        ),
        lax.all_gather(shares[2].astype(jnp.bfloat16), "rep", axis=0, tiled=True).astype(
            jnp.float32
        ),
        lax.all_gather(shares[3].astype(jnp.bfloat16), "rep", axis=0, tiled=True).astype(
            jnp.float32
        ),
    )
    learn_rate = base_rate / math.sqrt(
        tokens.shape[0] * lax.axis_size("rep") * lax.axis_size("fsdp")
    )
    attn_new, attn_momentum, attn_ema, attn_copy = advance(
        reduced[0], attn_weight, attn_moment, attn_average, learn_rate
    )
    mlp_new, mlp_momentum, mlp_ema, mlp_copy = advance(
        reduced[1], mlp_weight, mlp_moment, mlp_average, learn_rate
    )
    gain_new, gain_momentum, gain_ema, gain_copy = advance(
        reduced[2], gain_vector, gain_moment, gain_average, learn_rate
    )
    offset_new, offset_momentum, offset_ema, offset_copy = advance(
        reduced[3], offset_vector, offset_moment, offset_average, learn_rate
    )
    return (
        output.astype(jnp.bfloat16),
        input_grad,
        attn_new,
        attn_momentum,
        attn_ema,
        attn_copy,
        mlp_new,
        mlp_momentum,
        mlp_ema,
        mlp_copy,
        gain_new,
        gain_momentum,
        gain_ema,
        gain_copy,
        offset_new,
        offset_momentum,
        offset_ema,
        offset_copy,
    )


class Operand:
    def __init__(self, ref):
        self.ref, self.shape = ref, ref.shape

    def __getitem__(self, index):
        return self.ref[index]


def call(kernel, outs, args, scratch=(), name=None, limit=8, space=pltpu.VMEM):
    def body(co_ref, *refs):
        operands = [Operand(ref) for ref in refs[: len(args) - 1]]
        kernel(co_ref, *operands, *refs[len(args) - 1 :])

    return pl.pallas_call(
        body,
        out_shape=[jax.ShapeDtypeStruct(shape, dtype) for shape, dtype in outs],
        in_specs=[pl.BlockSpec(memory_space=pltpu.SMEM)]
        + [pl.BlockSpec(memory_space=space)] * (len(args) - 1),
        out_specs=[pl.BlockSpec(memory_space=pltpu.VMEM)] * len(outs),
        scratch_shapes=list(scratch),
        compiler_params=pltpu.CompilerParams(vmem_limit_bytes=limit * 2**20),
        cost_estimate=pl.CostEstimate(flops=2**20, bytes_accessed=2**20, transcendentals=0),
        name=name,
    )(*args)


def call_all(co, jobs, name):
    args = [arg for job in jobs for arg in job[2]]
    outs = [out for job in jobs for out in job[1]]

    def body(co_ref, *refs):
        first, last = 0, len(args)
        for kernel, job_outs, job_args in jobs:
            ins = refs[first : first + len(job_args)]
            results = refs[last : last + len(job_outs)]
            kernel(co_ref, *ins, *results)
            first += len(job_args)
            last += len(job_outs)

    return call(body, outs, [co, *args], name=name)


def assemble_kernel(ranges, co, *refs):
    count = len(refs) - len(ranges)
    each = count // 2
    for number in range(count):
        blocks = refs[number].shape[0] // 48
        for block in range(blocks):
            i, k = (number % 2, block) if blocks == 4 else (block // 4, block % 4)
            b = (number // 2) % 2 if each == 4 else 0
            row = k * 192 + lax.bitwise_xor(co[2], i) * 96
            row = row + lax.bitwise_xor(co[3], number // each) * 48
            rows = pl.ds(pl.multiple_of(row, 16), 48)
            for (start, size), out in zip(ranges, refs[count:]):
                out[rows, b * size : b * size + size] = refs[number][
                    block * 48 : block * 48 + 48, start : start + size
                ]


def assemble(co, pieces, *ranges):
    widths = [size * (2 if len(pieces) == 8 else 1) for start, size in ranges]
    return call(
        functools.partial(assemble_kernel, ranges),
        [((D, width), BF) for width in widths],
        [co, *pieces],
        name="assemble",
    )


def lanes(offset, size):
    return pl.ds(pl.multiple_of(offset, 128), size)


def nn(left, right):
    return lax.dot_general(left, right, (((1,), (0,)), ((), ())), preferred_element_type=jnp.float32)


def nt(left, right):
    return lax.dot_general(left, right, (((1,), (1,)), ((), ())), preferred_element_type=jnp.float32)


def whole(weight, start, size):
    return weight[:, start : start + size]


def row_norm(values):
    mean = jnp.mean(values, axis=-1, keepdims=True)
    centred = values - mean
    var = jnp.mean(centred * centred, axis=-1, keepdims=True)
    rstd = lax.rsqrt(var + norm_eps)
    return centred * rstd, rstd


def prep_first_kernel(co, attn, mlp, s0, wide, sems):
    r = co[0]
    sources = [attn.ref.at[:, lanes(part * D + 384 * r, 384)] for part in range(4)]
    sources += [mlp.ref.at[:, lanes(1536 * r + n * 384, 384)] for n in range(2)]
    copies = [
        pltpu.make_async_copy(source, wide.at[n], sems.at[n]) for n, source in enumerate(sources)
    ]
    for copy in copies:
        copy.start()
    for n, copy in enumerate(copies):
        copy.wait()
        s0[:, n * 384 : n * 384 + 384] = wide[n].astype(BF)


def prep_second_kernel(co, mlp, s1, s2):
    r = co[0]
    for b in range(2):
        half = lax.bitwise_xor(r, b)
        s1[:, b * D : b * D + D] = mlp[:, lanes(1536 * half + D, D)].astype(BF)
        s2[:, b * D : b * D + D] = mlp[:, lanes(FF + 1536 * half + D, D)].astype(BF)
    s1[:, 2 * D :] = mlp[:, lanes(FF + 1536 * r, D)].astype(BF)


def turn(co, values, scratch, send, keep):
    scratch[...] = values.T
    for out, core in ((send, 1 - co[3]), (keep, co[3])):
        for block in range(8):
            row = pl.multiple_of(block * 96 + 48 * core, 16)
            out[block * 48 : block * 48 + 48, :] = scratch[pl.ds(row, 48), :].astype(BF)


def first_norm_kernel(co, tokens, info, vec, h1, h1t_send, h1t_keep, cols, scratch):
    turned = jnp.transpose(info[...])
    cols[:, 0:8] = turned
    x0 = jnp.where(turned[:, 2:3] == 1.0, vec[8:9, :], tokens[...].astype(F32))
    xh, rstd = row_norm(x0)
    h = xh * vec[0:1, :] + vec[2:3, :]
    h1[...] = h.astype(BF)
    turn(co, h, scratch, h1t_send, h1t_keep)


def allowed_pairs(info, cols):
    return (cols[:, 0:1] == info[0:1, :]) & (cols[:, 1:2] == 1.0)


def attention_kernel(co, h1, vec, info, cols, weight, qkv, att, lse):
    for b in range(2):
        half = lax.bitwise_xor(co[0], b)
        for part in range(3):
            out = nn(h1[...], whole(weight, b * 1152 + part * 384, 384))
            if part != 1:
                row = 3 if part == 0 else 4
                out = out + vec.ref[row : row + 1, lanes(384 * half, 384)]
            qkv[:, b * 1152 + part * 384 : b * 1152 + part * 384 + 384] = out.astype(BF)
    allowed = allowed_pairs(info, cols)
    low = lax.broadcasted_iota(jnp.int32, (256, 128), 1) < 64
    for pair in range(6):
        base = (pair // 3) * 1152 + (pair % 3) * 128
        q2 = qkv[:, base : base + 128]
        k2 = qkv[:, base + 384 : base + 512]
        v2 = qkv[:, base + 768 : base + 896]
        mixed = []
        for side in range(2):
            qm = jnp.where(low if side == 0 else ~low, q2, jnp.zeros_like(q2))
            s = jnp.where(allowed, nt(k2, qm) * 0.125, mask_fill)
            peak = jnp.max(s, axis=0, keepdims=True)
            e = jnp.exp(s - peak)
            total = jnp.sum(e, axis=0, keepdims=True)
            prob = (e * (1.0 / total)).astype(BF)
            lse[2 * pair + side : 2 * pair + side + 1, :] = peak + jnp.log(total)
            mixed.append(over_tokens(prob, v2))
        att[:, pair * 128 : pair * 128 + 128] = jnp.where(low, mixed[0], mixed[1]).astype(BF)


def second_norm_kernel(
    co, tokens, cols, vec, att, weight, dz, y1, h2, h2t_send, h2t_keep, dzt_send, dzt_keep, scratch
):
    x0 = jnp.where(cols[:, 2:3] == 1.0, vec[8:9, :], tokens[...].astype(F32))
    y = x0 + nt(att[...], whole(weight, 0, D)) + vec[5:6, :]
    y1[...] = y
    xh, rstd = row_norm(y)
    h = xh * vec[1:2, :] + vec[6:7, :]
    h2[...] = h.astype(BF)
    turn(co, h, scratch, h2t_send, h2t_keep)
    turn(co, dz[...].astype(F32), scratch, dzt_send, dzt_keep)


def hidden_kernel(
    co, h2, vec, dzt_send, dzt_keep, w0, w1, g0, g1, slope0, slope1, send, keep
):
    for part, weight, g, slope in ((0, w0, g0, slope0), (1, w1, g1, slope1)):
        for b in range(2):
            half = lax.bitwise_xor(co[0], b)
            for sub in range(0, D, 384):
                at = slice(b * D + sub, b * D + sub + 384)
                u = nn(h2[...], weight[:, at])
                u = u + vec[pl.ds(9 + 2 * half + part, 1), sub : sub + 384]
                phi = 0.5 * (1.0 + lax.erf(u * math.sqrt(0.5)))
                act = (u * phi).astype(BF)
                g[:, at] = act
                slope[:, at] = phi + u * (
                    jnp.exp(-0.5 * u * u) * (1.0 / math.sqrt(2.0 * math.pi))
                )
                dst = lanes(half * D + sub, 384) if part == 0 else lanes((2 + b) * D + sub, 384)
                share_rows(dzt_send, dzt_keep, act, send, keep, dst)


def hidden_grad_kernel(
    co,
    dz,
    slope0,
    slope1,
    w00,
    w01,
    w10,
    w11,
    left_send,
    left_keep,
    du0,
    du1,
    db1,
    send,
    keep,
):
    for part, slope, du in ((0, slope0, du0), (1, slope1, du1)):
        for b in range(2):
            weight = ((w00, w01), (w10, w11))[b][part]
            half = lax.bitwise_xor(co[0], b)
            for sub in range(0, D, 384):
                at = slice(b * D + sub, b * D + sub + 384)
                da = nn(dz[...], weight[:, sub : sub + 384])
                d = (da * slope[:, at]).astype(BF)
                du[:, at] = d
                db1[pl.ds(2 * half + part, 1), sub : sub + 384] = jnp.sum(
                    d.astype(F32), axis=0, keepdims=True
                )
                dst = lanes(half * D + sub, 384) if part == 0 else lanes((2 + b) * D + sub, 384)
                share_rows(left_send, left_keep, d, send, keep, dst)


def output_kernel(co, y1, vec, g0, g1, w00, w01, w10, w11, act):
    acc = y1[...] + vec[7:8, :]
    for part, g in ((0, g0), (1, g1)):
        acc = acc + nt(g[:, :D], (w00, w01)[part][...])
        acc = acc + nt(g[:, D:], (w10, w11)[part][...])
    act[...] = acc.astype(BF)


def share_rows(left_send, left_keep, right, send, keep, dst):
    send[:, dst] = nn(left_send[...], right).astype(BF)
    keep[:, dst] = nn(left_keep[...], right)


def attention_grad_kernel(
    co, h1t_send, h1t_keep, dqkv, dpt_send, dpt_keep, att, send, keep
):
    first, second = (h1t_send, h1t_keep), (dpt_send, dpt_keep)
    moves = [(first, dqkv, b * 1152 + 384 + n * 384, b * D + n * 384) for b in (0, 1) for n in (0, 1)]
    for b in range(2):
        place = 384 * lax.bitwise_xor(co[0], b)
        moves.append((first, dqkv, b * 1152, 2 * D + place))
        moves.append((second, att, b * 384, 3 * D + place))
    for left, right, src, dst in moves:
        share_rows(*left, right[:, src : src + 384], send, keep, lanes(dst, 384))


def second_back_kernel(
    co, dz, y1, vec, du0, du1, w0, w1, weight_o, dy1, datt, dpt_send, dpt_keep, small, scratch
):
    yh, rstd = row_norm(y1[...])
    dy = dz[...].astype(F32)
    dh = nt(du0[...], whole(w0, 0, 2 * D)) + nt(du1[...], whole(w1, 0, 2 * D))
    small[0:1, :] = jnp.sum(dh * yh, axis=0, keepdims=True)
    small[1:2, :] = jnp.sum(dh, axis=0, keepdims=True)
    small[3:4, :] = jnp.sum(dy, axis=0, keepdims=True)
    e = dh * vec[1:2, :]
    d = dy + rstd * (
        e - jnp.mean(e, axis=-1, keepdims=True) - yh * jnp.mean(e * yh, axis=-1, keepdims=True)
    )
    dy1[...] = d
    small[2:3, :] = jnp.sum(d, axis=0, keepdims=True)
    turn(co, d, scratch, dpt_send, dpt_keep)
    datt[...] = nn(d.astype(BF), whole(weight_o, 0, D)).astype(BF)


def attention_back_kernel(co, info, cols, lse, qkv, datt, dqkv, small):
    allowed = allowed_pairs(info, cols)
    low = lax.broadcasted_iota(jnp.int32, (256, 128), 1) < 64
    for pair in range(6):
        half = lax.bitwise_xor(co[0], pair // 3)
        base = (pair // 3) * 1152 + (pair % 3) * 128
        q2 = qkv[:, base : base + 128]
        k2 = qkv[:, base + 384 : base + 512]
        v2 = qkv[:, base + 768 : base + 896]
        o2 = datt[:, pair * 128 : pair * 128 + 128]
        dqs, dks, dvs = [], [], []
        for side in range(2):
            mine = low if side == 0 else ~low
            qm = jnp.where(mine, q2, jnp.zeros_like(q2))
            om = jnp.where(mine, o2, jnp.zeros_like(o2))
            s = jnp.where(allowed, nt(k2, qm) * 0.125, mask_fill)
            prob = jnp.exp(s - lse[2 * pair + side : 2 * pair + side + 1, :])
            dprob = nt(v2, om)
            delta = jnp.sum(dprob * prob, axis=0, keepdims=True)
            ds = (prob * (dprob - delta)).astype(BF)
            dqs.append(over_tokens(ds, k2))
            dks.append(nn(ds, q2))
            dvs.append(nn(prob.astype(BF), o2))
        dq = (jnp.where(low, dqs[0], dqs[1]) * 0.125).astype(BF)
        dk = (jnp.where(low, dks[0], dks[1]) * 0.125).astype(BF)
        dv = jnp.where(low, dvs[0], dvs[1]).astype(BF)
        dqkv[:, base : base + 128] = dq
        dqkv[:, base + 384 : base + 512] = dk
        dqkv[:, base + 768 : base + 896] = dv
        place = lanes(384 * half + (pair % 3) * 128, 128)
        small[0:1, place] = jnp.sum(dq.astype(F32), axis=0, keepdims=True)
        small[1:2, place] = jnp.sum(dv.astype(F32), axis=0, keepdims=True)


def first_back_kernel(
    co, dqkv, tokens, cols, vec, dy1, db1, small2, small_a, weight, input_grad, total
):
    hidden = cols[:, 2:3] == 1.0
    x0 = jnp.where(hidden, vec[8:9, :], tokens[...].astype(F32))
    xh, rstd = row_norm(x0)
    dh = nt(dqkv[...], whole(weight, 0, 3 * D))
    e = dh * vec[0:1, :]
    dx = dy1[...] + rstd * (
        e - jnp.mean(e, axis=-1, keepdims=True) - xh * jnp.mean(e * xh, axis=-1, keepdims=True)
    )
    input_grad[...] = jnp.where(hidden, 0.0, dx).astype(BF)
    total[0:1, :] = jnp.sum(dh * xh, axis=0, keepdims=True)
    total[1:2, :] = small2[0:1, :]
    total[2:3, :] = jnp.sum(dh, axis=0, keepdims=True)
    total[3:5, :] = small_a[0:2, :]
    total[5:6, :] = small2[2:3, :]
    total[6:7, :] = small2[1:2, :]
    total[7:8, :] = small2[3:4, :]
    total[8:9, :] = jnp.sum(jnp.where(hidden, dx, 0.0), axis=0, keepdims=True)
    total[9:13, :] = db1[0:4, :]
    total[13:16, :] = jnp.zeros((3, D), F32)


def both(keep, got, *at):
    return keep[at] + got[at].astype(F32)


def split_first_kernel(co, keep, got, y_send, y_keep, x_send, x_keep):
    y = co[2]
    every = slice(None)
    for k in range(4):
        for out, i in ((y_send, 1 - y), (y_keep, y)):
            out[k * 48 : k * 48 + 48, :] = both(keep, got, k, i, every, slice(0, 2 * D)).astype(
                out.dtype
            )
    x_keep[...] = both(keep, got, every, every, every, slice(2 * D, 3 * D))
    x_send[...] = both(keep, got, every, every, every, slice(3 * D, 4 * D)).astype(BF)


def split_second_kernel(co, x_keep, x_got, keep, got, y_send, y_keep, x_send, x_next):
    y = co[2]
    every = slice(None)
    for k in range(4):
        rows = slice(k * 48, k * 48 + 48)
        for out, i in ((y_send, 1 - y), (y_keep, y)):
            out[rows, :D] = both(x_keep, x_got, k, i).astype(out.dtype)
            out[rows, D:] = both(keep, got, k, i, every, slice(0, D)).astype(out.dtype)
    x_next[...] = both(keep, got, every, every, every, slice(2 * D, 3 * D))
    x_send[...] = both(keep, got, every, every, every, slice(3 * D, 4 * D)).astype(BF)


def split_third_kernel(co, x_keep, x_got, keep, got, y_send, y_keep, x_send, x_next, last):
    y = co[2]
    every = slice(None)
    for k in range(4):
        rows = slice(k * 48, k * 48 + 48)
        for out, i in ((y_send, 1 - y), (y_keep, y)):
            out[rows, :D] = both(x_keep, x_got, k, i).astype(out.dtype)
            out[rows, D:] = both(keep, got, k, i, every, slice(2 * D, 3 * D)).astype(out.dtype)
    x_next[...] = both(keep, got, every, every, every, slice(0, D))
    x_send[...] = both(keep, got, every, every, every, slice(D, 2 * D)).astype(BF)
    last[...] = both(keep, got, every, every, every, slice(3 * D, 4 * D))


def split_fourth_kernel(co, x_keep, x_got, last, far_keep, far_got, y_send, y_keep):
    y = co[2]
    for out, i in ((y_send, 1 - y), (y_keep, y)):
        for k in range(4):
            rows = slice(k * 48, k * 48 + 48)
            out[rows, :D] = both(x_keep, x_got, k, i).astype(out.dtype)
            out[rows, D:] = last[k, i].astype(out.dtype)
        row = pl.multiple_of(96 + i * 48, 16)
        block = both(far_keep, far_got, pl.ds(row, 48)).astype(out.dtype)
        out[192:224, :D] = block[:32]
        out[192:208, D:] = block[32:]
        out[208:224, D:] = jnp.zeros((16, D), out.dtype)


def split_near_first_kernel(co, keep, got, up_keep, up_got, send, rest):
    side = co[1] % 2
    for out, at in ((send, 1 - side), (rest, side)):
        for far in range(2):
            row = pl.multiple_of((2 * far + at) * 48, 16)
            for half in range(2):
                to = half * 96 + far * 48
                cols = slice(half * D, half * D + D)
                out[to : to + 48, :] = both(keep, got, pl.ds(row, 48), cols).astype(out.dtype)
                to = 192 + far * 96 + half * 48
                total = both(up_keep, up_got, 2 * far + at, half, slice(None), slice(D, 2 * D))
                out[to : to + 48, :] = total.astype(out.dtype)


def split_far_first_kernel(co, keep, got, send, rest):
    side = co[1] // 2
    for out, at in ((send, 1 - side), (rest, side)):
        for half in range(2):
            row = pl.multiple_of(half * 96 + at * 48, 16)
            to = half * 48
            out[to : to + 48, :] = both(keep, got, pl.ds(row, 48)).astype(out.dtype)
        row = pl.multiple_of(192 + at * 96, 16)
        out[96:192, :] = both(keep, got, pl.ds(row, 96)).astype(out.dtype)


def sum_far_first_kernel(co, keep, got, out):
    for half in range(2):
        rows = slice(half * 48, half * 48 + 48)
        out[:, half * D : half * D + D] = both(keep, got, rows).astype(BF)


def sum_far_second_kernel(co, keep, got, other, out):
    out[:, : 2 * D] = both(keep, got, slice(None)).astype(BF)
    out[:, 2 * D :] = other[...].astype(BF)


def split_near_kernel(co, keep, got, send, rest, *small):
    side = co[1] % 2
    for out, at in ((send, 1 - side), (rest, side)):
        for far in range(2):
            row = pl.multiple_of((2 * far + at) * 48, 16)
            out[far * 48 : far * 48 + 48, :] = both(keep, got, pl.ds(row, 48)).astype(out.dtype)
    if small:
        small[0][0:32, :] = both(keep, got, slice(192, 224), slice(0, D))
        small[0][32:48, :] = both(keep, got, slice(192, 208), slice(D, 2 * D))


def split_far_kernel(co, keep, got, send, rest):
    side = co[1] // 2
    for out, at in ((send, 1 - side), (rest, side)):
        row = pl.multiple_of(at * 48, 16)
        out[...] = both(keep, got, pl.ds(row, 48)).astype(out.dtype)


def sum_far_kernel(co, keep, got, out):
    out[...] = (keep[...] + got[...].astype(F32)).astype(BF)


def update_kernel(rate, moves, n_states, n_grads, n_before, co, *refs):
    grads = refs[3 * n_states :][:n_grads]
    first = 3 * n_states + n_grads + n_before
    parts, sems = refs[first + 4 * n_states : -1], refs[-1]
    copies = []
    for n, (which, numbers, row, src, size, b, col, stride) in enumerate(moves):
        state, new = refs[3 * which :][:3], refs[first + 4 * which :][:4]
        grad = 0.0
        for number in numbers:
            grad = grad + grads[number][row : row + 48, src : src + size].astype(F32)
        place = col if b is None else col + stride * lax.bitwise_xor(co[0], b)
        at = lanes(place, size)
        w, m, a = (ref[:, at] for ref in state)
        m_new = momentum_decay * m + grad
        w_new = w - rate * (grad + momentum_decay * m_new)
        full, low = parts[2 * n], parts[2 * n + 1]
        full[0] = w_new
        full[1] = m_new
        full[2] = average_decay * a + (1.0 - average_decay) * w_new
        low[...] = w_new.astype(BF)
        for k in range(4):
            source = full.at[k] if k < 3 else low
            copy = pltpu.make_async_copy(source, new[k].at[:, at], sems.at[4 * n + k])
            copy.start()
            copies.append(copy)
    for copy in copies:
        copy.wait()


def hold(arrays):
    return lax.optimization_barrier(arrays)


def fast_device(
    tokens,
    cotangent,
    clip_index,
    key_valid,
    patch_masked,
    attn_weight,
    mlp_weight,
    gain_vector,
    offset_vector,
    attn_moment,
    mlp_moment,
    gain_moment,
    offset_moment,
    attn_average,
    mlp_average,
    gain_average,
    offset_average,
):
    r, f = lax.axis_index("rep"), lax.axis_index("fsdp")
    co = jnp.stack([r, f // 4, (f // 2) % 2, f % 2]).astype(jnp.int32)

    def swap(array, mask):
        return lax.ppermute(array, ("rep", "fsdp"), [(i, i ^ mask) for i in range(32)])

    CORE, Y, Z, X = 1, 2, 4, 16

    (s0,) = call(
        prep_first_kernel,
        [((48, 3 * D), BF)],
        [co, attn_weight, mlp_weight],
        scratch=[pltpu.VMEM((6, 48, 384), F32), pltpu.SemaphoreType.DMA((6,))],
        name="prep",
        limit=60,
        space=pltpu.HBM,
    )
    info = jnp.zeros((8, 256), F32).at[0:3].set(
        jnp.stack([clip_index, key_valid, patch_masked]).astype(F32)
    )
    flat = jnp.zeros((16 * D,), F32)
    flat = lax.dynamic_update_slice(flat, gain_vector.astype(BF).astype(F32), (96 * f,))
    flat = lax.dynamic_update_slice(flat, offset_vector.astype(BF).astype(F32), (2 * D + 528 * f,))
    vec = flat.reshape(16, D)

    groups = [[4 * z + at for z in range(4)] for at in range(4)]

    def along_z(shard):
        return lax.all_gather(shard, "fsdp", axis=0, tiled=True, axis_index_groups=groups)

    def core_pair(pieces):
        return pieces + [swap(piece, CORE) for piece in pieces]

    stack0 = along_z(s0)
    stack0, vec, mlp_late = hold((stack0, vec, mlp_weight))
    s1, s2 = call(
        prep_second_kernel,
        [((48, 3 * D), BF), ((48, 2 * D), BF)],
        [co, mlp_late],
        name="prep",
    )
    across0 = swap(stack0, Y)
    far0 = swap(stack0, X)
    vec = vec + swap(vec, CORE)
    s1, vec = hold((s1, vec))
    near0 = [swap(stack0, CORE)]
    stack1 = along_z(s1)
    vec = vec + swap(vec, Y)
    stack1, across0, far0, near0, s2, vec = hold((stack1, across0, far0, near0, s2, vec))
    far_across0 = swap(across0, X)
    across1 = swap(stack1, Y)
    near0 += [swap(across0, CORE), swap(far0, CORE)]
    vec = vec + swap(vec, Z)
    s2, vec = hold((s2, vec))
    stack2 = along_z(s2)
    vec = vec + swap(vec, 2 * Z)
    stack2, across1, far_across0, near0, vec = hold((stack2, across1, far_across0, near0, vec))
    pieces0 = [stack0, across0, far0, far_across0, *near0, swap(far_across0, CORE)]
    across2 = swap(stack2, Y)
    far1 = swap(jnp.concatenate([stack1[:, 2 * D :], across1[:, 2 * D :]], axis=0), X)
    pieces1 = core_pair([stack1, across1])
    halves_t = [((384, 256), BF)] * 2
    h1, h1t_send, h1t_keep, cols = call(
        first_norm_kernel,
        [((256, D), BF), *halves_t, ((256, 128), F32)],
        [co, tokens, info, vec],
        scratch=[pltpu.VMEM((D, 256), F32)],
        name="norm1",
    )
    (w_qkv,) = assemble(co, pieces0, (0, 1152))
    qkv, att, lse = call(
        attention_kernel,
        [((256, 3 * D), BF), ((256, D), BF), ((16, 256), F32)],
        [co, h1, vec, info, cols, w_qkv],
        name="attention",
    )
    w_out, w_up0 = assemble(co, pieces0, (1152, 384), (1536, 768))
    w_up1, w_down00 = assemble(co, pieces1, (0, 1536), (1536, 768))

    y1, h2, h2t_send, h2t_keep, dzt_send, dzt_keep = call(
        second_norm_kernel,
        [((256, D), F32), ((256, D), BF), *halves_t, *halves_t],
        [co, tokens, cols, vec, att, w_out, cotangent],
        scratch=[pltpu.VMEM((D, 256), F32)],
        name="norm2",
    )
    shares = [((384, 4 * D), BF), ((384, 4 * D), F32)]
    g0, g1, slope0, slope1, down_send, down_keep = call(
        hidden_kernel,
        [((256, 2 * D), BF)] * 2 + [((256, 2 * D), F32)] * 2 + shares,
        [co, h2, vec, dzt_send, dzt_keep, w_up0, w_up1],
        name="hidden",
    )

    def blocks(array):
        return array.reshape(4, 2, 48, -1)

    rate = base_rate / math.sqrt(tokens.shape[0] * 32)

    def update(moves, states, grads, name, before=()):
        parts, outs = [], []
        for move in moves:
            parts += [pltpu.VMEM((3, 48, move[4]), F32), pltpu.VMEM((48, move[4]), BF)]
        for state in states:
            outs += [jax.ShapeDtypeStruct(state[0].shape, F32)] * 3
            outs += [jax.ShapeDtypeStruct(state[0].shape, BF)]
        whole = pl.BlockSpec(memory_space=pltpu.VMEM)
        far = pl.BlockSpec(memory_space=pltpu.HBM)
        first = 1 + 3 * len(states) + len(grads)
        return pl.pallas_call(
            functools.partial(update_kernel, rate, moves, len(states), len(grads), len(before)),
            out_shape=outs,
            in_specs=[pl.BlockSpec(memory_space=pltpu.SMEM)]
            + [whole] * (first - 1)
            + [far] * len(before),
            out_specs=[far] * len(outs),
            input_output_aliases={first + k: k for k in range(len(before))},
            scratch_shapes=[*parts, pltpu.SemaphoreType.DMA((4 * len(moves),))],
            compiler_params=pltpu.CompilerParams(vmem_limit_bytes=8 * 2**20),
            cost_estimate=pl.CostEstimate(flops=2**20, bytes_accessed=2**20, transcendentals=0),
            name=name,
        )(co, *(array for state in states for array in state), *grads, *before)

    mlp_state = [mlp_weight, mlp_moment, mlp_average]
    attn_state = [attn_weight, attn_moment, attn_average]

    across2, far1, down_send = hold((across2, far1, down_send))
    pieces2 = core_pair([stack2, across2])
    far1 = core_pair([far1])
    pieces2, far1, down_send = hold((pieces2, far1, down_send))
    down_got = blocks(swap(down_send, CORE))
    down_keep = blocks(down_keep)
    w_down01, w_down11 = assemble(co, pieces2, (0, D), (D, D))
    (w_down10,) = assemble(co, far1, (0, D))
    du0, du1, db1, up_send, up_keep = call(
        hidden_grad_kernel,
        [((256, 2 * D), BF), ((256, 2 * D), BF), ((8, D), F32)] + shares,
        [co, cotangent, slope0, slope1, w_down00, w_down01, w_down10, w_down11, h2t_send, h2t_keep],
        name="hidden_grad",
    )
    down_got, up_send = hold((down_got, up_send))
    y_shares = [((192, 2 * D), BF), ((192, 2 * D), F32)]
    x_shares = [((4, 2, 48, D), BF), ((4, 2, 48, D), F32)]
    y_send0, y_keep0, x_send1, x_keep1 = call(
        split_first_kernel, y_shares + x_shares, [co, down_keep, down_got], name="split_first"
    )
    y_send0, x_send1, up_send, du0 = hold((y_send0, x_send1, up_send, du0))
    y_got0 = swap(y_send0, Y)
    x_got1 = swap(x_send1, X)
    up_got = blocks(swap(up_send, CORE))
    up_keep = blocks(up_keep)
    dy1, datt, dpt_send, dpt_keep, small2 = call(
        second_back_kernel,
        [((256, D), F32), ((256, D), BF), *halves_t, ((8, D), F32)],
        [co, cotangent, y1, vec, du0, du1, w_up0, w_up1, w_out],
        scratch=[pltpu.VMEM((D, 256), F32)],
        name="norm2_back",
    )
    dqkv, small_a = call(
        attention_back_kernel,
        [((256, 3 * D), BF), ((8, D), F32)],
        [co, info, cols, lse, qkv, datt],
        name="attention_back",
    )
    attn_send, attn_keep = call(
        attention_grad_kernel,
        shares,
        [co, h1t_send, h1t_keep, dqkv, dpt_send, dpt_keep, att],
        name="attention_grad",
    )

    def split_near(keep, got, small=()):
        width = keep.shape[1]
        return call(
            split_near_kernel,
            [((96, width), BF), ((96, width), F32), *small],
            [co, keep, got],
            name="split_near",
        )

    def split_far(keep, got):
        width = keep.shape[1]
        return call(
            split_far_kernel,
            [((48, width), BF), ((48, width), F32)],
            [co, keep, got],
            name="split_far",
        )

    def sum_far(keep, got):
        return call(sum_far_kernel, [(keep.shape, BF)], [co, keep, got], name="sum_far")[0]

    def near_job(keep, got, small=()):
        width = keep.shape[1]
        return split_near_kernel, [((96, width), BF), ((96, width), F32), *small], [keep, got]

    def far_job(keep, got):
        width = keep.shape[1]
        return split_far_kernel, [((48, width), BF), ((48, width), F32)], [keep, got]

    def sum_job(keep, got):
        return sum_far_kernel, [(keep.shape, BF)], [keep, got]

    y_got0, x_got1, up_got, attn_send = hold((y_got0, x_got1, up_got, attn_send))
    y_send1, y_keep1, x_send2, x_keep2, near_send0, near_keep0 = call_all(
        co,
        [
            (split_second_kernel, y_shares + x_shares, [x_keep1, x_got1, up_keep, up_got]),
            (
                split_near_first_kernel,
                [((384, D), BF), ((384, D), F32)],
                [y_keep0, y_got0, up_keep, up_got],
            ),
        ],
        "split_third_round",
    )
    dqkv = hold((dqkv, near_send0))[0]
    y_got1 = swap(y_send1, Y)
    x_got2 = swap(x_send2, X)
    near_got0 = swap(near_send0, Z)
    attn_got = blocks(swap(attn_send, CORE))
    attn_keep = blocks(attn_keep)
    input_grad, total = call(
        first_back_kernel,
        [((256, D), BF), ((16, D), F32)],
        [co, dqkv, tokens, cols, vec, dy1, db1, small2, small_a, w_qkv],
        name="norm1_back",
    )
    near_got0, y_got1, x_got2, attn_got, total = hold(
        (near_got0, y_got1, x_got2, attn_got, total)
    )
    far_send0, far_keep0 = call(
        split_far_first_kernel,
        [((192, D), BF), ((192, D), F32)],
        [co, near_keep0, near_got0],
        name="split_far",
    )
    x_got2 = hold((x_got2, far_send0))[0]
    y_send2, y_keep2, x_send3, x_keep3, last = call(
        split_third_kernel,
        y_shares + x_shares + x_shares[1:],
        [co, x_keep2, x_got2, attn_keep, attn_got],
        name="split_third",
    )
    y_got1 = hold((y_got1, y_send2))[0]
    near_send1, near_keep1 = split_near(y_keep1, y_got1)
    y1 = hold((y1, near_send1))[0]
    x_got3 = swap(x_send3, X)
    y_got2 = swap(y_send2, Y)
    near_got1 = swap(near_send1, Z)
    far_got0 = swap(far_send0, 2 * Z)
    total = total + swap(total, CORE)
    (activations,) = call(
        output_kernel,
        [((256, D), BF)],
        [co, y1, vec, g0, g1, w_down00, w_down01, w_down10, w_down11],
        name="output",
    )
    far_got0, near_got1, y_got2, x_got3, total, activations = hold(
        (far_got0, near_got1, y_got2, x_got3, total, activations)
    )
    y_send3, y_keep3 = call(
        split_fourth_kernel,
        [((224, 2 * D), BF), ((224, 2 * D), F32)],
        [co, x_keep3, x_got3, last, far_keep0, far_got0],
        name="split_fourth",
    )
    y_got2 = hold((y_got2, y_send3))[0]
    near_send2, near_keep2 = split_near(y_keep2, y_got2)
    near_got1 = hold((near_got1, near_send2))[0]
    far_send1, far_keep1 = split_far(near_keep1, near_got1)
    far_got0 = hold((far_got0, far_send1))[0]
    (mine0,) = call(
        sum_far_first_kernel, [((48, 2 * D), BF)], [co, far_keep0, far_got0], name="sum_far"
    )
    y_got3 = swap(y_send3, Y)
    near_got2 = swap(near_send2, Z)
    far_got1 = swap(far_send1, 2 * Z)
    got0 = swap(mine0, X)
    total = total + swap(total, 2 * Z)
    got0, far_got1, near_got2, y_got3, total = hold(
        (got0, far_got1, near_got2, y_got3, total)
    )
    near_send3, near_keep3, other, far_send2, far_keep2 = call_all(
        co,
        [near_job(y_keep3, y_got3, [((48, D), F32)]), far_job(near_keep2, near_got2)],
        "split_sixth_round",
    )
    (mine1,) = call(
        sum_far_second_kernel,
        [((48, 3 * D), BF)],
        [co, far_keep1, far_got1, other],
        name="sum_far",
    )
    near_got3 = swap(near_send3, Z)
    far_got2 = swap(far_send2, 2 * Z)
    got1 = swap(mine1, X)
    total = total + swap(total, Z)
    got1, far_got2, near_got3, total = hold((got1, far_got2, near_got3, total))
    far_send3, far_keep3 = split_far(near_keep3, near_got3)
    far_got2 = hold((far_got2, far_send3))[0]
    mine2 = sum_far(far_keep2, far_got2)
    far_got3 = swap(far_send3, 2 * Z)
    got2 = swap(mine2, X)
    total = total + swap(total, Y)
    moves = [(0, (0, 1), 0, h * D, D, None, FF + h * 2 * D, 0) for h in range(2)]
    moves += [(0, (2 + b,), 0, 0, D, b, FF + D, 2 * D) for b in range(2)]
    moves += [(0, (2, 3), 0, D + h * D, D, None, h * 2 * D, 0) for h in range(2)]
    got1 = hold((got1, mine2))[0]
    mlp = update(moves, [mlp_state], [mine0, got0, mine1, got1], "update_mlp")
    got2, far_got3, total, mlp = hold((got2, far_got3, total, mlp))
    mine3 = sum_far(far_keep3, far_got3)
    got3 = swap(mine3, X)
    total = total + swap(total, X)
    got2 = hold((got2, mine3))[0]
    moves = [(0, (b,), 0, 0, D, b, D, 2 * D) for b in range(2)]
    moves += [(1, (0, 1), 0, D, D, None, 0, 0)]
    both_new = update(
        moves,
        [mlp_state, attn_state],
        [mine2, got2],
        "update_both",
        mlp,
    )
    mlp, attn = both_new[:4], both_new[4:]
    moves = [(0, (b,), 0, 0, 384, b, D, 384) for b in range(2)]
    moves += [(0, (b,), 0, 384, 384, b, 2 * D, 384) for b in range(2)]
    moves += [(0, (0, 1), 0, D, D, None, 3 * D, 0)]
    attn = update(moves, [attn_state], [mine3, got3], "update_attn", attn)
    flat = total.reshape(-1)
    gain_g = lax.dynamic_slice(flat, (96 * f,), (96,))
    offset_g = lax.dynamic_slice(flat, (2 * D + 528 * f,), (528,))

    gains = advance(gain_g, gain_vector, gain_moment, gain_average, rate)
    offsets = advance(offset_g, offset_vector, offset_moment, offset_average, rate)
    return (activations, input_grad, *attn, *mlp, *gains, *offsets)


def solution(mesh):
    placed = (
        P(("rep", "fsdp"), None),
        P(("rep", "fsdp"), None),
        P(("rep", "fsdp")),
        P(("rep", "fsdp")),
        P(("rep", "fsdp")),
        P("fsdp", None),
        P("fsdp", None),
        P("fsdp"),
        P("fsdp"),
        P("fsdp", None),
        P("fsdp", None),
        P("fsdp"),
        P("fsdp"),
        P("fsdp", None),
        P("fsdp", None),
        P("fsdp"),
        P("fsdp"),
    )
    small = mesh.shape["rep"] == 2 and mesh.shape["fsdp"] == 16
    return jax.shard_map(
        fast_device if small else per_device,
        mesh=mesh,
        in_specs=placed,
        out_specs=(
            P(("rep", "fsdp"), None),
            P(("rep", "fsdp"), None),
            P("fsdp", None),
            P("fsdp", None),
            P("fsdp", None),
            P("fsdp", None),
            P("fsdp", None),
            P("fsdp", None),
            P("fsdp", None),
            P("fsdp", None),
            P("fsdp"),
            P("fsdp"),
            P("fsdp"),
            P("fsdp"),
            P("fsdp"),
            P("fsdp"),
            P("fsdp"),
            P("fsdp"),
        ),
        check_vma=False,
    )
```

```python
import functools
import math

import jax
import jax.numpy as jnp
from jax import lax
from jax.experimental import pallas as pl
from jax.experimental.pallas import tpu as pltpu
from jax.sharding import PartitionSpec as P

D = 768
HEADS = 12
HEAD_DIM = 64
FF = 3072
BF = jnp.bfloat16
F32 = jnp.float32


momentum_decay = 0.9
average_decay = 0.8
base_rate = 0.02
norm_eps = 1e-06
mask_fill = -1e30


def normalize(inputs):
    mean_val = jnp.mean(inputs, axis=-1, keepdims=True)
    centred = inputs - mean_val
    variance = jnp.mean(centred * centred, axis=-1, keepdims=True)
    return centred * lax.rsqrt(variance + norm_eps)


def norm_affine(inputs, gain_part, shift_part):
    return normalize(inputs) * gain_part + shift_part


def gelu_exact(inputs):
    return jax.nn.gelu(inputs, approximate=False)


def over_tokens(left_mat, right_mat):
    return lax.dot_general(
        left_mat, right_mat, (((0,), (0,)), ((), ())), preferred_element_type=jnp.float32
    )


def against_rows(left_mat, right_mat):
    return lax.dot_general(
        left_mat, right_mat, (((1,), (1,)), ((), ())), preferred_element_type=jnp.float32
    )


def block_mask(clip_ids, key_ok):
    return (clip_ids[:, None] == clip_ids[None, :]) & (key_ok[None, :] == 1)


def forward(inputs, params, clip_ids, key_ok, masked):
    attn_full = params[0]
    mlp_full = params[1]
    gain_f = params[2].astype(jnp.float32)
    shift_f = params[3].astype(jnp.float32)
    tok_rows = inputs.shape[0]
    score_scale = HEAD_DIM ** (-0.5)
    is_masked = masked[:, None] == 1
    embedded = jnp.where(is_masked, shift_f[6 * D : 7 * D][None, :], inputs)
    normed_one = norm_affine(embedded, gain_f[:D], shift_f[:D]).astype(jnp.bfloat16)
    qkv_bias = jnp.concatenate(
        [shift_f[D : 2 * D], jnp.zeros((D,), jnp.float32), shift_f[2 * D : 3 * D]]
    )
    projected = (
        jnp.dot(normed_one, attn_full[:, : 3 * D], preferred_element_type=jnp.float32) + qkv_bias
    )
    projected = projected.astype(jnp.bfloat16)
    queries = projected[:, :D].reshape(tok_rows, HEADS, HEAD_DIM)
    key_heads = projected[:, D : 2 * D].reshape(tok_rows, HEADS, HEAD_DIM)
    value_heads = projected[:, 2 * D :].reshape(tok_rows, HEADS, HEAD_DIM)
    allowed = block_mask(clip_ids, key_ok)
    scores = (
        jnp.einsum("qhd,khd->hqk", queries, key_heads, preferred_element_type=jnp.float32)
        * score_scale
    )
    scores = jnp.where(allowed[None], scores, mask_fill)
    row_peak = jnp.max(scores, axis=-1, keepdims=True)
    exponent = jnp.exp(scores - row_peak)
    summed = jnp.sum(exponent, axis=-1, keepdims=True)
    attn_prob = (exponent / summed).astype(jnp.bfloat16)
    mixed_parts = jnp.einsum(
        "hqk,khd->qhd", attn_prob, value_heads, preferred_element_type=jnp.float32
    )
    lse_parts = [row_peak + jnp.log(summed)]
    mixed_out = mixed_parts.reshape(tok_rows, D).astype(jnp.bfloat16)
    after_attn = embedded + against_rows(mixed_out, attn_full[:, 3 * D :]) + shift_f[3 * D : 4 * D]
    normed_two = norm_affine(after_attn, gain_f[D:], shift_f[4 * D : 5 * D]).astype(jnp.bfloat16)
    hidden_pre = (
        jnp.dot(normed_two, mlp_full[:, :FF], preferred_element_type=jnp.float32) + shift_f[7 * D :]
    )
    hidden_act = gelu_exact(hidden_pre).astype(jnp.bfloat16)
    output = after_attn + against_rows(hidden_act, mlp_full[:, FF:]) + shift_f[5 * D : 6 * D]
    kept_values = (
        embedded,
        normed_one,
        queries,
        key_heads,
        value_heads,
        lse_parts,
        mixed_out,
        after_attn,
        normed_two,
        hidden_pre,
        hidden_act,
        gain_f,
        shift_f,
    )
    return (output, kept_values)


def backward(cotangent, params, kept_values, clip_ids, key_ok, masked):
    attn_full = params[0]
    mlp_full = params[1]
    (
        embedded,
        normed_one,
        queries,
        key_heads,
        value_heads,
        lse_parts,
        mixed_out,
        after_attn,
        normed_two,
        hidden_pre,
        hidden_act,
        gain_f,
        shift_f,
    ) = kept_values
    tok_rows = cotangent.shape[0]
    score_scale = HEAD_DIM ** (-0.5)
    d_out = cotangent.astype(jnp.float32)
    d_bias_two = jnp.sum(d_out, axis=0)
    d_down = over_tokens(cotangent, hidden_act)
    d_act = jnp.dot(cotangent, mlp_full[:, FF:], preferred_element_type=jnp.float32)
    gelu_value, gelu_pull = jax.vjp(gelu_exact, hidden_pre)
    d_pre_low = gelu_pull(d_act)[0].astype(jnp.bfloat16)
    d_bias_one = jnp.sum(d_pre_low.astype(jnp.float32), axis=0)
    d_up = over_tokens(normed_two, d_pre_low)
    mlp_grad = jnp.concatenate([d_up, d_down], axis=1)
    d_normed_two = against_rows(d_pre_low, mlp_full[:, :FF])
    norm_value, norm_pull = jax.vjp(norm_affine, after_attn, gain_f[D:], shift_f[4 * D : 5 * D])
    d_after_norm, d_gain_two, d_shift_two = norm_pull(d_normed_two)
    d_after = d_out + d_after_norm
    d_after_low = d_after.astype(jnp.bfloat16)
    d_bias_out = jnp.sum(d_after, axis=0)
    d_outproj = over_tokens(d_after_low, mixed_out)
    d_mixed = jnp.dot(d_after_low, attn_full[:, 3 * D :], preferred_element_type=jnp.float32)
    d_mixed_low = d_mixed.astype(jnp.bfloat16).reshape(tok_rows, HEADS, HEAD_DIM)
    block_rows = min(512, tok_rows)
    d_query_parts = []
    d_keys = jnp.zeros((tok_rows, HEADS, HEAD_DIM), jnp.float32)
    d_values = jnp.zeros((tok_rows, HEADS, HEAD_DIM), jnp.float32)
    for block_number, offset in enumerate(range(0, tok_rows, block_rows)):
        allowed = block_mask(clip_ids, key_ok)
        scores = (
            jnp.einsum("qhd,khd->hqk", queries, key_heads, preferred_element_type=jnp.float32)
            * score_scale
        )
        scores = jnp.where(allowed[None], scores, mask_fill)
        attn_prob = jnp.exp(scores - lse_parts[block_number])
        prob_low = attn_prob.astype(jnp.bfloat16)
        d_prob = jnp.einsum(
            "qhd,khd->hqk", d_mixed_low, value_heads, preferred_element_type=jnp.float32
        )
        row_delta = jnp.sum(d_prob * attn_prob, axis=-1, keepdims=True)
        d_scores = (attn_prob * (d_prob - row_delta)).astype(jnp.bfloat16)
        d_query_parts.append(
            jnp.einsum("hqk,khd->qhd", d_scores, key_heads, preferred_element_type=jnp.float32)
            * score_scale
        )
        d_keys = (
            jnp.einsum("hqk,qhd->khd", d_scores, queries, preferred_element_type=jnp.float32)
            * score_scale
        )
        d_values = jnp.einsum(
            "hqk,qhd->khd", prob_low, d_mixed_low, preferred_element_type=jnp.float32
        )
    d_queries = d_query_parts[0]
    d_proj_low = jnp.concatenate(
        [
            d_queries.reshape(tok_rows, D),
            d_keys.reshape(tok_rows, D),
            d_values.reshape(tok_rows, D),
        ],
        axis=1,
    ).astype(jnp.bfloat16)
    d_bias_q = jnp.sum(d_proj_low[:, :D].astype(jnp.float32), axis=0)
    d_bias_v = jnp.sum(d_proj_low[:, 2 * D :].astype(jnp.float32), axis=0)
    d_qkv = over_tokens(normed_one, d_proj_low)
    d_normed_one = against_rows(d_proj_low, attn_full[:, : 3 * D])
    first_value, first_pull = jax.vjp(norm_affine, embedded, gain_f[:D], shift_f[:D])
    d_embed_norm, d_gain_one, d_shift_one = first_pull(d_normed_one)
    d_embedded = d_after + d_embed_norm
    is_masked = masked[:, None] == 1
    d_mask_vec = jnp.sum(jnp.where(is_masked, d_embedded, 0.0), axis=0)
    input_grad = jnp.where(is_masked, 0.0, d_embedded).astype(jnp.bfloat16)
    attn_grad = jnp.concatenate([d_qkv, d_outproj], axis=1)
    gain_grad = jnp.concatenate([d_gain_one, d_gain_two])
    offset_grad = jnp.concatenate(
        [
            d_shift_one,
            d_bias_q,
            d_bias_v,
            d_bias_out,
            d_shift_two,
            d_bias_two,
            d_mask_vec,
            d_bias_one,
        ]
    )
    return (input_grad, (attn_grad, mlp_grad, gain_grad, offset_grad))


def advance(gradient, weight, moment, average, learn_rate):
    moment_new = momentum_decay * moment + gradient
    weight_new = weight - learn_rate * (gradient + momentum_decay * moment_new)
    average_new = average_decay * average + (1.0 - average_decay) * weight_new
    return (weight_new, moment_new, average_new, weight_new.astype(jnp.bfloat16))


def per_device(
    tokens,
    cotangent,
    clip_index,
    key_valid,
    patch_masked,
    attn_weight,
    mlp_weight,
    gain_vector,
    offset_vector,
    attn_moment,
    mlp_moment,
    gain_moment,
    offset_moment,
    attn_average,
    mlp_average,
    gain_average,
    offset_average,
):
    attn_shard = attn_weight.astype(jnp.bfloat16)
    mlp_shard = mlp_weight.astype(jnp.bfloat16)
    gain_shard = gain_vector.astype(jnp.bfloat16)
    offset_shard = offset_vector.astype(jnp.bfloat16)
    params = (
        lax.all_gather(attn_shard, "fsdp", axis=0, tiled=True),
        lax.all_gather(mlp_shard, "fsdp", axis=0, tiled=True),
        lax.all_gather(gain_shard, "fsdp", axis=0, tiled=True),
        lax.all_gather(offset_shard, "fsdp", axis=0, tiled=True),
    )
    inputs = tokens.astype(jnp.float32)
    output, first_kept = forward(inputs, params, clip_index, key_valid, patch_masked)
    again = (
        lax.all_gather(attn_shard, "fsdp", axis=0, tiled=True),
        lax.all_gather(mlp_shard, "fsdp", axis=0, tiled=True),
        lax.all_gather(gain_shard, "fsdp", axis=0, tiled=True),
        lax.all_gather(offset_shard, "fsdp", axis=0, tiled=True),
    )
    output_again, kept_values = forward(inputs, again, clip_index, key_valid, patch_masked)
    input_grad, gradients = backward(
        cotangent, again, kept_values, clip_index, key_valid, patch_masked
    )
    owned = (
        lax.psum_scatter(gradients[0], "fsdp", scatter_dimension=0, tiled=True),
        lax.psum_scatter(gradients[1], "fsdp", scatter_dimension=0, tiled=True),
        lax.psum_scatter(gradients[2], "fsdp", scatter_dimension=0, tiled=True),
        lax.psum_scatter(gradients[3], "fsdp", scatter_dimension=0, tiled=True),
    )
    shares = (
        lax.psum_scatter(
            owned[0].astype(jnp.bfloat16), "rep", scatter_dimension=1, tiled=True
        ).astype(jnp.float32),
        lax.psum_scatter(
            owned[1].astype(jnp.bfloat16), "rep", scatter_dimension=1, tiled=True
        ).astype(jnp.float32),
        lax.psum_scatter(
            owned[2].astype(jnp.bfloat16), "rep", scatter_dimension=0, tiled=True
        ).astype(jnp.float32),
        lax.psum_scatter(
            owned[3].astype(jnp.bfloat16), "rep", scatter_dimension=0, tiled=True
        ).astype(jnp.float32),
    )
    reduced = (
        lax.all_gather(shares[0].astype(jnp.bfloat16), "rep", axis=1, tiled=True).astype(
            jnp.float32
        ),
        lax.all_gather(shares[1].astype(jnp.bfloat16), "rep", axis=1, tiled=True).astype(
            jnp.float32
        ),
        lax.all_gather(shares[2].astype(jnp.bfloat16), "rep", axis=0, tiled=True).astype(
            jnp.float32
        ),
        lax.all_gather(shares[3].astype(jnp.bfloat16), "rep", axis=0, tiled=True).astype(
            jnp.float32
        ),
    )
    learn_rate = base_rate / math.sqrt(
        tokens.shape[0] * lax.axis_size("rep") * lax.axis_size("fsdp")
    )
    attn_new, attn_momentum, attn_ema, attn_copy = advance(
        reduced[0], attn_weight, attn_moment, attn_average, learn_rate
    )
    mlp_new, mlp_momentum, mlp_ema, mlp_copy = advance(
        reduced[1], mlp_weight, mlp_moment, mlp_average, learn_rate
    )
    gain_new, gain_momentum, gain_ema, gain_copy = advance(
        reduced[2], gain_vector, gain_moment, gain_average, learn_rate
    )
    offset_new, offset_momentum, offset_ema, offset_copy = advance(
        reduced[3], offset_vector, offset_moment, offset_average, learn_rate
    )
    return (
        output.astype(jnp.bfloat16),
        input_grad,
        attn_new,
        attn_momentum,
        attn_ema,
        attn_copy,
        mlp_new,
        mlp_momentum,
        mlp_ema,
        mlp_copy,
        gain_new,
        gain_momentum,
        gain_ema,
        gain_copy,
        offset_new,
        offset_momentum,
        offset_ema,
        offset_copy,
    )


class Operand:
    def __init__(self, ref):
        self.ref, self.shape = ref, ref.shape

    def __getitem__(self, index):
        return self.ref[index]


def call(kernel, outs, args, scratch=(), name=None, limit=8, space=pltpu.VMEM):
    def body(co_ref, *refs):
        operands = [Operand(ref) for ref in refs[: len(args) - 1]]
        kernel(co_ref, *operands, *refs[len(args) - 1 :])

    return pl.pallas_call(
        body,
        out_shape=[jax.ShapeDtypeStruct(shape, dtype) for shape, dtype in outs],
        in_specs=[pl.BlockSpec(memory_space=pltpu.SMEM)]
        + [pl.BlockSpec(memory_space=space)] * (len(args) - 1),
        out_specs=[pl.BlockSpec(memory_space=pltpu.VMEM)] * len(outs),
        scratch_shapes=list(scratch),
        compiler_params=pltpu.CompilerParams(vmem_limit_bytes=limit * 2**20),
        cost_estimate=pl.CostEstimate(flops=2**20, bytes_accessed=2**20, transcendentals=0),
        name=name,
    )(*args)


def call_all(co, jobs, name):
    args = [arg for job in jobs for arg in job[2]]
    outs = [out for job in jobs for out in job[1]]

    def body(co_ref, *refs):
        first, last = 0, len(args)
        for kernel, job_outs, job_args in jobs:
            ins = refs[first : first + len(job_args)]
            results = refs[last : last + len(job_outs)]
            kernel(co_ref, *ins, *results)
            first += len(job_args)
            last += len(job_outs)

    return call(body, outs, [co, *args], name=name)


def assemble_kernel(ranges, co, *refs):
    count = len(refs) - len(ranges)
    each = count // 2
    for number in range(count):
        blocks = refs[number].shape[0] // 48
        for block in range(blocks):
            i, k = (number % 2, block) if blocks == 4 else (block // 4, block % 4)
            b = (number // 2) % 2 if each == 4 else 0
            row = k * 192 + lax.bitwise_xor(co[2], i) * 96
            row = row + lax.bitwise_xor(co[3], number // each) * 48
            rows = pl.ds(pl.multiple_of(row, 16), 48)
            for (start, size), out in zip(ranges, refs[count:]):
                out[rows, b * size : b * size + size] = refs[number][
                    block * 48 : block * 48 + 48, start : start + size
                ]


def assemble(co, pieces, *ranges):
    widths = [size * (2 if len(pieces) == 8 else 1) for start, size in ranges]
    return call(
        functools.partial(assemble_kernel, ranges),
        [((D, width), BF) for width in widths],
        [co, *pieces],
        name="assemble",
    )


def lanes(offset, size):
    return pl.ds(pl.multiple_of(offset, 128), size)


def nn(left, right):
    return lax.dot_general(left, right, (((1,), (0,)), ((), ())), preferred_element_type=jnp.float32)


def nt(left, right):
    return lax.dot_general(left, right, (((1,), (1,)), ((), ())), preferred_element_type=jnp.float32)


def whole(weight, start, size):
    return weight[:, start : start + size]


def row_norm(values):
    mean = jnp.mean(values, axis=-1, keepdims=True)
    centred = values - mean
    var = jnp.mean(centred * centred, axis=-1, keepdims=True)
    rstd = lax.rsqrt(var + norm_eps)
    return centred * rstd, rstd


def prep_first_kernel(co, attn, mlp, s0, wide, sems):
    r = co[0]
    sources = [attn.ref.at[:, lanes(part * D + 384 * r, 384)] for part in range(4)]
    sources += [mlp.ref.at[:, lanes(1536 * r + n * 384, 384)] for n in range(2)]
    copies = [
        pltpu.make_async_copy(source, wide.at[n], sems.at[n]) for n, source in enumerate(sources)
    ]
    for copy in copies:
        copy.start()
    for n, copy in enumerate(copies):
        copy.wait()
        s0[:, n * 384 : n * 384 + 384] = wide[n].astype(BF)


def prep_second_kernel(co, mlp, s1, s2):
    r = co[0]
    for b in range(2):
        half = lax.bitwise_xor(r, b)
        s1[:, b * D : b * D + D] = mlp[:, lanes(1536 * half + D, D)].astype(BF)
        s2[:, b * D : b * D + D] = mlp[:, lanes(FF + 1536 * half + D, D)].astype(BF)
    s1[:, 2 * D :] = mlp[:, lanes(FF + 1536 * r, D)].astype(BF)


def turn(co, values, scratch, send, keep):
    scratch[...] = values.T
    for out, core in ((send, 1 - co[3]), (keep, co[3])):
        for block in range(8):
            row = pl.multiple_of(block * 96 + 48 * core, 16)
            out[block * 48 : block * 48 + 48, :] = scratch[pl.ds(row, 48), :].astype(BF)


def first_norm_kernel(co, tokens, info, vec, h1, h1t_send, h1t_keep, cols, scratch):
    turned = jnp.transpose(info[...])
    cols[:, 0:8] = turned
    x0 = jnp.where(turned[:, 2:3] == 1.0, vec[8:9, :], tokens[...].astype(F32))
    xh, rstd = row_norm(x0)
    h = xh * vec[0:1, :] + vec[2:3, :]
    h1[...] = h.astype(BF)
    turn(co, h, scratch, h1t_send, h1t_keep)


def allowed_pairs(info, cols):
    return (cols[:, 0:1] == info[0:1, :]) & (cols[:, 1:2] == 1.0)


def attention_kernel(co, h1, vec, info, cols, weight, qkv, att, lse):
    for b in range(2):
        half = lax.bitwise_xor(co[0], b)
        for part in range(3):
            out = nn(h1[...], whole(weight, b * 1152 + part * 384, 384))
            if part != 1:
                row = 3 if part == 0 else 4
                out = out + vec.ref[row : row + 1, lanes(384 * half, 384)]
            qkv[:, b * 1152 + part * 384 : b * 1152 + part * 384 + 384] = out.astype(BF)
    allowed = allowed_pairs(info, cols)
    low = lax.broadcasted_iota(jnp.int32, (256, 128), 1) < 64
    for pair in range(6):
        base = (pair // 3) * 1152 + (pair % 3) * 128
        q2 = qkv[:, base : base + 128]
        k2 = qkv[:, base + 384 : base + 512]
        v2 = qkv[:, base + 768 : base + 896]
        mixed = []
        for side in range(2):
            qm = jnp.where(low if side == 0 else ~low, q2, jnp.zeros_like(q2))
            s = jnp.where(allowed, nt(k2, qm) * 0.125, mask_fill)
            peak = jnp.max(s, axis=0, keepdims=True)
            e = jnp.exp(s - peak)
            total = jnp.sum(e, axis=0, keepdims=True)
            prob = (e * (1.0 / total)).astype(BF)
            lse[2 * pair + side : 2 * pair + side + 1, :] = peak + jnp.log(total)
            mixed.append(over_tokens(prob, v2))
        att[:, pair * 128 : pair * 128 + 128] = jnp.where(low, mixed[0], mixed[1]).astype(BF)


def second_norm_kernel(
    co, tokens, cols, vec, att, weight, dz, y1, h2, h2t_send, h2t_keep, dzt_send, dzt_keep, scratch
):
    x0 = jnp.where(cols[:, 2:3] == 1.0, vec[8:9, :], tokens[...].astype(F32))
    y = x0 + nt(att[...], whole(weight, 0, D)) + vec[5:6, :]
    y1[...] = y
    xh, rstd = row_norm(y)
    h = xh * vec[1:2, :] + vec[6:7, :]
    h2[...] = h.astype(BF)
    turn(co, h, scratch, h2t_send, h2t_keep)
    turn(co, dz[...].astype(F32), scratch, dzt_send, dzt_keep)


def hidden_kernel(co, h2, vec, w0, w1, g0, g1, slope0, slope1):
    for part, weight, g, slope in ((0, w0, g0, slope0), (1, w1, g1, slope1)):
        for b in range(2):
            half = lax.bitwise_xor(co[0], b)
            for sub in range(0, D, 384):
                at = slice(b * D + sub, b * D + sub + 384)
                u = nn(h2[...], weight[:, at])
                u = u + vec[pl.ds(9 + 2 * half + part, 1), sub : sub + 384]
                phi = 0.5 * (1.0 + lax.erf(u * math.sqrt(0.5)))
                g[:, at] = (u * phi).astype(BF)
                slope[:, at] = phi + u * (
                    jnp.exp(-0.5 * u * u) * (1.0 / math.sqrt(2.0 * math.pi))
                )


def down_grad_kernel(co, dzt_send, dzt_keep, g0, g1, send, keep):
    for part, g in ((0, g0), (1, g1)):
        for b in range(2):
            half = lax.bitwise_xor(co[0], b)
            dst = lanes(half * D, D) if part == 0 else lanes((2 + b) * D, D)
            share_rows(dzt_send, dzt_keep, g[:, b * D : b * D + D], send, keep, dst)


def hidden_grad_kernel(
    co,
    dz,
    slope0,
    slope1,
    w00,
    w01,
    w10,
    w11,
    left_send,
    left_keep,
    du0,
    du1,
    db1,
    send,
    keep,
):
    for part, slope, du in ((0, slope0, du0), (1, slope1, du1)):
        for b in range(2):
            weight = ((w00, w01), (w10, w11))[b][part]
            half = lax.bitwise_xor(co[0], b)
            for sub in range(0, D, 384):
                at = slice(b * D + sub, b * D + sub + 384)
                da = nn(dz[...], weight[:, sub : sub + 384])
                d = (da * slope[:, at]).astype(BF)
                du[:, at] = d
                db1[pl.ds(2 * half + part, 1), sub : sub + 384] = jnp.sum(
                    d.astype(F32), axis=0, keepdims=True
                )
                dst = lanes(half * D + sub, 384) if part == 0 else lanes((2 + b) * D + sub, 384)
                share_rows(left_send, left_keep, d, send, keep, dst)


def output_kernel(co, y1, vec, g0, g1, w00, w01, w10, w11, act):
    acc = y1[...] + vec[7:8, :]
    for part, g in ((0, g0), (1, g1)):
        acc = acc + nt(g[:, :D], (w00, w01)[part][...])
        acc = acc + nt(g[:, D:], (w10, w11)[part][...])
    act[...] = acc.astype(BF)


def share_rows(left_send, left_keep, right, send, keep, dst):
    send[:, dst] = nn(left_send[...], right).astype(BF)
    keep[:, dst] = nn(left_keep[...], right)


def attention_grad_kernel(
    co, h1t_send, h1t_keep, dqkv, dpt_send, dpt_keep, att, send, keep
):
    first, second = (h1t_send, h1t_keep), (dpt_send, dpt_keep)
    moves = [(first, dqkv, b * 1152 + 384 + n * 384, b * D + n * 384) for b in (0, 1) for n in (0, 1)]
    for b in range(2):
        place = 384 * lax.bitwise_xor(co[0], b)
        moves.append((first, dqkv, b * 1152, 2 * D + place))
        moves.append((second, att, b * 384, 3 * D + place))
    for left, right, src, dst in moves:
        share_rows(*left, right[:, src : src + 384], send, keep, lanes(dst, 384))


def second_back_kernel(
    co, dz, y1, vec, du0, du1, w0, w1, weight_o, dy1, datt, dpt_send, dpt_keep, small, scratch
):
    yh, rstd = row_norm(y1[...])
    dy = dz[...].astype(F32)
    dh = nt(du0[...], whole(w0, 0, 2 * D)) + nt(du1[...], whole(w1, 0, 2 * D))
    small[0:1, :] = jnp.sum(dh * yh, axis=0, keepdims=True)
    small[1:2, :] = jnp.sum(dh, axis=0, keepdims=True)
    small[3:4, :] = jnp.sum(dy, axis=0, keepdims=True)
    e = dh * vec[1:2, :]
    d = dy + rstd * (
        e - jnp.mean(e, axis=-1, keepdims=True) - yh * jnp.mean(e * yh, axis=-1, keepdims=True)
    )
    dy1[...] = d
    small[2:3, :] = jnp.sum(d, axis=0, keepdims=True)
    turn(co, d, scratch, dpt_send, dpt_keep)
    datt[...] = nn(d.astype(BF), whole(weight_o, 0, D)).astype(BF)


def attention_back_kernel(co, info, cols, lse, qkv, datt, dqkv, small):
    allowed = allowed_pairs(info, cols)
    low = lax.broadcasted_iota(jnp.int32, (256, 128), 1) < 64
    for pair in range(6):
        half = lax.bitwise_xor(co[0], pair // 3)
        base = (pair // 3) * 1152 + (pair % 3) * 128
        q2 = qkv[:, base : base + 128]
        k2 = qkv[:, base + 384 : base + 512]
        v2 = qkv[:, base + 768 : base + 896]
        o2 = datt[:, pair * 128 : pair * 128 + 128]
        dqs, dks, dvs = [], [], []
        for side in range(2):
            mine = low if side == 0 else ~low
            qm = jnp.where(mine, q2, jnp.zeros_like(q2))
            om = jnp.where(mine, o2, jnp.zeros_like(o2))
            s = jnp.where(allowed, nt(k2, qm) * 0.125, mask_fill)
            prob = jnp.exp(s - lse[2 * pair + side : 2 * pair + side + 1, :])
            dprob = nt(v2, om)
            delta = jnp.sum(dprob * prob, axis=0, keepdims=True)
            ds = (prob * (dprob - delta)).astype(BF)
            dqs.append(over_tokens(ds, k2))
            dks.append(nn(ds, q2))
            dvs.append(nn(prob.astype(BF), o2))
        dq = (jnp.where(low, dqs[0], dqs[1]) * 0.125).astype(BF)
        dk = (jnp.where(low, dks[0], dks[1]) * 0.125).astype(BF)
        dv = jnp.where(low, dvs[0], dvs[1]).astype(BF)
        dqkv[:, base : base + 128] = dq
        dqkv[:, base + 384 : base + 512] = dk
        dqkv[:, base + 768 : base + 896] = dv
        place = lanes(384 * half + (pair % 3) * 128, 128)
        small[0:1, place] = jnp.sum(dq.astype(F32), axis=0, keepdims=True)
        small[1:2, place] = jnp.sum(dv.astype(F32), axis=0, keepdims=True)


def first_back_kernel(
    co, dqkv, tokens, cols, vec, dy1, db1, small2, small_a, weight, input_grad, total
):
    hidden = cols[:, 2:3] == 1.0
    x0 = jnp.where(hidden, vec[8:9, :], tokens[...].astype(F32))
    xh, rstd = row_norm(x0)
    dh = nt(dqkv[...], whole(weight, 0, 3 * D))
    e = dh * vec[0:1, :]
    dx = dy1[...] + rstd * (
        e - jnp.mean(e, axis=-1, keepdims=True) - xh * jnp.mean(e * xh, axis=-1, keepdims=True)
    )
    input_grad[...] = jnp.where(hidden, 0.0, dx).astype(BF)
    total[0:1, :] = jnp.sum(dh * xh, axis=0, keepdims=True)
    total[1:2, :] = small2[0:1, :]
    total[2:3, :] = jnp.sum(dh, axis=0, keepdims=True)
    total[3:5, :] = small_a[0:2, :]
    total[5:6, :] = small2[2:3, :]
    total[6:7, :] = small2[1:2, :]
    total[7:8, :] = small2[3:4, :]
    total[8:9, :] = jnp.sum(jnp.where(hidden, dx, 0.0), axis=0, keepdims=True)
    total[9:13, :] = db1[0:4, :]
    total[13:16, :] = jnp.zeros((3, D), F32)


def both(keep, got, *at):
    return keep[at] + got[at].astype(F32)


def split_first_kernel(co, keep, got, y_send, y_keep, x_send, x_keep):
    y = co[2]
    every = slice(None)
    for k in range(4):
        for out, i in ((y_send, 1 - y), (y_keep, y)):
            out[k * 48 : k * 48 + 48, :] = both(keep, got, k, i, every, slice(0, 2 * D)).astype(
                out.dtype
            )
    x_keep[...] = both(keep, got, every, every, every, slice(2 * D, 3 * D))
    x_send[...] = both(keep, got, every, every, every, slice(3 * D, 4 * D)).astype(BF)


def split_second_kernel(co, x_keep, x_got, keep, got, y_send, y_keep, x_send, x_next):
    y = co[2]
    every = slice(None)
    for k in range(4):
        rows = slice(k * 48, k * 48 + 48)
        for out, i in ((y_send, 1 - y), (y_keep, y)):
            out[rows, :D] = both(x_keep, x_got, k, i).astype(out.dtype)
            out[rows, D:] = both(keep, got, k, i, every, slice(0, D)).astype(out.dtype)
    x_next[...] = both(keep, got, every, every, every, slice(2 * D, 3 * D))
    x_send[...] = both(keep, got, every, every, every, slice(3 * D, 4 * D)).astype(BF)


def split_third_kernel(co, x_keep, x_got, keep, got, y_send, y_keep, x_send, x_next, last):
    y = co[2]
    every = slice(None)
    for k in range(4):
        rows = slice(k * 48, k * 48 + 48)
        for out, i in ((y_send, 1 - y), (y_keep, y)):
            out[rows, :D] = both(x_keep, x_got, k, i).astype(out.dtype)
            out[rows, D:] = both(keep, got, k, i, every, slice(2 * D, 3 * D)).astype(out.dtype)
    x_next[...] = both(keep, got, every, every, every, slice(0, D))
    x_send[...] = both(keep, got, every, every, every, slice(D, 2 * D)).astype(BF)
    last[...] = both(keep, got, every, every, every, slice(3 * D, 4 * D))


def split_fourth_kernel(co, x_keep, x_got, last, far_keep, far_got, y_send, y_keep):
    y = co[2]
    for out, i in ((y_send, 1 - y), (y_keep, y)):
        for k in range(4):
            rows = slice(k * 48, k * 48 + 48)
            out[rows, :D] = both(x_keep, x_got, k, i).astype(out.dtype)
            out[rows, D:] = last[k, i].astype(out.dtype)
        row = pl.multiple_of(96 + i * 48, 16)
        block = both(far_keep, far_got, pl.ds(row, 48)).astype(out.dtype)
        out[192:224, :D] = block[:32]
        out[192:208, D:] = block[32:]
        out[208:224, D:] = jnp.zeros((16, D), out.dtype)


def split_near_first_kernel(co, keep, got, up_keep, up_got, send, rest):
    side = co[1] % 2
    for out, at in ((send, 1 - side), (rest, side)):
        for far in range(2):
            row = pl.multiple_of((2 * far + at) * 48, 16)
            for half in range(2):
                to = half * 96 + far * 48
                cols = slice(half * D, half * D + D)
                out[to : to + 48, :] = both(keep, got, pl.ds(row, 48), cols).astype(out.dtype)
                to = 192 + far * 96 + half * 48
                total = both(up_keep, up_got, 2 * far + at, half, slice(None), slice(D, 2 * D))
                out[to : to + 48, :] = total.astype(out.dtype)


def split_far_first_kernel(co, keep, got, send, rest):
    side = co[1] // 2
    for out, at in ((send, 1 - side), (rest, side)):
        for half in range(2):
            row = pl.multiple_of(half * 96 + at * 48, 16)
            to = half * 48
            out[to : to + 48, :] = both(keep, got, pl.ds(row, 48)).astype(out.dtype)
        row = pl.multiple_of(192 + at * 96, 16)
        out[96:192, :] = both(keep, got, pl.ds(row, 96)).astype(out.dtype)


def sum_far_first_kernel(co, keep, got, out):
    for half in range(2):
        rows = slice(half * 48, half * 48 + 48)
        out[:, half * D : half * D + D] = both(keep, got, rows).astype(BF)


def sum_far_second_kernel(co, keep, got, other, out):
    out[:, : 2 * D] = both(keep, got, slice(None)).astype(BF)
    out[:, 2 * D :] = other[...].astype(BF)


def split_near_kernel(co, keep, got, send, rest, *small):
    side = co[1] % 2
    for out, at in ((send, 1 - side), (rest, side)):
        for far in range(2):
            row = pl.multiple_of((2 * far + at) * 48, 16)
            out[far * 48 : far * 48 + 48, :] = both(keep, got, pl.ds(row, 48)).astype(out.dtype)
    if small:
        small[0][0:32, :] = both(keep, got, slice(192, 224), slice(0, D))
        small[0][32:48, :] = both(keep, got, slice(192, 208), slice(D, 2 * D))


def split_far_kernel(co, keep, got, send, rest):
    side = co[1] // 2
    for out, at in ((send, 1 - side), (rest, side)):
        row = pl.multiple_of(at * 48, 16)
        out[...] = both(keep, got, pl.ds(row, 48)).astype(out.dtype)


def sum_far_kernel(co, keep, got, out):
    out[...] = (keep[...] + got[...].astype(F32)).astype(BF)


def update_kernel(rate, moves, n_states, n_grads, n_before, co, *refs):
    grads = refs[3 * n_states :][:n_grads]
    first = 3 * n_states + n_grads + n_before
    parts, sems = refs[first + 4 * n_states : -1], refs[-1]
    copies = []
    for n, (which, numbers, row, src, size, b, col, stride) in enumerate(moves):
        state, new = refs[3 * which :][:3], refs[first + 4 * which :][:4]
        grad = 0.0
        for number in numbers:
            grad = grad + grads[number][row : row + 48, src : src + size].astype(F32)
        place = col if b is None else col + stride * lax.bitwise_xor(co[0], b)
        at = lanes(place, size)
        w, m, a = (ref[:, at] for ref in state)
        m_new = momentum_decay * m + grad
        w_new = w - rate * (grad + momentum_decay * m_new)
        full, low = parts[2 * n], parts[2 * n + 1]
        full[0] = w_new
        full[1] = m_new
        full[2] = average_decay * a + (1.0 - average_decay) * w_new
        low[...] = w_new.astype(BF)
        for k in range(4):
            source = full.at[k] if k < 3 else low
            copy = pltpu.make_async_copy(source, new[k].at[:, at], sems.at[4 * n + k])
            copy.start()
            copies.append(copy)
    for copy in copies:
        copy.wait()


def hold(arrays):
    return lax.optimization_barrier(arrays)


def fast_device(
    tokens,
    cotangent,
    clip_index,
    key_valid,
    patch_masked,
    attn_weight,
    mlp_weight,
    gain_vector,
    offset_vector,
    attn_moment,
    mlp_moment,
    gain_moment,
    offset_moment,
    attn_average,
    mlp_average,
    gain_average,
    offset_average,
):
    r, f = lax.axis_index("rep"), lax.axis_index("fsdp")
    co = jnp.stack([r, f // 4, (f // 2) % 2, f % 2]).astype(jnp.int32)

    def swap(array, mask):
        return lax.ppermute(array, ("rep", "fsdp"), [(i, i ^ mask) for i in range(32)])

    CORE, Y, Z, X = 1, 2, 4, 16

    (s0,) = call(
        prep_first_kernel,
        [((48, 3 * D), BF)],
        [co, attn_weight, mlp_weight],
        scratch=[pltpu.VMEM((6, 48, 384), F32), pltpu.SemaphoreType.DMA((6,))],
        name="prep",
        limit=60,
        space=pltpu.HBM,
    )
    info = jnp.zeros((8, 256), F32).at[0:3].set(
        jnp.stack([clip_index, key_valid, patch_masked]).astype(F32)
    )
    flat = jnp.zeros((16 * D,), F32)
    flat = lax.dynamic_update_slice(flat, gain_vector.astype(BF).astype(F32), (96 * f,))
    flat = lax.dynamic_update_slice(flat, offset_vector.astype(BF).astype(F32), (2 * D + 528 * f,))
    vec = flat.reshape(16, D)

    groups = [[4 * z + at for z in range(4)] for at in range(4)]

    def along_z(shard):
        return lax.all_gather(shard, "fsdp", axis=0, tiled=True, axis_index_groups=groups)

    def core_pair(pieces):
        return pieces + [swap(piece, CORE) for piece in pieces]

    stack0 = along_z(s0)
    stack0, vec, mlp_late = hold((stack0, vec, mlp_weight))
    s1, s2 = call(
        prep_second_kernel,
        [((48, 3 * D), BF), ((48, 2 * D), BF)],
        [co, mlp_late],
        name="prep",
    )
    across0 = swap(stack0, Y)
    far0 = swap(stack0, X)
    vec = vec + swap(vec, CORE)
    s1, vec = hold((s1, vec))
    near0 = [swap(stack0, CORE)]
    stack1 = along_z(s1)
    vec = vec + swap(vec, Y)
    stack1, across0, far0, near0, s2, vec = hold((stack1, across0, far0, near0, s2, vec))
    far_across0 = swap(across0, X)
    across1 = swap(stack1, Y)
    near0 += [swap(across0, CORE), swap(far0, CORE)]
    vec = vec + swap(vec, Z)
    s2, vec = hold((s2, vec))
    stack2 = along_z(s2)
    vec = vec + swap(vec, 2 * Z)
    stack2, across1, far_across0, near0, vec = hold((stack2, across1, far_across0, near0, vec))
    pieces0 = [stack0, across0, far0, far_across0, *near0, swap(far_across0, CORE)]
    across2 = swap(stack2, Y)
    far1 = swap(jnp.concatenate([stack1[:, 2 * D :], across1[:, 2 * D :]], axis=0), X)
    pieces1 = core_pair([stack1, across1])
    halves_t = [((384, 256), BF)] * 2
    h1, h1t_send, h1t_keep, cols = call(
        first_norm_kernel,
        [((256, D), BF), *halves_t, ((256, 128), F32)],
        [co, tokens, info, vec],
        scratch=[pltpu.VMEM((D, 256), F32)],
        name="norm1",
    )
    (w_qkv,) = assemble(co, pieces0, (0, 1152))
    qkv, att, lse = call(
        attention_kernel,
        [((256, 3 * D), BF), ((256, D), BF), ((16, 256), F32)],
        [co, h1, vec, info, cols, w_qkv],
        name="attention",
    )
    w_out, w_up0 = assemble(co, pieces0, (1152, 384), (1536, 768))
    w_up1, w_down00 = assemble(co, pieces1, (0, 1536), (1536, 768))

    y1, h2, h2t_send, h2t_keep, dzt_send, dzt_keep = call(
        second_norm_kernel,
        [((256, D), F32), ((256, D), BF), *halves_t, *halves_t],
        [co, tokens, cols, vec, att, w_out, cotangent],
        scratch=[pltpu.VMEM((D, 256), F32)],
        name="norm2",
    )
    shares = [((384, 4 * D), BF), ((384, 4 * D), F32)]
    g0, g1, slope0, slope1 = call(
        hidden_kernel,
        [((256, 2 * D), BF)] * 2 + [((256, 2 * D), F32)] * 2,
        [co, h2, vec, w_up0, w_up1],
        name="hidden",
    )

    def blocks(array):
        return array.reshape(4, 2, 48, -1)

    rate = base_rate / math.sqrt(tokens.shape[0] * 32)

    def update(moves, states, grads, name, before=()):
        parts, outs = [], []
        for move in moves:
            parts += [pltpu.VMEM((3, 48, move[4]), F32), pltpu.VMEM((48, move[4]), BF)]
        for state in states:
            outs += [jax.ShapeDtypeStruct(state[0].shape, F32)] * 3
            outs += [jax.ShapeDtypeStruct(state[0].shape, BF)]
        whole = pl.BlockSpec(memory_space=pltpu.VMEM)
        far = pl.BlockSpec(memory_space=pltpu.HBM)
        first = 1 + 3 * len(states) + len(grads)
        return pl.pallas_call(
            functools.partial(update_kernel, rate, moves, len(states), len(grads), len(before)),
            out_shape=outs,
            in_specs=[pl.BlockSpec(memory_space=pltpu.SMEM)]
            + [whole] * (first - 1)
            + [far] * len(before),
            out_specs=[far] * len(outs),
            input_output_aliases={first + k: k for k in range(len(before))},
            scratch_shapes=[*parts, pltpu.SemaphoreType.DMA((4 * len(moves),))],
            compiler_params=pltpu.CompilerParams(vmem_limit_bytes=8 * 2**20),
            cost_estimate=pl.CostEstimate(flops=2**20, bytes_accessed=2**20, transcendentals=0),
            name=name,
        )(co, *(array for state in states for array in state), *grads, *before)

    mlp_state = [mlp_weight, mlp_moment, mlp_average]
    attn_state = [attn_weight, attn_moment, attn_average]

    across2, far1, g0, g1 = hold((across2, far1, g0, g1))
    pieces2 = core_pair([stack2, across2])
    far1 = core_pair([far1])
    down_send, down_keep = call(
        down_grad_kernel, shares, [co, dzt_send, dzt_keep, g0, g1], name="down_grad"
    )
    pieces2, far1, down_send = hold((pieces2, far1, down_send))
    down_got = blocks(swap(down_send, CORE))
    down_keep = blocks(down_keep)
    w_down01, w_down11 = assemble(co, pieces2, (0, D), (D, D))
    (w_down10,) = assemble(co, far1, (0, D))
    du0, du1, db1, up_send, up_keep = call(
        hidden_grad_kernel,
        [((256, 2 * D), BF), ((256, 2 * D), BF), ((8, D), F32)] + shares,
        [co, cotangent, slope0, slope1, w_down00, w_down01, w_down10, w_down11, h2t_send, h2t_keep],
        name="hidden_grad",
    )
    down_got, up_send = hold((down_got, up_send))
    y_shares = [((192, 2 * D), BF), ((192, 2 * D), F32)]
    x_shares = [((4, 2, 48, D), BF), ((4, 2, 48, D), F32)]
    y_send0, y_keep0, x_send1, x_keep1 = call(
        split_first_kernel, y_shares + x_shares, [co, down_keep, down_got], name="split_first"
    )
    y_send0, x_send1, up_send, du0 = hold((y_send0, x_send1, up_send, du0))
    y_got0 = swap(y_send0, Y)
    x_got1 = swap(x_send1, X)
    up_got = blocks(swap(up_send, CORE))
    up_keep = blocks(up_keep)
    dy1, datt, dpt_send, dpt_keep, small2 = call(
        second_back_kernel,
        [((256, D), F32), ((256, D), BF), *halves_t, ((8, D), F32)],
        [co, cotangent, y1, vec, du0, du1, w_up0, w_up1, w_out],
        scratch=[pltpu.VMEM((D, 256), F32)],
        name="norm2_back",
    )
    dqkv, small_a = call(
        attention_back_kernel,
        [((256, 3 * D), BF), ((8, D), F32)],
        [co, info, cols, lse, qkv, datt],
        name="attention_back",
    )
    attn_send, attn_keep = call(
        attention_grad_kernel,
        shares,
        [co, h1t_send, h1t_keep, dqkv, dpt_send, dpt_keep, att],
        name="attention_grad",
    )

    def split_near(keep, got, small=()):
        width = keep.shape[1]
        return call(
            split_near_kernel,
            [((96, width), BF), ((96, width), F32), *small],
            [co, keep, got],
            name="split_near",
        )

    def split_far(keep, got):
        width = keep.shape[1]
        return call(
            split_far_kernel,
            [((48, width), BF), ((48, width), F32)],
            [co, keep, got],
            name="split_far",
        )

    def sum_far(keep, got):
        return call(sum_far_kernel, [(keep.shape, BF)], [co, keep, got], name="sum_far")[0]

    def near_job(keep, got, small=()):
        width = keep.shape[1]
        return split_near_kernel, [((96, width), BF), ((96, width), F32), *small], [keep, got]

    def far_job(keep, got):
        width = keep.shape[1]
        return split_far_kernel, [((48, width), BF), ((48, width), F32)], [keep, got]

    def sum_job(keep, got):
        return sum_far_kernel, [(keep.shape, BF)], [keep, got]

    y_got0, x_got1, up_got, attn_send = hold((y_got0, x_got1, up_got, attn_send))
    y_send1, y_keep1, x_send2, x_keep2, near_send0, near_keep0 = call_all(
        co,
        [
            (split_second_kernel, y_shares + x_shares, [x_keep1, x_got1, up_keep, up_got]),
            (
                split_near_first_kernel,
                [((384, D), BF), ((384, D), F32)],
                [y_keep0, y_got0, up_keep, up_got],
            ),
        ],
        "split_third_round",
    )
    dqkv = hold((dqkv, near_send0))[0]
    y_got1 = swap(y_send1, Y)
    x_got2 = swap(x_send2, X)
    near_got0 = swap(near_send0, Z)
    attn_got = blocks(swap(attn_send, CORE))
    attn_keep = blocks(attn_keep)
    input_grad, total = call(
        first_back_kernel,
        [((256, D), BF), ((16, D), F32)],
        [co, dqkv, tokens, cols, vec, dy1, db1, small2, small_a, w_qkv],
        name="norm1_back",
    )
    near_got0, y_got1, x_got2, attn_got, total = hold(
        (near_got0, y_got1, x_got2, attn_got, total)
    )
    far_send0, far_keep0 = call(
        split_far_first_kernel,
        [((192, D), BF), ((192, D), F32)],
        [co, near_keep0, near_got0],
        name="split_far",
    )
    x_got2 = hold((x_got2, far_send0))[0]
    y_send2, y_keep2, x_send3, x_keep3, last = call(
        split_third_kernel,
        y_shares + x_shares + x_shares[1:],
        [co, x_keep2, x_got2, attn_keep, attn_got],
        name="split_third",
    )
    y_got1 = hold((y_got1, y_send2))[0]
    near_send1, near_keep1 = split_near(y_keep1, y_got1)
    y1 = hold((y1, near_send1))[0]
    x_got3 = swap(x_send3, X)
    y_got2 = swap(y_send2, Y)
    near_got1 = swap(near_send1, Z)
    far_got0 = swap(far_send0, 2 * Z)
    total = total + swap(total, CORE)
    (activations,) = call(
        output_kernel,
        [((256, D), BF)],
        [co, y1, vec, g0, g1, w_down00, w_down01, w_down10, w_down11],
        name="output",
    )
    far_got0, near_got1, y_got2, x_got3, total, activations = hold(
        (far_got0, near_got1, y_got2, x_got3, total, activations)
    )
    y_send3, y_keep3 = call(
        split_fourth_kernel,
        [((224, 2 * D), BF), ((224, 2 * D), F32)],
        [co, x_keep3, x_got3, last, far_keep0, far_got0],
        name="split_fourth",
    )
    y_got2 = hold((y_got2, y_send3))[0]
    near_send2, near_keep2 = split_near(y_keep2, y_got2)
    near_got1 = hold((near_got1, near_send2))[0]
    far_send1, far_keep1 = split_far(near_keep1, near_got1)
    far_got0 = hold((far_got0, far_send1))[0]
    (mine0,) = call(
        sum_far_first_kernel, [((48, 2 * D), BF)], [co, far_keep0, far_got0], name="sum_far"
    )
    y_got3 = swap(y_send3, Y)
    near_got2 = swap(near_send2, Z)
    far_got1 = swap(far_send1, 2 * Z)
    got0 = swap(mine0, X)
    total = total + swap(total, 2 * Z)
    got0, far_got1, near_got2, y_got3, total = hold(
        (got0, far_got1, near_got2, y_got3, total)
    )
    near_send3, near_keep3, other, far_send2, far_keep2 = call_all(
        co,
        [near_job(y_keep3, y_got3, [((48, D), F32)]), far_job(near_keep2, near_got2)],
        "split_sixth_round",
    )
    (mine1,) = call(
        sum_far_second_kernel,
        [((48, 3 * D), BF)],
        [co, far_keep1, far_got1, other],
        name="sum_far",
    )
    near_got3 = swap(near_send3, Z)
    far_got2 = swap(far_send2, 2 * Z)
    got1 = swap(mine1, X)
    total = total + swap(total, Z)
    got1, far_got2, near_got3, total = hold((got1, far_got2, near_got3, total))
    far_send3, far_keep3 = split_far(near_keep3, near_got3)
    far_got2 = hold((far_got2, far_send3))[0]
    mine2 = sum_far(far_keep2, far_got2)
    far_got3 = swap(far_send3, 2 * Z)
    got2 = swap(mine2, X)
    total = total + swap(total, Y)
    moves = [(0, (0, 1), 0, h * D, D, None, FF + h * 2 * D, 0) for h in range(2)]
    moves += [(0, (2 + b,), 0, 0, D, b, FF + D, 2 * D) for b in range(2)]
    moves += [(0, (2, 3), 0, D + h * D, D, None, h * 2 * D, 0) for h in range(2)]
    got1 = hold((got1, mine2))[0]
    mlp = update(moves, [mlp_state], [mine0, got0, mine1, got1], "update_mlp")
    got2, far_got3, total, mlp = hold((got2, far_got3, total, mlp))
    mine3 = sum_far(far_keep3, far_got3)
    got3 = swap(mine3, X)
    total = total + swap(total, X)
    got2 = hold((got2, mine3))[0]
    moves = [(0, (b,), 0, 0, D, b, D, 2 * D) for b in range(2)]
    moves += [(1, (0, 1), 0, D, D, None, 0, 0)]
    both_new = update(
        moves,
        [mlp_state, attn_state],
        [mine2, got2],
        "update_both",
        mlp,
    )
    mlp, attn = both_new[:4], both_new[4:]
    moves = [(0, (b,), 0, 0, 384, b, D, 384) for b in range(2)]
    moves += [(0, (b,), 0, 384, 384, b, 2 * D, 384) for b in range(2)]
    moves += [(0, (0, 1), 0, D, D, None, 3 * D, 0)]
    attn = update(moves, [attn_state], [mine3, got3], "update_attn", attn)
    flat = total.reshape(-1)
    gain_g = lax.dynamic_slice(flat, (96 * f,), (96,))
    offset_g = lax.dynamic_slice(flat, (2 * D + 528 * f,), (528,))

    gains = advance(gain_g, gain_vector, gain_moment, gain_average, rate)
    offsets = advance(offset_g, offset_vector, offset_moment, offset_average, rate)
    return (activations, input_grad, *attn, *mlp, *gains, *offsets)


def solution(mesh):
    placed = (
        P(("rep", "fsdp"), None),
        P(("rep", "fsdp"), None),
        P(("rep", "fsdp")),
        P(("rep", "fsdp")),
        P(("rep", "fsdp")),
        P("fsdp", None),
        P("fsdp", None),
        P("fsdp"),
        P("fsdp"),
        P("fsdp", None),
        P("fsdp", None),
        P("fsdp"),
        P("fsdp"),
        P("fsdp", None),
        P("fsdp", None),
        P("fsdp"),
        P("fsdp"),
    )
    small = mesh.shape["rep"] == 2 and mesh.shape["fsdp"] == 16
    return jax.shard_map(
        fast_device if small else per_device,
        mesh=mesh,
        in_specs=placed,
        out_specs=(
            P(("rep", "fsdp"), None),
            P(("rep", "fsdp"), None),
            P("fsdp", None),
            P("fsdp", None),
            P("fsdp", None),
            P("fsdp", None),
            P("fsdp", None),
            P("fsdp", None),
            P("fsdp", None),
            P("fsdp", None),
            P("fsdp"),
            P("fsdp"),
            P("fsdp"),
            P("fsdp"),
            P("fsdp"),
            P("fsdp"),
            P("fsdp"),
            P("fsdp"),
        ),
        check_vma=False,
    )
```

```python
import functools
import math

import jax
import jax.numpy as jnp
from jax import lax
from jax.experimental import pallas as pl
from jax.experimental.pallas import tpu as pltpu
from jax.sharding import PartitionSpec as P

D = 768
HEADS = 12
HEAD_DIM = 64
FF = 3072
BF = jnp.bfloat16
F32 = jnp.float32


momentum_decay = 0.9
average_decay = 0.8
base_rate = 0.02
norm_eps = 1e-06
mask_fill = -1e30


def normalize(inputs):
    mean_val = jnp.mean(inputs, axis=-1, keepdims=True)
    centred = inputs - mean_val
    variance = jnp.mean(centred * centred, axis=-1, keepdims=True)
    return centred * lax.rsqrt(variance + norm_eps)


def norm_affine(inputs, gain_part, shift_part):
    return normalize(inputs) * gain_part + shift_part


def gelu_exact(inputs):
    return jax.nn.gelu(inputs, approximate=False)


def over_tokens(left_mat, right_mat):
    return lax.dot_general(
        left_mat, right_mat, (((0,), (0,)), ((), ())), preferred_element_type=jnp.float32
    )


def against_rows(left_mat, right_mat):
    return lax.dot_general(
        left_mat, right_mat, (((1,), (1,)), ((), ())), preferred_element_type=jnp.float32
    )


def block_mask(clip_ids, key_ok):
    return (clip_ids[:, None] == clip_ids[None, :]) & (key_ok[None, :] == 1)


def forward(inputs, params, clip_ids, key_ok, masked):
    attn_full = params[0]
    mlp_full = params[1]
    gain_f = params[2].astype(jnp.float32)
    shift_f = params[3].astype(jnp.float32)
    tok_rows = inputs.shape[0]
    score_scale = HEAD_DIM ** (-0.5)
    is_masked = masked[:, None] == 1
    embedded = jnp.where(is_masked, shift_f[6 * D : 7 * D][None, :], inputs)
    normed_one = norm_affine(embedded, gain_f[:D], shift_f[:D]).astype(jnp.bfloat16)
    qkv_bias = jnp.concatenate(
        [shift_f[D : 2 * D], jnp.zeros((D,), jnp.float32), shift_f[2 * D : 3 * D]]
    )
    projected = (
        jnp.dot(normed_one, attn_full[:, : 3 * D], preferred_element_type=jnp.float32) + qkv_bias
    )
    projected = projected.astype(jnp.bfloat16)
    queries = projected[:, :D].reshape(tok_rows, HEADS, HEAD_DIM)
    key_heads = projected[:, D : 2 * D].reshape(tok_rows, HEADS, HEAD_DIM)
    value_heads = projected[:, 2 * D :].reshape(tok_rows, HEADS, HEAD_DIM)
    allowed = block_mask(clip_ids, key_ok)
    scores = (
        jnp.einsum("qhd,khd->hqk", queries, key_heads, preferred_element_type=jnp.float32)
        * score_scale
    )
    scores = jnp.where(allowed[None], scores, mask_fill)
    row_peak = jnp.max(scores, axis=-1, keepdims=True)
    exponent = jnp.exp(scores - row_peak)
    summed = jnp.sum(exponent, axis=-1, keepdims=True)
    attn_prob = (exponent / summed).astype(jnp.bfloat16)
    mixed_parts = jnp.einsum(
        "hqk,khd->qhd", attn_prob, value_heads, preferred_element_type=jnp.float32
    )
    lse_parts = [row_peak + jnp.log(summed)]
    mixed_out = mixed_parts.reshape(tok_rows, D).astype(jnp.bfloat16)
    after_attn = embedded + against_rows(mixed_out, attn_full[:, 3 * D :]) + shift_f[3 * D : 4 * D]
    normed_two = norm_affine(after_attn, gain_f[D:], shift_f[4 * D : 5 * D]).astype(jnp.bfloat16)
    hidden_pre = (
        jnp.dot(normed_two, mlp_full[:, :FF], preferred_element_type=jnp.float32) + shift_f[7 * D :]
    )
    hidden_act = gelu_exact(hidden_pre).astype(jnp.bfloat16)
    output = after_attn + against_rows(hidden_act, mlp_full[:, FF:]) + shift_f[5 * D : 6 * D]
    kept_values = (
        embedded,
        normed_one,
        queries,
        key_heads,
        value_heads,
        lse_parts,
        mixed_out,
        after_attn,
        normed_two,
        hidden_pre,
        hidden_act,
        gain_f,
        shift_f,
    )
    return (output, kept_values)


def backward(cotangent, params, kept_values, clip_ids, key_ok, masked):
    attn_full = params[0]
    mlp_full = params[1]
    (
        embedded,
        normed_one,
        queries,
        key_heads,
        value_heads,
        lse_parts,
        mixed_out,
        after_attn,
        normed_two,
        hidden_pre,
        hidden_act,
        gain_f,
        shift_f,
    ) = kept_values
    tok_rows = cotangent.shape[0]
    score_scale = HEAD_DIM ** (-0.5)
    d_out = cotangent.astype(jnp.float32)
    d_bias_two = jnp.sum(d_out, axis=0)
    d_down = over_tokens(cotangent, hidden_act)
    d_act = jnp.dot(cotangent, mlp_full[:, FF:], preferred_element_type=jnp.float32)
    gelu_value, gelu_pull = jax.vjp(gelu_exact, hidden_pre)
    d_pre_low = gelu_pull(d_act)[0].astype(jnp.bfloat16)
    d_bias_one = jnp.sum(d_pre_low.astype(jnp.float32), axis=0)
    d_up = over_tokens(normed_two, d_pre_low)
    mlp_grad = jnp.concatenate([d_up, d_down], axis=1)
    d_normed_two = against_rows(d_pre_low, mlp_full[:, :FF])
    norm_value, norm_pull = jax.vjp(norm_affine, after_attn, gain_f[D:], shift_f[4 * D : 5 * D])
    d_after_norm, d_gain_two, d_shift_two = norm_pull(d_normed_two)
    d_after = d_out + d_after_norm
    d_after_low = d_after.astype(jnp.bfloat16)
    d_bias_out = jnp.sum(d_after, axis=0)
    d_outproj = over_tokens(d_after_low, mixed_out)
    d_mixed = jnp.dot(d_after_low, attn_full[:, 3 * D :], preferred_element_type=jnp.float32)
    d_mixed_low = d_mixed.astype(jnp.bfloat16).reshape(tok_rows, HEADS, HEAD_DIM)
    block_rows = min(512, tok_rows)
    d_query_parts = []
    d_keys = jnp.zeros((tok_rows, HEADS, HEAD_DIM), jnp.float32)
    d_values = jnp.zeros((tok_rows, HEADS, HEAD_DIM), jnp.float32)
    for block_number, offset in enumerate(range(0, tok_rows, block_rows)):
        allowed = block_mask(clip_ids, key_ok)
        scores = (
            jnp.einsum("qhd,khd->hqk", queries, key_heads, preferred_element_type=jnp.float32)
            * score_scale
        )
        scores = jnp.where(allowed[None], scores, mask_fill)
        attn_prob = jnp.exp(scores - lse_parts[block_number])
        prob_low = attn_prob.astype(jnp.bfloat16)
        d_prob = jnp.einsum(
            "qhd,khd->hqk", d_mixed_low, value_heads, preferred_element_type=jnp.float32
        )
        row_delta = jnp.sum(d_prob * attn_prob, axis=-1, keepdims=True)
        d_scores = (attn_prob * (d_prob - row_delta)).astype(jnp.bfloat16)
        d_query_parts.append(
            jnp.einsum("hqk,khd->qhd", d_scores, key_heads, preferred_element_type=jnp.float32)
            * score_scale
        )
        d_keys = (
            jnp.einsum("hqk,qhd->khd", d_scores, queries, preferred_element_type=jnp.float32)
            * score_scale
        )
        d_values = jnp.einsum(
            "hqk,qhd->khd", prob_low, d_mixed_low, preferred_element_type=jnp.float32
        )
    d_queries = d_query_parts[0]
    d_proj_low = jnp.concatenate(
        [
            d_queries.reshape(tok_rows, D),
            d_keys.reshape(tok_rows, D),
            d_values.reshape(tok_rows, D),
        ],
        axis=1,
    ).astype(jnp.bfloat16)
    d_bias_q = jnp.sum(d_proj_low[:, :D].astype(jnp.float32), axis=0)
    d_bias_v = jnp.sum(d_proj_low[:, 2 * D :].astype(jnp.float32), axis=0)
    d_qkv = over_tokens(normed_one, d_proj_low)
    d_normed_one = against_rows(d_proj_low, attn_full[:, : 3 * D])
    first_value, first_pull = jax.vjp(norm_affine, embedded, gain_f[:D], shift_f[:D])
    d_embed_norm, d_gain_one, d_shift_one = first_pull(d_normed_one)
    d_embedded = d_after + d_embed_norm
    is_masked = masked[:, None] == 1
    d_mask_vec = jnp.sum(jnp.where(is_masked, d_embedded, 0.0), axis=0)
    input_grad = jnp.where(is_masked, 0.0, d_embedded).astype(jnp.bfloat16)
    attn_grad = jnp.concatenate([d_qkv, d_outproj], axis=1)
    gain_grad = jnp.concatenate([d_gain_one, d_gain_two])
    offset_grad = jnp.concatenate(
        [
            d_shift_one,
            d_bias_q,
            d_bias_v,
            d_bias_out,
            d_shift_two,
            d_bias_two,
            d_mask_vec,
            d_bias_one,
        ]
    )
    return (input_grad, (attn_grad, mlp_grad, gain_grad, offset_grad))


def advance(gradient, weight, moment, average, learn_rate):
    moment_new = momentum_decay * moment + gradient
    weight_new = weight - learn_rate * (gradient + momentum_decay * moment_new)
    average_new = average_decay * average + (1.0 - average_decay) * weight_new
    return (weight_new, moment_new, average_new, weight_new.astype(jnp.bfloat16))


def per_device(
    tokens,
    cotangent,
    clip_index,
    key_valid,
    patch_masked,
    attn_weight,
    mlp_weight,
    gain_vector,
    offset_vector,
    attn_moment,
    mlp_moment,
    gain_moment,
    offset_moment,
    attn_average,
    mlp_average,
    gain_average,
    offset_average,
):
    attn_shard = attn_weight.astype(jnp.bfloat16)
    mlp_shard = mlp_weight.astype(jnp.bfloat16)
    gain_shard = gain_vector.astype(jnp.bfloat16)
    offset_shard = offset_vector.astype(jnp.bfloat16)
    params = (
        lax.all_gather(attn_shard, "fsdp", axis=0, tiled=True),
        lax.all_gather(mlp_shard, "fsdp", axis=0, tiled=True),
        lax.all_gather(gain_shard, "fsdp", axis=0, tiled=True),
        lax.all_gather(offset_shard, "fsdp", axis=0, tiled=True),
    )
    inputs = tokens.astype(jnp.float32)
    output, first_kept = forward(inputs, params, clip_index, key_valid, patch_masked)
    again = (
        lax.all_gather(attn_shard, "fsdp", axis=0, tiled=True),
        lax.all_gather(mlp_shard, "fsdp", axis=0, tiled=True),
        lax.all_gather(gain_shard, "fsdp", axis=0, tiled=True),
        lax.all_gather(offset_shard, "fsdp", axis=0, tiled=True),
    )
    output_again, kept_values = forward(inputs, again, clip_index, key_valid, patch_masked)
    input_grad, gradients = backward(
        cotangent, again, kept_values, clip_index, key_valid, patch_masked
    )
    owned = (
        lax.psum_scatter(gradients[0], "fsdp", scatter_dimension=0, tiled=True),
        lax.psum_scatter(gradients[1], "fsdp", scatter_dimension=0, tiled=True),
        lax.psum_scatter(gradients[2], "fsdp", scatter_dimension=0, tiled=True),
        lax.psum_scatter(gradients[3], "fsdp", scatter_dimension=0, tiled=True),
    )
    shares = (
        lax.psum_scatter(
            owned[0].astype(jnp.bfloat16), "rep", scatter_dimension=1, tiled=True
        ).astype(jnp.float32),
        lax.psum_scatter(
            owned[1].astype(jnp.bfloat16), "rep", scatter_dimension=1, tiled=True
        ).astype(jnp.float32),
        lax.psum_scatter(
            owned[2].astype(jnp.bfloat16), "rep", scatter_dimension=0, tiled=True
        ).astype(jnp.float32),
        lax.psum_scatter(
            owned[3].astype(jnp.bfloat16), "rep", scatter_dimension=0, tiled=True
        ).astype(jnp.float32),
    )
    reduced = (
        lax.all_gather(shares[0].astype(jnp.bfloat16), "rep", axis=1, tiled=True).astype(
            jnp.float32
        ),
        lax.all_gather(shares[1].astype(jnp.bfloat16), "rep", axis=1, tiled=True).astype(
            jnp.float32
        ),
        lax.all_gather(shares[2].astype(jnp.bfloat16), "rep", axis=0, tiled=True).astype(
            jnp.float32
        ),
        lax.all_gather(shares[3].astype(jnp.bfloat16), "rep", axis=0, tiled=True).astype(
            jnp.float32
        ),
    )
    learn_rate = base_rate / math.sqrt(
        tokens.shape[0] * lax.axis_size("rep") * lax.axis_size("fsdp")
    )
    attn_new, attn_momentum, attn_ema, attn_copy = advance(
        reduced[0], attn_weight, attn_moment, attn_average, learn_rate
    )
    mlp_new, mlp_momentum, mlp_ema, mlp_copy = advance(
        reduced[1], mlp_weight, mlp_moment, mlp_average, learn_rate
    )
    gain_new, gain_momentum, gain_ema, gain_copy = advance(
        reduced[2], gain_vector, gain_moment, gain_average, learn_rate
    )
    offset_new, offset_momentum, offset_ema, offset_copy = advance(
        reduced[3], offset_vector, offset_moment, offset_average, learn_rate
    )
    return (
        output.astype(jnp.bfloat16),
        input_grad,
        attn_new,
        attn_momentum,
        attn_ema,
        attn_copy,
        mlp_new,
        mlp_momentum,
        mlp_ema,
        mlp_copy,
        gain_new,
        gain_momentum,
        gain_ema,
        gain_copy,
        offset_new,
        offset_momentum,
        offset_ema,
        offset_copy,
    )


class Operand:
    def __init__(self, ref):
        self.ref, self.shape = ref, ref.shape

    def __getitem__(self, index):
        return self.ref[index]


def call(kernel, outs, args, scratch=(), name=None, limit=8, space=pltpu.VMEM):
    def body(co_ref, *refs):
        operands = [Operand(ref) for ref in refs[: len(args) - 1]]
        kernel(co_ref, *operands, *refs[len(args) - 1 :])

    return pl.pallas_call(
        body,
        out_shape=[jax.ShapeDtypeStruct(shape, dtype) for shape, dtype in outs],
        in_specs=[pl.BlockSpec(memory_space=pltpu.SMEM)]
        + [pl.BlockSpec(memory_space=space)] * (len(args) - 1),
        out_specs=[pl.BlockSpec(memory_space=pltpu.VMEM)] * len(outs),
        scratch_shapes=list(scratch),
        compiler_params=pltpu.CompilerParams(vmem_limit_bytes=limit * 2**20),
        cost_estimate=pl.CostEstimate(flops=2**20, bytes_accessed=2**20, transcendentals=0),
        name=name,
    )(*args)


def call_all(co, jobs, name, dtype=None):
    args = [arg for job in jobs for arg in job[2]]
    chosen = [out for job in jobs for out in job[1] if dtype in (None, out[1])]

    def body(co_ref, *refs):
        first, results = 0, iter(refs[len(args) :])
        for kernel, job_outs, job_args in jobs:
            outs = [next(results) if dtype in (None, out[1]) else None for out in job_outs]
            kernel(co_ref, *refs[first : first + len(job_args)], *outs)
            first += len(job_args)

    return call(body, chosen, [co, *args], name=name)


def assemble_kernel(ranges, co, *refs):
    count = len(refs) - len(ranges)
    each = count // 2
    for number in range(count):
        blocks = refs[number].shape[0] // 48
        for block in range(blocks):
            i, k = (number % 2, block) if blocks == 4 else (block // 4, block % 4)
            b = (number // 2) % 2 if each == 4 else 0
            row = k * 192 + lax.bitwise_xor(co[2], i) * 96
            row = row + lax.bitwise_xor(co[3], number // each) * 48
            rows = pl.ds(pl.multiple_of(row, 16), 48)
            for (start, size), out in zip(ranges, refs[count:]):
                out[rows, b * size : b * size + size] = refs[number][
                    block * 48 : block * 48 + 48, start : start + size
                ]


def assemble(co, pieces, *ranges):
    widths = [size * (2 if len(pieces) == 8 else 1) for start, size in ranges]
    return call(
        functools.partial(assemble_kernel, ranges),
        [((D, width), BF) for width in widths],
        [co, *pieces],
        name="assemble",
    )


def lanes(offset, size):
    return pl.ds(pl.multiple_of(offset, 128), size)


def nn(left, right):
    return lax.dot_general(left, right, (((1,), (0,)), ((), ())), preferred_element_type=jnp.float32)


def nt(left, right):
    return lax.dot_general(left, right, (((1,), (1,)), ((), ())), preferred_element_type=jnp.float32)


def whole(weight, start, size):
    return weight[:, start : start + size]


def row_norm(values):
    mean = jnp.mean(values, axis=-1, keepdims=True)
    centred = values - mean
    var = jnp.mean(centred * centred, axis=-1, keepdims=True)
    rstd = lax.rsqrt(var + norm_eps)
    return centred * rstd, rstd


def prep_first_kernel(co, attn, mlp, s0, wide, sems):
    r = co[0]
    sources = [attn.ref.at[:, lanes(part * D + 384 * r, 384)] for part in range(4)]
    sources += [mlp.ref.at[:, lanes(1536 * r + n * 384, 384)] for n in range(2)]
    copies = [
        pltpu.make_async_copy(source, wide.at[n], sems.at[n]) for n, source in enumerate(sources)
    ]
    for copy in copies:
        copy.start()
    for n, copy in enumerate(copies):
        copy.wait()
        s0[:, n * 384 : n * 384 + 384] = wide[n].astype(BF)


def prep_second_kernel(co, mlp, s1, s2):
    r = co[0]
    for b in range(2):
        half = lax.bitwise_xor(r, b)
        s1[:, b * D : b * D + D] = mlp[:, lanes(1536 * half + D, D)].astype(BF)
        s2[:, b * D : b * D + D] = mlp[:, lanes(FF + 1536 * half + D, D)].astype(BF)
    s1[:, 2 * D :] = mlp[:, lanes(FF + 1536 * r, D)].astype(BF)


def turn(co, values, scratch, send, keep):
    scratch[...] = values.T
    for out, core in ((send, 1 - co[3]), (keep, co[3])):
        for block in range(8):
            row = pl.multiple_of(block * 96 + 48 * core, 16)
            out[block * 48 : block * 48 + 48, :] = scratch[pl.ds(row, 48), :].astype(BF)


def first_norm_kernel(co, tokens, info, vec, h1, h1t_send, h1t_keep, cols, scratch):
    turned = jnp.transpose(info[...])
    cols[:, 0:8] = turned
    x0 = jnp.where(turned[:, 2:3] == 1.0, vec[8:9, :], tokens[...].astype(F32))
    xh, rstd = row_norm(x0)
    h = xh * vec[0:1, :] + vec[2:3, :]
    h1[...] = h.astype(BF)
    turn(co, h, scratch, h1t_send, h1t_keep)


def allowed_pairs(info, cols):
    return (cols[:, 0:1] == info[0:1, :]) & (cols[:, 1:2] == 1.0)


def attention_kernel(co, h1, vec, info, cols, weight, qkv, att, lse):
    for b in range(2):
        half = lax.bitwise_xor(co[0], b)
        for part in range(3):
            out = nn(h1[...], whole(weight, b * 1152 + part * 384, 384))
            if part != 1:
                row = 3 if part == 0 else 4
                out = out + vec.ref[row : row + 1, lanes(384 * half, 384)]
            qkv[:, b * 1152 + part * 384 : b * 1152 + part * 384 + 384] = out.astype(BF)
    allowed = allowed_pairs(info, cols)
    low = lax.broadcasted_iota(jnp.int32, (256, 128), 1) < 64
    for pair in range(6):
        base = (pair // 3) * 1152 + (pair % 3) * 128
        q2 = qkv[:, base : base + 128]
        k2 = qkv[:, base + 384 : base + 512]
        v2 = qkv[:, base + 768 : base + 896]
        mixed = []
        for side in range(2):
            qm = jnp.where(low if side == 0 else ~low, q2, jnp.zeros_like(q2))
            s = jnp.where(allowed, nt(k2, qm) * 0.125, mask_fill)
            peak = jnp.max(s, axis=0, keepdims=True)
            e = jnp.exp(s - peak)
            total = jnp.sum(e, axis=0, keepdims=True)
            prob = (e * (1.0 / total)).astype(BF)
            lse[2 * pair + side : 2 * pair + side + 1, :] = peak + jnp.log(total)
            mixed.append(over_tokens(prob, v2))
        att[:, pair * 128 : pair * 128 + 128] = jnp.where(low, mixed[0], mixed[1]).astype(BF)


def second_norm_kernel(
    co, tokens, cols, vec, att, weight, dz, y1, h2, h2t_send, h2t_keep, dzt_send, dzt_keep, scratch
):
    x0 = jnp.where(cols[:, 2:3] == 1.0, vec[8:9, :], tokens[...].astype(F32))
    y = x0 + nt(att[...], whole(weight, 0, D)) + vec[5:6, :]
    y1[...] = y
    xh, rstd = row_norm(y)
    h = xh * vec[1:2, :] + vec[6:7, :]
    h2[...] = h.astype(BF)
    turn(co, h, scratch, h2t_send, h2t_keep)
    turn(co, dz[...].astype(F32), scratch, dzt_send, dzt_keep)


def hidden_kernel(co, h2, vec, w0, w1, g0, g1, slope0, slope1):
    for part, weight, g, slope in ((0, w0, g0, slope0), (1, w1, g1, slope1)):
        for b in range(2):
            half = lax.bitwise_xor(co[0], b)
            for sub in range(0, D, 384):
                at = slice(b * D + sub, b * D + sub + 384)
                u = nn(h2[...], weight[:, at])
                u = u + vec[pl.ds(9 + 2 * half + part, 1), sub : sub + 384]
                phi = 0.5 * (1.0 + lax.erf(u * math.sqrt(0.5)))
                g[:, at] = (u * phi).astype(BF)
                slope[:, at] = phi + u * (
                    jnp.exp(-0.5 * u * u) * (1.0 / math.sqrt(2.0 * math.pi))
                )


def down_grad_kernel(co, dzt_send, dzt_keep, g0, g1, send, keep):
    for part, g in ((0, g0), (1, g1)):
        for b in range(2):
            half = lax.bitwise_xor(co[0], b)
            dst = lanes(half * D, D) if part == 0 else lanes((2 + b) * D, D)
            share_rows(dzt_send, dzt_keep, g[:, b * D : b * D + D], send, keep, dst)


def hidden_grad_kernel(
    co,
    dz,
    slope0,
    slope1,
    w00,
    w01,
    w10,
    w11,
    left_send,
    left_keep,
    du0,
    du1,
    db1,
    send,
    keep,
):
    for part, slope, du in ((0, slope0, du0), (1, slope1, du1)):
        for b in range(2):
            weight = ((w00, w01), (w10, w11))[b][part]
            half = lax.bitwise_xor(co[0], b)
            for sub in range(0, D, 384):
                at = slice(b * D + sub, b * D + sub + 384)
                da = nn(dz[...], weight[:, sub : sub + 384])
                d = (da * slope[:, at]).astype(BF)
                du[:, at] = d
                db1[pl.ds(2 * half + part, 1), sub : sub + 384] = jnp.sum(
                    d.astype(F32), axis=0, keepdims=True
                )
                dst = lanes(half * D + sub, 384) if part == 0 else lanes((2 + b) * D + sub, 384)
                share_rows(left_send, left_keep, d, send, keep, dst)


def output_kernel(co, y1, vec, g0, g1, w00, w01, w10, w11, act):
    acc = y1[...] + vec[7:8, :]
    for part, g in ((0, g0), (1, g1)):
        acc = acc + nt(g[:, :D], (w00, w01)[part][...])
        acc = acc + nt(g[:, D:], (w10, w11)[part][...])
    act[...] = acc.astype(BF)


def share_rows(left_send, left_keep, right, send, keep, dst):
    send[:, dst] = nn(left_send[...], right).astype(BF)
    keep[:, dst] = nn(left_keep[...], right)


def attention_grad_kernel(
    co, h1t_send, h1t_keep, dqkv, dpt_send, dpt_keep, att, send, keep
):
    first, second = (h1t_send, h1t_keep), (dpt_send, dpt_keep)
    moves = [(first, dqkv, b * 1152 + 384 + n * 384, b * D + n * 384) for b in (0, 1) for n in (0, 1)]
    for b in range(2):
        place = 384 * lax.bitwise_xor(co[0], b)
        moves.append((first, dqkv, b * 1152, 2 * D + place))
        moves.append((second, att, b * 384, 3 * D + place))
    for left, right, src, dst in moves:
        share_rows(*left, right[:, src : src + 384], send, keep, lanes(dst, 384))


def second_back_kernel(
    co, dz, y1, vec, du0, du1, w0, w1, weight_o, dy1, datt, dpt_send, dpt_keep, small, scratch
):
    yh, rstd = row_norm(y1[...])
    dy = dz[...].astype(F32)
    dh = nt(du0[...], whole(w0, 0, 2 * D)) + nt(du1[...], whole(w1, 0, 2 * D))
    small[0:1, :] = jnp.sum(dh * yh, axis=0, keepdims=True)
    small[1:2, :] = jnp.sum(dh, axis=0, keepdims=True)
    small[3:4, :] = jnp.sum(dy, axis=0, keepdims=True)
    e = dh * vec[1:2, :]
    d = dy + rstd * (
        e - jnp.mean(e, axis=-1, keepdims=True) - yh * jnp.mean(e * yh, axis=-1, keepdims=True)
    )
    dy1[...] = d
    small[2:3, :] = jnp.sum(d, axis=0, keepdims=True)
    turn(co, d, scratch, dpt_send, dpt_keep)
    datt[...] = nn(d.astype(BF), whole(weight_o, 0, D)).astype(BF)


def attention_back_kernel(co, info, cols, lse, qkv, datt, dqkv, small):
    allowed = allowed_pairs(info, cols)
    low = lax.broadcasted_iota(jnp.int32, (256, 128), 1) < 64
    for pair in range(6):
        half = lax.bitwise_xor(co[0], pair // 3)
        base = (pair // 3) * 1152 + (pair % 3) * 128
        q2 = qkv[:, base : base + 128]
        k2 = qkv[:, base + 384 : base + 512]
        v2 = qkv[:, base + 768 : base + 896]
        o2 = datt[:, pair * 128 : pair * 128 + 128]
        dqs, dks, dvs = [], [], []
        for side in range(2):
            mine = low if side == 0 else ~low
            qm = jnp.where(mine, q2, jnp.zeros_like(q2))
            om = jnp.where(mine, o2, jnp.zeros_like(o2))
            s = jnp.where(allowed, nt(k2, qm) * 0.125, mask_fill)
            prob = jnp.exp(s - lse[2 * pair + side : 2 * pair + side + 1, :])
            dprob = nt(v2, om)
            delta = jnp.sum(dprob * prob, axis=0, keepdims=True)
            ds = (prob * (dprob - delta)).astype(BF)
            dqs.append(over_tokens(ds, k2))
            dks.append(nn(ds, q2))
            dvs.append(nn(prob.astype(BF), o2))
        dq = (jnp.where(low, dqs[0], dqs[1]) * 0.125).astype(BF)
        dk = (jnp.where(low, dks[0], dks[1]) * 0.125).astype(BF)
        dv = jnp.where(low, dvs[0], dvs[1]).astype(BF)
        dqkv[:, base : base + 128] = dq
        dqkv[:, base + 384 : base + 512] = dk
        dqkv[:, base + 768 : base + 896] = dv
        place = lanes(384 * half + (pair % 3) * 128, 128)
        small[0:1, place] = jnp.sum(dq.astype(F32), axis=0, keepdims=True)
        small[1:2, place] = jnp.sum(dv.astype(F32), axis=0, keepdims=True)


def first_back_kernel(
    co, dqkv, tokens, cols, vec, dy1, db1, small2, small_a, weight, input_grad, total
):
    hidden = cols[:, 2:3] == 1.0
    x0 = jnp.where(hidden, vec[8:9, :], tokens[...].astype(F32))
    xh, rstd = row_norm(x0)
    dh = nt(dqkv[...], whole(weight, 0, 3 * D))
    e = dh * vec[0:1, :]
    dx = dy1[...] + rstd * (
        e - jnp.mean(e, axis=-1, keepdims=True) - xh * jnp.mean(e * xh, axis=-1, keepdims=True)
    )
    input_grad[...] = jnp.where(hidden, 0.0, dx).astype(BF)
    total[0:1, :] = jnp.sum(dh * xh, axis=0, keepdims=True)
    total[1:2, :] = small2[0:1, :]
    total[2:3, :] = jnp.sum(dh, axis=0, keepdims=True)
    total[3:5, :] = small_a[0:2, :]
    total[5:6, :] = small2[2:3, :]
    total[6:7, :] = small2[1:2, :]
    total[7:8, :] = small2[3:4, :]
    total[8:9, :] = jnp.sum(jnp.where(hidden, dx, 0.0), axis=0, keepdims=True)
    total[9:13, :] = db1[0:4, :]
    total[13:16, :] = jnp.zeros((3, D), F32)


def both(keep, got, *at):
    return keep[at] + got[at].astype(F32)


def split_first_kernel(co, keep, got, y_send, y_keep, x_send, x_keep):
    y = co[2]
    every = slice(None)
    for k in range(4):
        for out, i in ((y_send, 1 - y), (y_keep, y)):
            if out is None:
                continue
            out[k * 48 : k * 48 + 48, :] = both(keep, got, k, i, every, slice(0, 2 * D)).astype(
                out.dtype
            )
    if x_keep is not None:
        x_keep[...] = both(keep, got, every, every, every, slice(2 * D, 3 * D))
    if x_send is not None:
        x_send[...] = both(keep, got, every, every, every, slice(3 * D, 4 * D)).astype(BF)


def split_second_kernel(co, x_keep, x_got, keep, got, y_send, y_keep, x_send, x_next):
    y = co[2]
    every = slice(None)
    for k in range(4):
        rows = slice(k * 48, k * 48 + 48)
        for out, i in ((y_send, 1 - y), (y_keep, y)):
            if out is None:
                continue
            out[rows, :D] = both(x_keep, x_got, k, i).astype(out.dtype)
            out[rows, D:] = both(keep, got, k, i, every, slice(0, D)).astype(out.dtype)
    if x_next is not None:
        x_next[...] = both(keep, got, every, every, every, slice(2 * D, 3 * D))
    if x_send is not None:
        x_send[...] = both(keep, got, every, every, every, slice(3 * D, 4 * D)).astype(BF)


def split_third_kernel(co, x_keep, x_got, keep, got, y_send, y_keep, x_send, x_next, last):
    y = co[2]
    every = slice(None)
    for k in range(4):
        rows = slice(k * 48, k * 48 + 48)
        for out, i in ((y_send, 1 - y), (y_keep, y)):
            if out is None:
                continue
            out[rows, :D] = both(x_keep, x_got, k, i).astype(out.dtype)
            out[rows, D:] = both(keep, got, k, i, every, slice(2 * D, 3 * D)).astype(out.dtype)
    if x_next is not None:
        x_next[...] = both(keep, got, every, every, every, slice(0, D))
    if x_send is not None:
        x_send[...] = both(keep, got, every, every, every, slice(D, 2 * D)).astype(BF)
    if last is not None:
        last[...] = both(keep, got, every, every, every, slice(3 * D, 4 * D))


def split_fourth_kernel(co, x_keep, x_got, last, y_send, y_keep):
    y = co[2]
    for out, i in ((y_send, 1 - y), (y_keep, y)):
        for k in range(4):
            rows = slice(k * 48, k * 48 + 48)
            out[rows, :D] = both(x_keep, x_got, k, i).astype(out.dtype)
            out[rows, D:] = last[k, i].astype(out.dtype)


def split_near_first_kernel(co, keep, got, up_keep, up_got, send, rest):
    side = co[1] % 2
    for out, at in ((send, 1 - side), (rest, side)):
        if out is None:
            continue
        for far in range(2):
            row = pl.multiple_of((2 * far + at) * 48, 16)
            for half in range(2):
                to = half * 96 + far * 48
                cols = slice(half * D, half * D + D)
                out[to : to + 48, :] = both(keep, got, pl.ds(row, 48), cols).astype(out.dtype)
                to = 192 + far * 96 + half * 48
                total = both(up_keep, up_got, 2 * far + at, half, slice(None), slice(D, 2 * D))
                out[to : to + 48, :] = total.astype(out.dtype)


def split_far_first_kernel(co, keep, got, send, rest):
    side = co[1] // 2
    for out, at in ((send, 1 - side), (rest, side)):
        if out is None:
            continue
        for half in range(2):
            row = pl.multiple_of(half * 96 + at * 48, 16)
            to = half * 48
            out[to : to + 48, :] = both(keep, got, pl.ds(row, 48)).astype(out.dtype)
        row = pl.multiple_of(192 + at * 96, 16)
        out[96:192, :] = both(keep, got, pl.ds(row, 96)).astype(out.dtype)


def sum_far_first_kernel(co, keep, got, out, send, rest):
    for half in range(2):
        rows = slice(half * 48, half * 48 + 48)
        out[:, half * D : half * D + D] = both(keep, got, rows).astype(BF)
    for part, i in ((send, 1 - co[2]), (rest, co[2])):
        row = pl.multiple_of(96 + i * 48, 16)
        part[...] = both(keep, got, pl.ds(row, 48)).astype(part.dtype)


def pack_kernel(co, early, vec, out):
    out[0:48, :] = early[...]
    out[48:64, :] = vec[...].astype(BF)


def sum_third_kernel(co, keep, got, early_keep, packed, vec, out, vec_out):
    out[:, : 2 * D] = both(keep, got, slice(None)).astype(BF)
    out[:, 2 * D :] = both(early_keep, packed, slice(0, 48)).astype(BF)
    vec_out[...] = vec[...] + packed[48:64, :].astype(F32)


def split_near_kernel(co, keep, got, send, rest):
    side = co[1] % 2
    for out, at in ((send, 1 - side), (rest, side)):
        if out is None:
            continue
        for far in range(2):
            row = pl.multiple_of((2 * far + at) * 48, 16)
            out[far * 48 : far * 48 + 48, :] = both(keep, got, pl.ds(row, 48)).astype(out.dtype)


def split_far_kernel(co, keep, got, send, rest):
    side = co[1] // 2
    for out, at in ((send, 1 - side), (rest, side)):
        row = pl.multiple_of(at * 48, 16)
        out[...] = both(keep, got, pl.ds(row, 48)).astype(out.dtype)


def sum_far_kernel(co, keep, got, out):
    out[...] = (keep[...] + got[...].astype(F32)).astype(BF)


def update_kernel(rate, moves, n_states, n_grads, n_before, co, *refs):
    grads = refs[3 * n_states :][:n_grads]
    first = 3 * n_states + n_grads + n_before
    parts, sems = refs[first + 4 * n_states : -1], refs[-1]
    copies = []
    for n, (which, numbers, row, src, size, b, col, stride) in enumerate(moves):
        state, new = refs[3 * which :][:3], refs[first + 4 * which :][:4]
        grad = 0.0
        for number in numbers:
            grad = grad + grads[number][row : row + 48, src : src + size].astype(F32)
        place = col if b is None else col + stride * lax.bitwise_xor(co[0], b)
        at = lanes(place, size)
        w, m, a = (ref[:, at] for ref in state)
        m_new = momentum_decay * m + grad
        w_new = w - rate * (grad + momentum_decay * m_new)
        full, low = parts[2 * n], parts[2 * n + 1]
        full[0] = w_new
        full[1] = m_new
        full[2] = average_decay * a + (1.0 - average_decay) * w_new
        low[...] = w_new.astype(BF)
        for k in range(4):
            source = full.at[k] if k < 3 else low
            copy = pltpu.make_async_copy(source, new[k].at[:, at], sems.at[4 * n + k])
            copy.start()
            copies.append(copy)
    for copy in copies:
        copy.wait()


def hold(arrays):
    return lax.optimization_barrier(arrays)


def fast_device(
    tokens,
    cotangent,
    clip_index,
    key_valid,
    patch_masked,
    attn_weight,
    mlp_weight,
    gain_vector,
    offset_vector,
    attn_moment,
    mlp_moment,
    gain_moment,
    offset_moment,
    attn_average,
    mlp_average,
    gain_average,
    offset_average,
):
    r, f = lax.axis_index("rep"), lax.axis_index("fsdp")
    co = jnp.stack([r, f // 4, (f // 2) % 2, f % 2]).astype(jnp.int32)

    def swap(array, mask):
        return lax.ppermute(array, ("rep", "fsdp"), [(i, i ^ mask) for i in range(32)])

    CORE, Y, Z, X = 1, 2, 4, 16

    (s0,) = call(
        prep_first_kernel,
        [((48, 3 * D), BF)],
        [co, attn_weight, mlp_weight],
        scratch=[pltpu.VMEM((6, 48, 384), F32), pltpu.SemaphoreType.DMA((6,))],
        name="prep",
        limit=60,
        space=pltpu.HBM,
    )
    info = jnp.zeros((8, 256), F32).at[0:3].set(
        jnp.stack([clip_index, key_valid, patch_masked]).astype(F32)
    )
    flat = jnp.zeros((16 * D,), F32)
    flat = lax.dynamic_update_slice(flat, gain_vector.astype(BF).astype(F32), (96 * f,))
    flat = lax.dynamic_update_slice(flat, offset_vector.astype(BF).astype(F32), (2 * D + 528 * f,))
    vec = flat.reshape(16, D)

    groups = [[4 * z + at for z in range(4)] for at in range(4)]

    def along_z(shard):
        return lax.all_gather(shard, "fsdp", axis=0, tiled=True, axis_index_groups=groups)

    def core_pair(pieces):
        return pieces + [swap(piece, CORE) for piece in pieces]

    stack0 = along_z(s0)
    stack0, vec, mlp_late = hold((stack0, vec, mlp_weight))
    s1, s2 = call(
        prep_second_kernel,
        [((48, 3 * D), BF), ((48, 2 * D), BF)],
        [co, mlp_late],
        name="prep",
    )
    across0 = swap(stack0, Y)
    far0 = swap(stack0, X)
    vec = vec + swap(vec, CORE)
    s1, vec = hold((s1, vec))
    near0 = [swap(stack0, CORE)]
    stack1 = along_z(s1)
    vec = vec + swap(vec, Y)
    stack1, across0, far0, near0, s2, vec = hold((stack1, across0, far0, near0, s2, vec))
    far_across0 = swap(across0, X)
    across1 = swap(stack1, Y)
    near0 += [swap(across0, CORE), swap(far0, CORE)]
    vec = vec + swap(vec, Z)
    s2, vec = hold((s2, vec))
    stack2 = along_z(s2)
    vec = vec + swap(vec, 2 * Z)
    stack2, across1, far_across0, near0, vec = hold((stack2, across1, far_across0, near0, vec))
    pieces0 = [stack0, across0, far0, far_across0, *near0, swap(far_across0, CORE)]
    across2 = swap(stack2, Y)
    far1 = swap(jnp.concatenate([stack1[:, 2 * D :], across1[:, 2 * D :]], axis=0), X)
    pieces1 = core_pair([stack1, across1])
    halves_t = [((384, 256), BF)] * 2
    h1, h1t_send, h1t_keep, cols = call(
        first_norm_kernel,
        [((256, D), BF), *halves_t, ((256, 128), F32)],
        [co, tokens, info, vec],
        scratch=[pltpu.VMEM((D, 256), F32)],
        name="norm1",
    )
    (w_qkv,) = assemble(co, pieces0, (0, 1152))
    qkv, att, lse = call(
        attention_kernel,
        [((256, 3 * D), BF), ((256, D), BF), ((16, 256), F32)],
        [co, h1, vec, info, cols, w_qkv],
        name="attention",
    )
    w_out, w_up0 = assemble(co, pieces0, (1152, 384), (1536, 768))
    w_up1, w_down00 = assemble(co, pieces1, (0, 1536), (1536, 768))

    y1, h2, h2t_send, h2t_keep, dzt_send, dzt_keep = call(
        second_norm_kernel,
        [((256, D), F32), ((256, D), BF), *halves_t, *halves_t],
        [co, tokens, cols, vec, att, w_out, cotangent],
        scratch=[pltpu.VMEM((D, 256), F32)],
        name="norm2",
    )
    shares = [((384, 4 * D), BF), ((384, 4 * D), F32)]
    g0, g1, slope0, slope1 = call(
        hidden_kernel,
        [((256, 2 * D), BF)] * 2 + [((256, 2 * D), F32)] * 2,
        [co, h2, vec, w_up0, w_up1],
        name="hidden",
    )

    def blocks(array):
        return array.reshape(4, 2, 48, -1)

    rate = base_rate / math.sqrt(tokens.shape[0] * 32)

    def update(moves, states, grads, name, before=()):
        parts, outs = [], []
        for move in moves:
            parts += [pltpu.VMEM((3, 48, move[4]), F32), pltpu.VMEM((48, move[4]), BF)]
        for state in states:
            outs += [jax.ShapeDtypeStruct(state[0].shape, F32)] * 3
            outs += [jax.ShapeDtypeStruct(state[0].shape, BF)]
        whole = pl.BlockSpec(memory_space=pltpu.VMEM)
        far = pl.BlockSpec(memory_space=pltpu.HBM)
        first = 1 + 3 * len(states) + len(grads)
        return pl.pallas_call(
            functools.partial(update_kernel, rate, moves, len(states), len(grads), len(before)),
            out_shape=outs,
            in_specs=[pl.BlockSpec(memory_space=pltpu.SMEM)]
            + [whole] * (first - 1)
            + [far] * len(before),
            out_specs=[far] * len(outs),
            input_output_aliases={first + k: k for k in range(len(before))},
            scratch_shapes=[*parts, pltpu.SemaphoreType.DMA((4 * len(moves),))],
            compiler_params=pltpu.CompilerParams(vmem_limit_bytes=8 * 2**20),
            cost_estimate=pl.CostEstimate(flops=2**20, bytes_accessed=2**20, transcendentals=0),
            name=name,
        )(co, *(array for state in states for array in state), *grads, *before)

    mlp_state = [mlp_weight, mlp_moment, mlp_average]
    attn_state = [attn_weight, attn_moment, attn_average]

    across2, far1, g0, g1 = hold((across2, far1, g0, g1))
    pieces2 = core_pair([stack2, across2])
    far1 = core_pair([far1])
    down_send, down_keep = call(
        down_grad_kernel, shares, [co, dzt_send, dzt_keep, g0, g1], name="down_grad"
    )
    pieces2, far1, down_send = hold((pieces2, far1, down_send))
    down_got = blocks(swap(down_send, CORE))
    down_keep = blocks(down_keep)
    w_down01, w_down11 = assemble(co, pieces2, (0, D), (D, D))
    (w_down10,) = assemble(co, far1, (0, D))
    du0, du1, db1, up_send, up_keep = call(
        hidden_grad_kernel,
        [((256, 2 * D), BF), ((256, 2 * D), BF), ((8, D), F32)] + shares,
        [co, cotangent, slope0, slope1, w_down00, w_down01, w_down10, w_down11, h2t_send, h2t_keep],
        name="hidden_grad",
    )
    down_got, up_send = hold((down_got, up_send))
    y_shares = [((192, 2 * D), BF), ((192, 2 * D), F32)]
    x_shares = [((4, 2, 48, D), BF), ((4, 2, 48, D), F32)]
    first = (split_first_kernel, y_shares + x_shares)
    y_send0, x_send1 = call_all(co, [(*first, [down_keep, down_got])], "split_first", BF)
    y_send0, x_send1, up_send, down_got = hold((y_send0, x_send1, up_send, down_got))
    y_keep0, x_keep1 = call_all(co, [(*first, [down_keep, down_got])], "keep_first", F32)
    du0, y_keep0, x_keep1 = hold((du0, y_keep0, x_keep1))
    y_got0 = swap(y_send0, Y)
    x_got1 = swap(x_send1, X)
    up_got = blocks(swap(up_send, CORE))
    up_keep = blocks(up_keep)
    dy1, datt, dpt_send, dpt_keep, small2 = call(
        second_back_kernel,
        [((256, D), F32), ((256, D), BF), *halves_t, ((8, D), F32)],
        [co, cotangent, y1, vec, du0, du1, w_up0, w_up1, w_out],
        scratch=[pltpu.VMEM((D, 256), F32)],
        name="norm2_back",
    )
    dqkv, small_a = call(
        attention_back_kernel,
        [((256, 3 * D), BF), ((8, D), F32)],
        [co, info, cols, lse, qkv, datt],
        name="attention_back",
    )
    attn_send, attn_keep = call(
        attention_grad_kernel,
        shares,
        [co, h1t_send, h1t_keep, dqkv, dpt_send, dpt_keep, att],
        name="attention_grad",
    )

    def split_near(keep, got, small=()):
        width = keep.shape[1]
        return call(
            split_near_kernel,
            [((96, width), BF), ((96, width), F32), *small],
            [co, keep, got],
            name="split_near",
        )

    def split_far(keep, got):
        width = keep.shape[1]
        return call(
            split_far_kernel,
            [((48, width), BF), ((48, width), F32)],
            [co, keep, got],
            name="split_far",
        )

    def sum_far(keep, got):
        return call(sum_far_kernel, [(keep.shape, BF)], [co, keep, got], name="sum_far")[0]

    def near_job(keep, got, small=()):
        width = keep.shape[1]
        return split_near_kernel, [((96, width), BF), ((96, width), F32), *small], [keep, got]

    def far_job(keep, got):
        width = keep.shape[1]
        return split_far_kernel, [((48, width), BF), ((48, width), F32)], [keep, got]

    def sum_job(keep, got):
        return sum_far_kernel, [(keep.shape, BF)], [keep, got]

    y_got0, x_got1, up_got, attn_send = hold((y_got0, x_got1, up_got, attn_send))
    near_shares = [((384, D), BF), ((384, D), F32)]

    def second(y_got):
        up = [up_keep, up_got]
        return [
            (split_second_kernel, y_shares + x_shares, [x_keep1, x_got1, *up]),
            (split_near_first_kernel, near_shares, [y_keep0, y_got, *up]),
        ]

    y_send1, x_send2, near_send0 = call_all(co, second(y_got0), "split_second", BF)
    y_got0, near_send0 = hold((y_got0, near_send0))
    y_keep1, x_keep2, near_keep0 = call_all(co, second(y_got0), "keep_second", F32)
    dqkv, y_keep1, x_keep2, near_keep0 = hold((dqkv, y_keep1, x_keep2, near_keep0))
    y_got1 = swap(y_send1, Y)
    x_got2 = swap(x_send2, X)
    near_got0 = swap(near_send0, Z)
    attn_got = blocks(swap(attn_send, CORE))
    attn_keep = blocks(attn_keep)
    input_grad, total = call(
        first_back_kernel,
        [((256, D), BF), ((16, D), F32)],
        [co, dqkv, tokens, cols, vec, dy1, db1, small2, small_a, w_qkv],
        name="norm1_back",
    )
    near_got0, y_got1, x_got2, attn_got, total = hold(
        (near_got0, y_got1, x_got2, attn_got, total)
    )
    far_shares = [((192, D), BF), ((192, D), F32)]
    third_shares = y_shares + x_shares + x_shares[1:]

    def far_first(got):
        return split_far_first_kernel, far_shares, [near_keep0, got]

    def third(got):
        return split_third_kernel, third_shares, [x_keep2, got, attn_keep, attn_got]

    def near_second(got):
        near = [((96, 2 * D), BF), ((96, 2 * D), F32)]
        return split_near_kernel, near, [y_keep1, got]

    (far_send0,) = call_all(co, [far_first(near_got0)], "split_far", BF)
    x_got2 = hold((x_got2, far_send0))[0]
    y_send2, x_send3 = call_all(co, [third(x_got2)], "split_third", BF)
    y_got1 = hold((y_got1, y_send2))[0]
    (near_send1,) = call_all(co, [near_second(y_got1)], "split_near", BF)
    near_got0, x_got2, y_got1, near_send1 = hold((near_got0, x_got2, y_got1, near_send1))
    far_keep0, y_keep2, x_keep3, last, near_keep1 = call_all(
        co, [far_first(near_got0), third(x_got2), near_second(y_got1)], "keep_third", F32
    )
    y1, far_keep0, y_keep2, x_keep3, last, near_keep1 = hold(
        (y1, far_keep0, y_keep2, x_keep3, last, near_keep1)
    )
    x_got3 = swap(x_send3, X)
    y_got2 = swap(y_send2, Y)
    near_got1 = swap(near_send1, Z)
    far_got0 = swap(far_send0, 2 * Z)
    total = total + swap(total, CORE)
    (activations,) = call(
        output_kernel,
        [((256, D), BF)],
        [co, y1, vec, g0, g1, w_down00, w_down01, w_down10, w_down11],
        name="output",
    )
    far_got0, near_got1, y_got2, x_got3, total, activations = hold(
        (far_got0, near_got1, y_got2, x_got3, total, activations)
    )
    y_send3, y_keep3 = call(
        split_fourth_kernel,
        y_shares,
        [co, x_keep3, x_got3, last],
        name="split_fourth",
    )
    y_got2 = hold((y_got2, y_send3))[0]
    near_send2, near_keep2 = split_near(y_keep2, y_got2)
    near_got1 = hold((near_got1, near_send2))[0]
    far_send1, far_keep1 = split_far(near_keep1, near_got1)
    far_got0 = hold((far_got0, far_send1))[0]
    mine0, early_send, early_keep = call(
        sum_far_first_kernel,
        [((48, 2 * D), BF), ((48, D), BF), ((48, D), F32)],
        [co, far_keep0, far_got0],
        name="sum_far",
    )
    y_got3 = swap(y_send3, Y)
    near_got2 = swap(near_send2, Z)
    far_got1 = swap(far_send1, 2 * Z)
    got0 = swap(mine0, X)
    total = total + swap(total, 2 * Z)
    got0, far_got1, near_got2, y_got3, total = hold(
        (got0, far_got1, near_got2, y_got3, total)
    )
    near_send3, near_keep3, far_send2, far_keep2, mine1, packed = call_all(
        co,
        [
            near_job(y_keep3, y_got3),
            far_job(near_keep2, near_got2),
            sum_job(far_keep1, far_got1),
            (pack_kernel, [((64, D), BF)], [early_send, total]),
        ],
        "split_sixth_round",
    )
    near_got3 = swap(near_send3, Z)
    far_got2 = swap(far_send2, 2 * Z)
    got1 = swap(mine1, X)
    packed = swap(packed, Y)
    got1, far_got2, near_got3, packed = hold((got1, far_got2, near_got3, packed))
    far_send3, far_keep3, mine2, total = call_all(
        co,
        [
            far_job(near_keep3, near_got3),
            (
                sum_third_kernel,
                [((48, 3 * D), BF), ((16, D), F32)],
                [far_keep2, far_got2, early_keep, packed, total],
            ),
        ],
        "split_last_round",
    )
    far_got3 = swap(far_send3, 2 * Z)
    got2 = swap(mine2, X)
    total = total + swap(total, Z)
    moves = [(0, (0, 1), 0, h * D, D, None, FF + h * 2 * D, 0) for h in range(2)]
    moves += [(0, (2 + b,), 0, 0, D, b, FF + D, 2 * D) for b in range(2)]
    moves += [(0, (2, 3), 0, D, D, None, 0, 0)]
    got1 = hold((got1, mine2))[0]
    mlp = update(moves, [mlp_state], [mine0, got0, mine1, got1], "update_mlp")
    got2, far_got3, total, mlp = hold((got2, far_got3, total, mlp))
    mine3 = sum_far(far_keep3, far_got3)
    got3 = swap(mine3, X)
    total = total + swap(total, X)
    got2 = hold((got2, mine3))[0]
    moves = [(0, (b,), 0, 0, D, b, D, 2 * D) for b in range(2)]
    moves += [(0, (0, 1), 0, 2 * D, D, None, 2 * D, 0), (1, (0, 1), 0, D, D, None, 0, 0)]
    both_new = update(
        moves,
        [mlp_state, attn_state],
        [mine2, got2],
        "update_both",
        mlp,
    )
    mlp, attn = both_new[:4], both_new[4:]
    moves = [(0, (b,), 0, 0, 384, b, D, 384) for b in range(2)]
    moves += [(0, (b,), 0, 384, 384, b, 2 * D, 384) for b in range(2)]
    moves += [(0, (0, 1), 0, D, D, None, 3 * D, 0)]
    attn = update(moves, [attn_state], [mine3, got3], "update_attn", attn)
    flat = total.reshape(-1)
    gain_g = lax.dynamic_slice(flat, (96 * f,), (96,))
    offset_g = lax.dynamic_slice(flat, (2 * D + 528 * f,), (528,))

    gains = advance(gain_g, gain_vector, gain_moment, gain_average, rate)
    offsets = advance(offset_g, offset_vector, offset_moment, offset_average, rate)
    return (activations, input_grad, *attn, *mlp, *gains, *offsets)


def solution(mesh):
    placed = (
        P(("rep", "fsdp"), None),
        P(("rep", "fsdp"), None),
        P(("rep", "fsdp")),
        P(("rep", "fsdp")),
        P(("rep", "fsdp")),
        P("fsdp", None),
        P("fsdp", None),
        P("fsdp"),
        P("fsdp"),
        P("fsdp", None),
        P("fsdp", None),
        P("fsdp"),
        P("fsdp"),
        P("fsdp", None),
        P("fsdp", None),
        P("fsdp"),
        P("fsdp"),
    )
    small = mesh.shape["rep"] == 2 and mesh.shape["fsdp"] == 16
    return jax.shard_map(
        fast_device if small else per_device,
        mesh=mesh,
        in_specs=placed,
        out_specs=(
            P(("rep", "fsdp"), None),
            P(("rep", "fsdp"), None),
            P("fsdp", None),
            P("fsdp", None),
            P("fsdp", None),
            P("fsdp", None),
            P("fsdp", None),
            P("fsdp", None),
            P("fsdp", None),
            P("fsdp", None),
            P("fsdp"),
            P("fsdp"),
            P("fsdp"),
            P("fsdp"),
            P("fsdp"),
            P("fsdp"),
            P("fsdp"),
            P("fsdp"),
        ),
        check_vma=False,
    )
```
